256 devices in a mesh: gx: 16 (over z, core), gy: 16 (over x, y).
Axes of the slice: x: 4, y: 4, z: 8, core: 2. Of those that a mesh axis runs over, the one named last changes fastest.
Arguments:
- fields: float32 [256, 6, 8100], P(('gx', 'gy')), may hold values from -6 to 6
- wet_mask: int32 [256, 8100], P(('gx', 'gy')), may hold values 0 or 1
- tile_of_slot: int32 [256], replicated, may hold values from -1 to 255, as said below
- neighbor: int32 [256, 4], replicated, may hold values from -1 to 255, as said below
- rotation: int32 [256, 4], replicated, may hold values from 0 to 3
Outputs:
- updated: float32 [256, 6, 8100], P(('gx', 'gy'))
The draws below stay inside these ranges and needn't reach their ends.
Inputs may be any that keep to these rules, and one draw needn't show every extreme that they name: `tile_of_slot`: slot s lies on device s, devices numbered gx-major; each tile is held by at most one slot, and every tile named in neighbor is held. Rows of tiles held by no slot are -1. The relation is mutual: side (k + 2 + rotation[t][k]) mod 4 of neighbor[t][k] leads back to t with rotation (4 - rotation[t][k]) mod 4. A tile's neighbour is held on the tile's device, on a device next to it along gx or along gy (gx wrapping at its ends), or, across a pole, on the device 16 / 2 away along gx at the same gy index, for devices at the first or last gy index. For two different devices at most 1 pairs (tile of the first, side) lead to tiles of the second; in every draw some device has exactly 1 such pairs leading to it from each of the four devices next to it.
All inputs are finite; a program needn't handle non-finite values. No bound on the sum of `wet_mask` on one device may be relied on, other than what follows from the above.
Results may differ from the reference program's by a relative error of at most 0.00002.
Values sent between devices are 32-bit elements; how exact they have to be, the bound alone decides.
No kernel may reach another device: no remote copies, remote signals or barrier semaphores. Data moves between devices by JAX's collectives and lax.ppermute only.
A program may use at most 64 MiB of HBM per device.

```python
import jax
import jax.numpy as jnp
from jax import lax

BLOCK = 1
TILE = 90
SLOTS_DEV = 1
CELLS = 8100
SLOTS = 256
FACE = 2
N_GX = 16
N_GY = 16


def world_layout(key):
    size_x = BLOCK * N_GX
    size_y = BLOCK * N_GY
    face_key, land_key, pick_key, order_key = jax.random.split(key, 4)
    face_turns = jax.random.randint(face_key, (size_x // FACE, size_y // FACE), 0, 4)
    orient = jnp.repeat(jnp.repeat(face_turns, FACE, axis=0), FACE, axis=1)
    land_tile = jax.random.randint(land_key, (size_x, size_y), 0, 4) == 0
    centre_x = jax.random.randint(jax.random.fold_in(pick_key, 1), (), 0, N_GX)
    centre_y = jax.random.randint(jax.random.fold_in(pick_key, 2), (), 1, N_GY - 1)
    grid_x = jnp.arange(size_x, dtype=jnp.int32)[:, None] + jnp.zeros((1, size_y), jnp.int32)
    grid_y = jnp.arange(size_y, dtype=jnp.int32)[None, :] + jnp.zeros((size_x, 1), jnp.int32)
    close_x = (grid_x - centre_x * BLOCK + 1) % size_x < BLOCK + 2
    close_y = (grid_y >= centre_y * BLOCK - 1) & (grid_y <= centre_y * BLOCK + BLOCK)
    polar_row = (grid_y == 0) | (grid_y == size_y - 1)
    wet_tile = jnp.logical_not(land_tile) | close_x & close_y | polar_row
    device = grid_x // BLOCK * N_GY + grid_y // BLOCK
    local_index = grid_x % BLOCK * BLOCK + grid_y % BLOCK
    orders = jax.vmap(lambda one_key: jax.random.permutation(one_key, SLOTS_DEV))(jax.random.split(order_key, N_GX * N_GY))
    slot_index = device * SLOTS_DEV + orders[device, local_index]
    tile_id = grid_x * size_y + grid_y
    slot_tiles = jnp.full((SLOTS,), -1, jnp.int32).at[slot_index.reshape(-1)].set(jnp.where(wet_tile, tile_id, -1).reshape(-1).astype(jnp.int32))
    side_order = jnp.arange(4, dtype=jnp.int32)[None, None, :]
    global_side = (side_order + orient[:, :, None]) % 4
    step_x = jnp.where(global_side == 1, 1, 0) - jnp.where(global_side == 3, 1, 0)
    step_y = jnp.where(global_side == 2, 1, 0) - jnp.where(global_side == 0, 1, 0)
    raw_y = grid_y[:, :, None] + step_y
    crossing = (raw_y < 0) | (raw_y >= size_y)
    other_x = jnp.where(crossing, (grid_x[:, :, None] + size_x // 2) % size_x, (grid_x[:, :, None] + step_x) % size_x)
    other_y = jnp.clip(raw_y, 0, size_y - 1)
    linked = wet_tile[other_x, other_y] & wet_tile[:, :, None]
    neighbor = jnp.where(linked, other_x * size_y + other_y, -1).reshape(SLOTS, 4)
    turn = orient[:, :, None] - orient[other_x, other_y] - jnp.where(crossing, 2, 0)
    rotation = jnp.where(linked, turn % 4, 0).reshape(SLOTS, 4)
    return (slot_tiles.astype(jnp.int32), neighbor.astype(jnp.int32), rotation.astype(jnp.int32))


def draw_tile_of_slot(key, part):
    layout = world_layout(key)
    return layout[0]


def draw_neighbor(key, part):
    layout = world_layout(key)
    return layout[1]


def draw_rotation(key, part):
    layout = world_layout(key)
    return layout[2]


def with_ends(entries, rng, low, top_value):
    shape = entries.shape
    index_at = [jax.random.randint(jax.random.fold_in(rng, axis), (), 0, shape[axis]) for axis in range(len(shape))]
    entries = entries.at[tuple(index_at)].set(low)
    longest = shape.index(max(shape))
    index_at[longest] = (index_at[longest] + 1) % shape[longest]
    return entries.at[tuple(index_at)].set(top_value)


def shard_levels(own_key, dims, shards, smallest, top_value):
    def one(axis_at, shards_of):
        steps = jax.random.uniform(jax.random.fold_in(jax.random.fold_in(own_key, 6), axis_at), (shards_of,), jnp.float32, smallest / len(shards), top_value / len(shards))
        return jnp.repeat(jnp.exp(steps), dims[axis_at] // shards_of).reshape((-1,) + (1,) * (len(dims) - axis_at - 1))

    level = one(*shards[0])
    for cut in shards[1:]:
        level = level * one(*cut)
    return level


def scatter_about(stream_key, dims, scale, limit, pieces=(), kind=jnp.bfloat16):
    entries = jax.random.normal(stream_key, dims, jnp.float32) * scale
    if len(pieces) > 0:
        entries = shard_levels(stream_key, dims, pieces, -0.22, 0.18) * entries
    return jnp.clip(entries, min=-limit, max=limit).astype(kind)


def setup_inputs(seed: int = 0) -> dict:
    splits = jax.random.split(jax.random.key(seed), 6)
    return {
        "fields": scatter_about(splits[0], (SLOTS, 6, CELLS), 1.0, 6.0, ((0, 256),), jnp.float32),
        "wet_mask": with_ends((jax.random.randint(splits[1], (SLOTS, CELLS), 0, 8) < 7).astype(jnp.int32), jax.random.fold_in(splits[1], 1), 0, 1),
        "tile_of_slot": draw_tile_of_slot(jax.random.fold_in(splits[5], 71), 0),
        "neighbor": draw_neighbor(jax.random.fold_in(splits[5], 71), 0),
        "rotation": draw_rotation(jax.random.fold_in(splits[5], 71), 0),
    }


ADVECT = 0.25
DIFFUSE = 0.15
VISCOUS = 0.15
STEP_SIZE = 0.5
CORIOLIS = 0.3
GRAVITY = 0.8


def quarter(first_part, second_part, quarter_turns):
    if quarter_turns == 0:
        return first_part, second_part
    if quarter_turns == 1:
        return second_part, -first_part
    if quarter_turns == 2:
        return -first_part, -second_part
    return -second_part, first_part


def edge_strips(values, side_len, vector):
    cell_count = values.shape[-1]
    segments = [values[..., :side_len], values[..., side_len - 1::side_len],
                values[..., cell_count - side_len:][..., ::-1], values[..., 0::side_len][..., ::-1]]
    if vector:
        for facing in range(4):
            segment = segments[facing]
            first_part, second_part = quarter(segment[:, 0:2], segment[:, 2:4], facing)
            segments[facing] = jnp.concatenate([first_part, second_part, segment[:, 4:]], axis=1)
    return jnp.stack(segments, axis=1)


def place_strips(strips, vector):
    placed = []
    for facing in range(4):
        segment = strips[:, facing]
        if facing < 2:
            segment = segment[..., ::-1]
        if vector:
            first_part, second_part = quarter(segment[:, 0:2], segment[:, 2:4], (2 - facing) % 4)
            segment = jnp.concatenate([first_part, second_part, segment[:, 4:]], axis=1)
        placed.append(segment)
    return placed


def shifted(values, rims, side_len):
    south_rim, east_rim, north_rim, west_rim = rims
    cell_count = values.shape[-1]
    column = jnp.arange(cell_count, dtype=jnp.int32) % side_len
    upward = jnp.concatenate([values[..., side_len:], north_rim], axis=-1)
    downward = jnp.concatenate([south_rim, values[..., :cell_count - side_len]], axis=-1)
    rightward = jnp.where(column == side_len - 1, jnp.repeat(east_rim, side_len, axis=-1), jnp.roll(values, -1, axis=-1))
    leftward = jnp.where(column == 0, jnp.repeat(west_rim, side_len, axis=-1), jnp.roll(values, 1, axis=-1))
    return rightward, leftward, upward, downward


def tracer_step(masked, shifts, wet_real):
    rightward, leftward, upward, downward = shifts
    tracer = masked[:, 4:6]
    tracer_dx = 0.5 * (rightward[:, 4:6] - leftward[:, 4:6])
    tracer_dy = 0.5 * (upward[:, 4:6] - downward[:, 4:6])
    laplacian = rightward[:, 4:6] + leftward[:, 4:6] + upward[:, 4:6] + downward[:, 4:6] - 4.0 * tracer
    advection = masked[:, 0:2] * tracer_dx + masked[:, 2:4] * tracer_dy
    return wet_real[:, None, :] * (tracer - ADVECT * advection + DIFFUSE * laplacian)


def momentum_step(masked, shifts, pressure_shifts, wet_real):
    rightward, leftward, upward, downward = shifts
    press_right, press_left, press_up, press_down = pressure_shifts
    velocity_first = masked[:, 0:2]
    velocity_second = masked[:, 2:4]

    def advance(current, start_ch, stop_ch, turning, gradient):
        along_first = 0.5 * (rightward[:, start_ch:stop_ch] - leftward[:, start_ch:stop_ch])
        along_second = 0.5 * (upward[:, start_ch:stop_ch] - downward[:, start_ch:stop_ch])
        laplacian = (rightward[:, start_ch:stop_ch] + leftward[:, start_ch:stop_ch]
                     + upward[:, start_ch:stop_ch] + downward[:, start_ch:stop_ch] - 4.0 * current)
        change = (STEP_SIZE * (turning - gradient)
                  - ADVECT * (velocity_first * along_first + velocity_second * along_second)
                  + VISCOUS * laplacian)
        return wet_real[:, None, :] * (current + change)

    first_new = advance(velocity_first, 0, 2, CORIOLIS * velocity_second, 0.5 * (press_right - press_left))
    second_new = advance(velocity_second, 2, 4, -CORIOLIS * velocity_first, 0.5 * (press_up - press_down))
    return first_new, second_new


def sources(tile_of_slot, neighbor, rotation):
    slot_count = tile_of_slot.shape[0]
    tile_count = neighbor.shape[0]
    target = jnp.where(tile_of_slot >= 0, tile_of_slot, tile_count)
    slot_of_tile = jnp.full((tile_count,), -1, jnp.int32).at[target].set(
        jnp.arange(slot_count, dtype=jnp.int32), mode="drop")
    held_tile = jnp.clip(tile_of_slot, 0, tile_count - 1)
    near_tile = jnp.where(tile_of_slot[:, None] >= 0, neighbor[held_tile], -1)
    facing_side = (jnp.arange(4, dtype=jnp.int32)[None, :] + 2 + rotation[held_tile]) % 4
    near_slot = jnp.where(near_tile >= 0, slot_of_tile[jnp.clip(near_tile, 0, tile_count - 1)], -1)
    return jnp.where(near_slot >= 0, near_slot * 4 + facing_side, -1).astype(jnp.int32)


def fetch_rims(strips, source):
    slot_count = strips.shape[0]
    flat = strips.reshape((slot_count * 4,) + strips.shape[2:])
    picked = flat[jnp.clip(source, 0, slot_count * 4 - 1).reshape(-1)].reshape(strips.shape)
    return picked * (source >= 0).astype(jnp.float32)[:, :, None, None]


def reference(fields, wet_mask, tile_of_slot, neighbor, rotation):
    wet_real = wet_mask.astype(jnp.float32)
    live = (tile_of_slot >= 0).astype(jnp.float32)
    masked = fields * wet_real[:, None, :]
    source = sources(tile_of_slot, neighbor, rotation)
    rim_one = place_strips(fetch_rims(edge_strips(masked, TILE, True), source), True)
    block_count = SLOTS // SLOTS_DEV

    def blocks(stacked):
        return stacked.reshape((block_count, SLOTS_DEV) + stacked.shape[1:])

    def first_half(packed):
        local_masked, local_rims, local_wet = packed
        return tracer_step(local_masked, shifted(local_masked, local_rims, TILE), local_wet)

    tracer_new = lax.map(first_half, (blocks(masked), [blocks(one_rim) for one_rim in rim_one], blocks(wet_real)))
    tracer_new = tracer_new.reshape(SLOTS, 2, CELLS)
    pressure = GRAVITY * jnp.concatenate([tracer_new[:, 0:1], tracer_new[:, 0:1] + tracer_new[:, 1:2]], axis=1)
    rim_two = place_strips(fetch_rims(edge_strips(pressure, TILE, False), source), False)

    def second_half(packed):
        local_masked, local_rims, local_press, local_press_rims, local_wet = packed
        return momentum_step(local_masked, shifted(local_masked, local_rims, TILE),
                             shifted(local_press, local_press_rims, TILE), local_wet)

    first_new, second_new = lax.map(second_half, (blocks(masked), [blocks(one_rim) for one_rim in rim_one],
                                                  blocks(pressure), [blocks(one_rim) for one_rim in rim_two],
                                                  blocks(wet_real)))
    updated = jnp.concatenate([first_new.reshape(SLOTS, 2, CELLS), second_new.reshape(SLOTS, 2, CELLS),
                               tracer_new], axis=1)
    return updated * live[:, None, None]
```

```python
import jax
import jax.numpy as jnp
from jax import lax
from jax.experimental import pallas as pl
from jax.experimental.pallas import tpu as pltpu
from jax.sharding import PartitionSpec as P

TILE = 90
CELLS = TILE * TILE
LANES = 128
CHUNKS = 64
WIDE = LANES * CHUNKS
HALF = 45
LAST = CELLS - TILE - (CHUNKS - 2) * LANES

ADVECT = 0.25
DIFFUSE = 0.15
STEP_SIZE = 0.5
CORIOLIS = 0.3
GRAVITY = 0.8

AXES = ("gx", "gy")
VMEM = pl.BlockSpec(memory_space=pltpu.VMEM)
SMEM = pl.BlockSpec(memory_space=pltpu.SMEM)
ANY = pl.BlockSpec(memory_space=pl.ANY)


def link_x_even(x, y, nx, ny):
    return x ^ 1, y


def link_x_odd(x, y, nx, ny):
    return (((x + nx - 1) % nx ^ 1) + 1) % nx, y


def link_y_even(x, y, nx, ny):
    return x, y ^ 1


def link_y_odd(x, y, nx, ny):
    if y == 0 or y == ny - 1:
        return (x + nx // 2) % nx, y
    return x, ((y - 1) ^ 1) + 1


LINKS = (link_y_odd, link_x_even, link_y_even, link_x_odd)


def pairs_of(link, nx, ny):
    out = []
    for x in range(nx):
        for y in range(ny):
            to_x, to_y = link(x, y, nx, ny)
            out.append((x * ny + y, to_x * ny + to_y))
    return out


def partner(me, which, nx, ny):
    x, y = me // ny, me % ny
    if which == 0:
        pole = (y == 0) | (y == ny - 1)
        step = jnp.where(y % 2 == 1, 1, -1)
        return jnp.where(pole, (x + nx // 2) % nx * ny + y, me + step)
    if which == 1:
        return me + jnp.where(x % 2 == 0, ny, -ny)
    if which == 2:
        return me + jnp.where(y % 2 == 0, 1, -1)
    return (x + jnp.where(x % 2 == 1, 1, nx - 1)) % nx * ny + y


def lanes():
    return lax.broadcasted_iota(jnp.int32, (8, LANES), 1)


def rows():
    return lax.broadcasted_iota(jnp.int32, (8, LANES), 0)


def pick(values, index):
    return jnp.take_along_axis(values, index, axis=1)


def tiled(values, count):
    return jnp.concatenate([values] * count, axis=1)


def column_of():
    cell = lax.broadcasted_iota(jnp.int32, (8, WIDE), 1)
    line = jnp.floor((cell.astype(jnp.float32) + 0.5) * (1.0 / TILE)).astype(jnp.int32)
    return cell, cell - TILE * line


def edge_lines(state, column):
    lane = lanes()
    edge = (column == 0) | (column == TILE - 1)
    parts = []
    for low, high in ((0, HALF), (HALF, CHUNKS)):
        found = jnp.zeros((8, LANES), jnp.float32)
        for c in range(low, high):
            cut = slice(c * LANES, (c + 1) * LANES)
            found = jnp.where(edge[:, cut], state[:, cut], found)
        parts.append(found)
    east_at = (TILE * lane + TILE - 1) & (LANES - 1)
    west_at = (TILE * lane) & (LANES - 1)
    east = jnp.where(lane < 64, pick(parts[0], east_at), pick(parts[1], east_at))
    west = jnp.where(lane < 64, pick(parts[0], west_at), pick(parts[1], west_at))
    south = state[:, :LANES]
    before = pltpu.roll(state[:, (CHUNKS - 2) * LANES:(CHUNKS - 1) * LANES], LANES - LAST, 1)
    after = pltpu.roll(state[:, (CHUNKS - 1) * LANES:], LANES - LAST, 1)
    north = jnp.where(lane < LANES - LAST, before, after)
    return [south, east, north, west]


def spread(lines, cell, column):
    south, east, north, west = lines
    lane = lanes()
    odd = (lane & 1) == 1
    line_at = (37 * ((lane + jnp.where(odd, 39, 0)) >> 1)) & 63
    early = jnp.where(odd, pick(east, line_at), pick(west, line_at))
    late = jnp.where(odd, pick(east, line_at + 64), pick(west, line_at + 64))
    sides = jnp.concatenate([early] * HALF + [late] * (CHUNKS - HALF), axis=1)
    edge = (column == 0) | (column == TILE - 1)
    out = jnp.where(edge, sides, 0.0)
    first = jnp.where(lane < TILE, south, 0.0) + out[:, :LANES]
    moved = pltpu.roll(north, LAST, 1)
    before = out[:, (CHUNKS - 2) * LANES:(CHUNKS - 1) * LANES] + jnp.where(lane >= LAST, moved, 0.0)
    after = out[:, (CHUNKS - 1) * LANES:] + jnp.where(lane < LAST + TILE - LANES, moved, 0.0)
    return jnp.concatenate([first, out[:, LANES:(CHUNKS - 2) * LANES], before, after], axis=1)


def neighbours(state):
    cell, column = column_of()
    right = jnp.where(column == TILE - 1, 0.0, pltpu.roll(state, WIDE - 1, 1))
    left = jnp.where(column == 0, 0.0, pltpu.roll(state, 1, 1))
    up = jnp.where(cell >= CELLS - TILE, 0.0, pltpu.roll(state, WIDE - TILE, 1))
    down = jnp.where(cell < TILE, 0.0, pltpu.roll(state, TILE, 1))
    return right, left, up, down, cell, column


def row_of(values):
    return lax.broadcasted_iota(jnp.int32, values.shape, 0)


def repeated(values, first):
    row = row_of(values)
    if first == 0:
        pair = jnp.where(row < 2, values, pltpu.roll(values, 2, 0))
    else:
        pair = jnp.where(row < 4, values, pltpu.roll(values, 2, 0))
        pair = jnp.where(row < 2, pltpu.roll(values, 6, 0), pair)
        return pair
    return jnp.where(row < 4, pair, pltpu.roll(values, 4, 0))


def wet_rows(values):
    return jnp.broadcast_to(values[6:7], values.shape)


def turned(line, turns):
    row = row_of(line)
    swapped = jnp.where(row < 2, pltpu.roll(line, 6, 0), pltpu.roll(line, 2, 0))
    velocity = row < 4
    second = jnp.where(row < 2, swapped, -swapped)
    odd = jnp.where(turns % 2 == 1, 1, 0)
    out = jnp.where(jnp.logical_and(velocity, odd == 1), second, line)
    back = jnp.where(turns >= 2, 1, 0)
    return jnp.where(jnp.logical_and(velocity, back == 1), -out, out)


def flipped(line):
    return pick(line, jnp.maximum(TILE - 1 - lanes(), 0))


ROUTE = 48


def outgoing(lines, route, pay_refs, own_ref, vector):
    sent = []
    for side in range(4):
        line = jnp.where(route[32 + side] == 1, flipped(lines[side]), lines[side])
        if vector:
            line = turned(line, route[36 + side])
        sent.append(line)
    for link in range(4):
        total = jnp.zeros((8, LANES), jnp.float32)
        for side in range(4):
            total = jnp.where(route[4 * link + side] == 1, sent[side], total)
        pay_refs[link][...] = total
    for target in range(4):
        total = jnp.zeros((8, LANES), jnp.float32)
        for side in range(4):
            total = jnp.where(route[16 + 4 * side + target] == 1, sent[side], total)
        own_ref[8 * target:8 * target + 8, :] = total


def rims_of(route, own_ref, came_refs):
    out = []
    for side in range(4):
        rim = own_ref[8 * side:8 * side + 8, :]
        for link in range(4):
            rim = jnp.where(route[4 * link + side] == 1, came_refs[link][...], rim)
        out.append(rim)
    return out


def load_kernel(shape, me_ref, tiles_ref, near_ref, turn_ref, fields_ref, wet_ref,
                state_ref, lines_ref, own_ref, pay0, pay1, pay2, pay3, route, raw, wet_raw, sems):
    nx, ny = shape
    copies = [pltpu.make_async_copy(fields_ref.at[c, 0], raw.at[c], sems.at[c])
              for c in range(6)]
    copies.append(pltpu.make_async_copy(wet_ref.at[0], wet_raw.at[0], sems.at[6]))
    for copy in copies:
        copy.start()
    me = me_ref[0]
    tile = tiles_ref[me]
    live = tile >= 0
    held = jnp.maximum(tile, 0)
    near = [jnp.where(live, near_ref[side, held], -1) for side in range(4)]
    turn = [turn_ref[side, held] for side in range(4)]
    for link in range(4):
        other = tiles_ref[partner(me, link, nx, ny)]
        for side in range(4):
            route[4 * link + side] = jnp.where((near[side] >= 0) & (near[side] == other), 1, 0)
    for side in range(4):
        target = (side + 2 + turn[side]) % 4
        for k in range(4):
            route[16 + 4 * side + k] = jnp.where((near[side] >= 0) & (near[side] == tile) & (target == k), 1, 0)
        route[32 + side] = jnp.where((target < 2) != (side >= 2), 1, 0)
        route[36 + side] = (4 - turn[side]) % 4
    route[40] = jnp.where(live, 1, 0)
    for copy in copies:
        copy.wait()
    state_ref[:, (CHUNKS - 1) * LANES:] = jnp.zeros((8, LANES), jnp.float32)
    for low, high in ((0, (CHUNKS - 1) * LANES), ((CHUNKS - 1) * LANES, CELLS)):
        size = (8, high - low)
        row = lax.broadcasted_iota(jnp.int32, size, 0)
        wet = jnp.broadcast_to(wet_raw[0:1, low:high].astype(jnp.float32), size)
        state_ref[:, low:high] = jnp.where(row < 6, raw[:, low:high] * wet, jnp.where(row == 6, wet, 0.0))
    state = state_ref[...]
    cell, column = column_of()
    lines = edge_lines(state, column)
    for side in range(4):
        lines_ref[8 * side:8 * side + 8, :] = lines[side]
    outgoing(lines, route, (pay0, pay1, pay2, pay3), own_ref, True)


def inner_kernel(state_ref, base_ref, base_lines_ref):
    state = state_ref[...]
    right, left, up, down, cell, column = neighbours(state)
    first, second, wet = repeated(state, 0), repeated(state, 2), wet_rows(state)
    along = first * (right - left) + second * (up - down)
    round_sum = right + left + up + down - 4.0 * state
    base = wet * (state - (0.5 * ADVECT) * along + DIFFUSE * round_sum)
    base_ref[...] = base
    lines = edge_lines(base, column)
    for side in range(4):
        base_lines_ref[8 * side:8 * side + 8, :] = lines[side]


def at_ends(line, lane_from, lane_to):
    value = jnp.broadcast_to(line[:, lane_from:lane_from + 1], (8, LANES))
    return jnp.where(lanes() == lane_to, value, 0.0)


def edge_kernel(route, lines_ref, own_ref, base_lines_ref, came0, came1, came2, came3,
                patch_ref, own_two_ref, pay0, pay1, pay2, pay3):
    rims = rims_of(route, own_ref, (came0, came1, came2, came3))
    patch = []
    for side in range(4):
        line = lines_ref[8 * side:8 * side + 8, :]
        drift = repeated(line, 0 if side % 2 == 1 else 2)
        sign = 1.0 if side in (1, 2) else -1.0
        patch.append(wet_rows(line) * (DIFFUSE - (sign * 0.5 * ADVECT) * drift) * rims[side])
    south, east, north, west = patch
    for side in range(4):
        patch_ref[8 * side:8 * side + 8, :] = patch[side]
    end = TILE - 1
    whole = [
        south + at_ends(west, 0, 0) + at_ends(east, 0, end),
        east + at_ends(south, end, 0) + at_ends(north, end, end),
        north + at_ends(west, end, 0) + at_ends(east, end, end),
        west + at_ends(south, 0, 0) + at_ends(north, 0, end),
    ]
    press = []
    for side in range(4):
        tracer = base_lines_ref[8 * side:8 * side + 8, :] + whole[side]
        row = row_of(tracer)
        press.append(GRAVITY * jnp.where(row == 5, tracer + pltpu.roll(tracer, 1, 0), tracer))
    outgoing(press, route, (pay0, pay1, pay2, pay3), own_two_ref, False)


def middle_kernel(route, state_ref, base_ref, patch_ref, out_ref):
    state = state_ref[...]
    cell, column = column_of()
    patch = [patch_ref[8 * side:8 * side + 8, :] for side in range(4)]
    base = base_ref[...] + spread(patch, cell, column)
    row = lax.broadcasted_iota(jnp.int32, (8, WIDE), 0)
    pressure = GRAVITY * jnp.where(row == 5, base + pltpu.roll(base, 1, 0), base)
    right, left, up, down, cell, column = neighbours(pressure)
    slope = jnp.where(row < 2, pltpu.roll(right - left, 4, 0), pltpu.roll(up - down, 6, 0))
    swapped = jnp.where(row < 2, pltpu.roll(state, 6, 0), -pltpu.roll(state, 2, 0))
    force = STEP_SIZE * (CORIOLIS * swapped - 0.5 * slope)
    live = jnp.where(route[40] == 1, 1.0, 0.0)
    out_ref[...] = (base + jnp.where(row < 4, wet_rows(state) * force, 0.0)) * live


def last_kernel(route, lines_ref, own_ref, almost_ref, came0, came1, came2, came3, out_ref, full, sems):
    rims = rims_of(route, own_ref, (came0, came1, came2, came3))
    patch = []
    for side in range(4):
        wet = wet_rows(lines_ref[8 * side:8 * side + 8, :])
        row = row_of(wet)
        shift = 4 if side % 2 == 1 else 6
        rim = pltpu.roll(rims[side], shift, 0)
        mine = row < 2 if side % 2 == 1 else (row >= 2) & (row < 4)
        sign = -1.0 if side in (1, 2) else 1.0
        patch.append(jnp.where(mine, (sign * 0.5 * STEP_SIZE) * wet * rim, 0.0))
    cell, column = column_of()
    full[...] = (almost_ref[...] + spread(patch, cell, column))[:, :CELLS]
    copies = [pltpu.make_async_copy(full.at[c], out_ref.at[c, 0], sems.at[c])
              for c in range(6)]
    for copy in copies:
        copy.start()
    for copy in copies:
        copy.wait()


def sds(*shape, dtype=jnp.float32):
    return jax.ShapeDtypeStruct(shape, dtype)


PARAMS = pltpu.CompilerParams(vmem_limit_bytes=16 * 1024 * 1024)


def on_device(nx, ny, fields, wet_mask, tile_of_slot, neighbor, rotation):
    me = (lax.axis_index("gx") * ny + lax.axis_index("gy")).astype(jnp.int32).reshape(1)
    line = sds(8, LANES)
    wide = sds(8, WIDE)
    four = sds(32, LANES)
    state, lines, own, *pays, route = pl.pallas_call(
        lambda *refs: load_kernel((nx, ny), *refs),
        out_shape=[wide, four, four, line, line, line, line, sds(ROUTE, dtype=jnp.int32)],
        in_specs=[SMEM, SMEM, SMEM, SMEM, ANY, ANY],
        out_specs=[VMEM] * 7 + [SMEM],
        scratch_shapes=[pltpu.VMEM((8, CELLS), jnp.float32), pltpu.VMEM((8, CELLS), jnp.int32),
                        pltpu.SemaphoreType.DMA((7,))],
        compiler_params=PARAMS, name="load",
    )(me, tile_of_slot, neighbor.T, rotation.T, fields.reshape(6, 1, CELLS), wet_mask)
    pairs = [pairs_of(link, nx, ny) for link in LINKS]
    came = [lax.ppermute(pay, AXES, pair) for pay, pair in zip(pays, pairs)]
    base, base_lines = pl.pallas_call(
        inner_kernel, out_shape=[wide, four], in_specs=[VMEM], out_specs=[VMEM] * 2,
        compiler_params=PARAMS, name="inner",
        cost_estimate=pl.CostEstimate(flops=2000000, bytes_accessed=600000, transcendentals=0),
    )(state)
    patch, own_two, *pays = pl.pallas_call(
        edge_kernel, out_shape=[four, four, line, line, line, line],
        in_specs=[SMEM] + [VMEM] * 7, out_specs=[VMEM] * 6,
        compiler_params=PARAMS, name="edge",
    )(route, lines, own, base_lines, *came)
    came = [lax.ppermute(pay, AXES, pair) for pay, pair in zip(pays, pairs)]
    almost = pl.pallas_call(
        middle_kernel, out_shape=wide, in_specs=[SMEM] + [VMEM] * 3, out_specs=VMEM,
        compiler_params=PARAMS, name="middle",
        cost_estimate=pl.CostEstimate(flops=2000000, bytes_accessed=800000, transcendentals=0),
    )(route, state, base, patch)
    out = pl.pallas_call(
        last_kernel, out_shape=sds(6, 1, CELLS), in_specs=[SMEM] + [VMEM] * 7, out_specs=ANY,
        scratch_shapes=[pltpu.VMEM((8, CELLS), jnp.float32), pltpu.SemaphoreType.DMA((6,))],
        compiler_params=PARAMS, name="last",
    )(route, lines, own_two, almost, *came)
    return out.reshape(1, 6, CELLS)


def solution(mesh):
    nx, ny = mesh.shape["gx"], mesh.shape["gy"]
    in_specs = (P(AXES, None, None), P(AXES, None), P(), P(), P())
    return jax.shard_map(lambda *args: on_device(nx, ny, *args), mesh=mesh, in_specs=in_specs,
                         out_specs=P(AXES, None, None), check_vma=False)
```

```python
import jax
import jax.numpy as jnp
from jax import lax
from jax.experimental import pallas as pl
from jax.experimental.pallas import tpu as pltpu
from jax.sharding import PartitionSpec as P

TILE = 90
CELLS = TILE * TILE
LANES = 128
CHUNKS = 64
WIDE = LANES * CHUNKS
HALF = 45
LAST = CELLS - TILE - (CHUNKS - 2) * LANES

ADVECT = 0.25
DIFFUSE = 0.15
STEP_SIZE = 0.5
CORIOLIS = 0.3
GRAVITY = 0.8

AXES = ("gx", "gy")
VMEM = pl.BlockSpec(memory_space=pltpu.VMEM)
SMEM = pl.BlockSpec(memory_space=pltpu.SMEM)
ANY = pl.BlockSpec(memory_space=pl.ANY)
HBM = pl.BlockSpec(memory_space=pltpu.HBM)


def link_x_even(x, y, nx, ny):
    return x ^ 1, y


def link_x_odd(x, y, nx, ny):
    return (((x + nx - 1) % nx ^ 1) + 1) % nx, y


def link_y_even(x, y, nx, ny):
    return x, y ^ 1


def link_y_odd(x, y, nx, ny):
    if y == 0 or y == ny - 1:
        return (x + nx // 2) % nx, y
    return x, ((y - 1) ^ 1) + 1


LINKS = (link_y_odd, link_x_even, link_y_even, link_x_odd)


def pairs_of(link, nx, ny):
    out = []
    for x in range(nx):
        for y in range(ny):
            to_x, to_y = link(x, y, nx, ny)
            out.append((x * ny + y, to_x * ny + to_y))
    return out


FIRST_ORDER = (0, 3, 2, 1)
SECOND_ORDER = (2, 0, 3, 1)


def exchanged(pays, order, nx, ny):
    return [lax.ppermute(pay, AXES, pairs_of(LINKS[link], nx, ny)) for pay, link in zip(pays, order)]


def by_link(refs, order):
    return [refs[order.index(link)] for link in range(len(LINKS))]


def partner(me, which, nx, ny):
    x, y = me // ny, me % ny
    if which == 0:
        pole = (y == 0) | (y == ny - 1)
        step = jnp.where(y % 2 == 1, 1, -1)
        return jnp.where(pole, (x + nx // 2) % nx * ny + y, me + step)
    if which == 1:
        return me + jnp.where(x % 2 == 0, ny, -ny)
    if which == 2:
        return me + jnp.where(y % 2 == 0, 1, -1)
    return (x + jnp.where(x % 2 == 1, 1, nx - 1)) % nx * ny + y


def lanes():
    return lax.broadcasted_iota(jnp.int32, (8, LANES), 1)


def rows():
    return lax.broadcasted_iota(jnp.int32, (8, LANES), 0)


def pick(values, index):
    return jnp.take_along_axis(values, index, axis=1)


def tiled(values, count):
    return jnp.concatenate([values] * count, axis=1)


def column_of():
    cell = lax.broadcasted_iota(jnp.int32, (8, WIDE), 1)
    line = jnp.floor((cell.astype(jnp.float32) + 0.5) * (1.0 / TILE)).astype(jnp.int32)
    return cell, cell - TILE * line


def edge_lines(state, column):
    lane = lanes()
    edge = (column == 0) | (column == TILE - 1)
    parts = []
    for low, high in ((0, HALF), (HALF, CHUNKS)):
        found = jnp.zeros((8, LANES), jnp.float32)
        for c in range(low, high):
            cut = slice(c * LANES, (c + 1) * LANES)
            found = jnp.where(edge[:, cut], state[:, cut], found)
        parts.append(found)
    east_at = (TILE * lane + TILE - 1) & (LANES - 1)
    west_at = (TILE * lane) & (LANES - 1)
    east = jnp.where(lane < 64, pick(parts[0], east_at), pick(parts[1], east_at))
    west = jnp.where(lane < 64, pick(parts[0], west_at), pick(parts[1], west_at))
    south = state[:, :LANES]
    before = pltpu.roll(state[:, (CHUNKS - 2) * LANES:(CHUNKS - 1) * LANES], LANES - LAST, 1)
    after = pltpu.roll(state[:, (CHUNKS - 1) * LANES:], LANES - LAST, 1)
    north = jnp.where(lane < LANES - LAST, before, after)
    return [south, east, north, west]


def spread(lines, cell, column):
    south, east, north, west = lines
    lane = lanes()
    odd = (lane & 1) == 1
    line_at = (37 * ((lane + jnp.where(odd, 39, 0)) >> 1)) & 63
    early = jnp.where(odd, pick(east, line_at), pick(west, line_at))
    late = jnp.where(odd, pick(east, line_at + 64), pick(west, line_at + 64))
    sides = jnp.concatenate([early] * HALF + [late] * (CHUNKS - HALF), axis=1)
    edge = (column == 0) | (column == TILE - 1)
    out = jnp.where(edge, sides, 0.0)
    first = jnp.where(lane < TILE, south, 0.0) + out[:, :LANES]
    moved = pltpu.roll(north, LAST, 1)
    before = out[:, (CHUNKS - 2) * LANES:(CHUNKS - 1) * LANES] + jnp.where(lane >= LAST, moved, 0.0)
    after = out[:, (CHUNKS - 1) * LANES:] + jnp.where(lane < LAST + TILE - LANES, moved, 0.0)
    return jnp.concatenate([first, out[:, LANES:(CHUNKS - 2) * LANES], before, after], axis=1)


def neighbours(state):
    cell, column = column_of()
    right = jnp.where(column == TILE - 1, 0.0, pltpu.roll(state, WIDE - 1, 1))
    left = jnp.where(column == 0, 0.0, pltpu.roll(state, 1, 1))
    up = jnp.where(cell >= CELLS - TILE, 0.0, pltpu.roll(state, WIDE - TILE, 1))
    down = jnp.where(cell < TILE, 0.0, pltpu.roll(state, TILE, 1))
    return right, left, up, down, cell, column


def row_of(values):
    return lax.broadcasted_iota(jnp.int32, values.shape, 0)


def repeated(values, first):
    row = row_of(values)
    if first == 0:
        pair = jnp.where(row < 2, values, pltpu.roll(values, 2, 0))
    else:
        pair = jnp.where(row < 4, values, pltpu.roll(values, 2, 0))
        pair = jnp.where(row < 2, pltpu.roll(values, 6, 0), pair)
        return pair
    return jnp.where(row < 4, pair, pltpu.roll(values, 4, 0))


def wet_rows(values):
    return jnp.broadcast_to(values[6:7], values.shape)


def turned(line, turns):
    row = row_of(line)
    swapped = jnp.where(row < 2, pltpu.roll(line, 6, 0), pltpu.roll(line, 2, 0))
    velocity = row < 4
    second = jnp.where(row < 2, swapped, -swapped)
    odd = jnp.where(turns % 2 == 1, 1, 0)
    out = jnp.where(jnp.logical_and(velocity, odd == 1), second, line)
    back = jnp.where(turns >= 2, 1, 0)
    return jnp.where(jnp.logical_and(velocity, back == 1), -out, out)


def flipped(line):
    return pick(line, jnp.maximum(TILE - 1 - lanes(), 0))


ROUTE = 48


def outgoing(lines, route, pay_refs, own_ref, vector):
    sent = []
    for side in range(4):
        line = jnp.where(route[32 + side] == 1, flipped(lines[side]), lines[side])
        if vector:
            line = turned(line, route[36 + side])
        sent.append(line)
    for link in range(4):
        total = jnp.zeros((8, LANES), jnp.float32)
        for side in range(4):
            total = jnp.where(route[4 * link + side] == 1, sent[side], total)
        pay_refs[link][...] = total
    for target in range(4):
        total = jnp.zeros((8, LANES), jnp.float32)
        for side in range(4):
            total = jnp.where(route[16 + 4 * side + target] == 1, sent[side], total)
        own_ref[8 * target:8 * target + 8, :] = total


def rims_of(route, own_ref, came_refs):
    out = []
    for side in range(4):
        rim = own_ref[8 * side:8 * side + 8, :]
        for link in range(4):
            rim = jnp.where(route[4 * link + side] == 1, came_refs[link][...], rim)
        out.append(rim)
    return out


def raw_lines(chunk_of, low_row):
    lane = lanes()
    odd = lane & 1
    line_at = (37 * ((lane + 39 * odd) >> 1)) & 63
    home = (TILE * line_at + (TILE - 1) * odd) >> 7
    parts = []
    for low, high in ((0, HALF), (HALF, CHUNKS)):
        found = chunk_of(low)
        for c in range(low + 1, high):
            found = jnp.where(home == c - low, chunk_of(c), found)
        parts.append(found)
    early = lane < 64
    east_at = (TILE * lane + TILE - 1) & (LANES - 1)
    west_at = (TILE * lane) & (LANES - 1)
    east = jnp.where(early, pick(parts[0], east_at), pick(parts[1], east_at))
    west = jnp.where(early, pick(parts[0], west_at), pick(parts[1], west_at))
    before = pltpu.roll(chunk_of(CHUNKS - 2), LANES - LAST, 1)
    after = pltpu.roll(chunk_of(CHUNKS - 1), LANES - LAST, 1)
    north = jnp.where(lane < LANES - LAST, before, after)
    return [chunk_of(0), east, north, west]


def load_kernel(shape, me_ref, tiles_hbm, near_hbm, turn_hbm, fields_ref, wet_ref,
                raw, wet_raw, lines_ref, own_ref, pay0, pay1, pay2, pay3, route,
                tiles_ref, near_ref, turn_ref, sems):
    nx, ny = shape
    tables = [pltpu.make_async_copy(tiles_hbm, tiles_ref, sems.at[7]),
              pltpu.make_async_copy(near_hbm, near_ref, sems.at[8]),
              pltpu.make_async_copy(turn_hbm, turn_ref, sems.at[9])]
    copies = [pltpu.make_async_copy(fields_ref.at[c, 0], raw.at[c], sems.at[c]) for c in range(6)]
    copies.append(pltpu.make_async_copy(wet_ref.at[0], wet_raw.at[0], sems.at[6]))
    for copy in tables + copies:
        copy.start()
    for copy in tables:
        copy.wait()
    me = me_ref[0]
    tile = tiles_ref[me]
    live = tile >= 0
    held = jnp.maximum(tile, 0)
    near = [jnp.where(live, near_ref[side, held], -1) for side in range(4)]
    turn = [turn_ref[side, held] for side in range(4)]
    for link in range(4):
        other = tiles_ref[partner(me, link, nx, ny)]
        for side in range(4):
            route[4 * link + side] = jnp.where((near[side] >= 0) & (near[side] == other), 1, 0)
    for side in range(4):
        target = (side + 2 + turn[side]) % 4
        for k in range(4):
            route[16 + 4 * side + k] = jnp.where((near[side] >= 0) & (near[side] == tile) & (target == k), 1, 0)
        route[32 + side] = jnp.where((target < 2) != (side >= 2), 1, 0)
        route[36 + side] = (4 - turn[side]) % 4
    route[40] = jnp.where(live, 1, 0)
    for copy in copies:
        copy.wait()

    def chunk(ref, c):
        if c < CHUNKS - 1:
            return ref[:, c * LANES:(c + 1) * LANES]
        rest = CELLS - c * LANES
        part = ref[:, c * LANES:CELLS]
        return jnp.concatenate([part, jnp.zeros((8, LANES - rest), part.dtype)], axis=1)

    values = raw_lines(lambda c: chunk(raw, c), 0)
    wets = raw_lines(lambda c: chunk(wet_raw, c), 0)
    row = rows()
    lines = []
    for value, wet in zip(values, wets):
        wet = jnp.broadcast_to(wet[0:1], (8, LANES)).astype(jnp.float32)
        lines.append(jnp.where(row < 6, value * wet, jnp.where(row == 6, wet, 0.0)))
    for side in range(4):
        lines_ref[8 * side:8 * side + 8, :] = lines[side]
    outgoing(lines, route, by_link((pay0, pay1, pay2, pay3), FIRST_ORDER), own_ref, True)


def inner_kernel(raw, wet_raw, state_ref, base_ref, base_lines_ref):
    state_ref[:, (CHUNKS - 1) * LANES:] = jnp.zeros((8, LANES), jnp.float32)
    for low, high in ((0, (CHUNKS - 1) * LANES), ((CHUNKS - 1) * LANES, CELLS)):
        size = (8, high - low)
        row = lax.broadcasted_iota(jnp.int32, size, 0)
        wet = jnp.broadcast_to(wet_raw[0:1, low:high].astype(jnp.float32), size)
        state_ref[:, low:high] = jnp.where(row < 6, raw[:, low:high] * wet, jnp.where(row == 6, wet, 0.0))
    state = state_ref[...]
    right, left, up, down, cell, column = neighbours(state)
    first, second, wet = repeated(state, 0), repeated(state, 2), wet_rows(state)
    along = first * (right - left) + second * (up - down)
    round_sum = right + left + up + down - 4.0 * state
    base = wet * (state - (0.5 * ADVECT) * along + DIFFUSE * round_sum)
    base_ref[...] = base
    lines = edge_lines(base, column)
    for side in range(4):
        base_lines_ref[8 * side:8 * side + 8, :] = lines[side]


def at_ends(line, lane_from, lane_to):
    value = jnp.broadcast_to(line[:, lane_from:lane_from + 1], (8, LANES))
    return jnp.where(lanes() == lane_to, value, 0.0)


def edge_kernel(route, lines_ref, own_ref, base_lines_ref, came0, came1, came2, came3,
                patch_ref, own_two_ref, pay0, pay1, pay2, pay3):
    rims = rims_of(route, own_ref, by_link((came0, came1, came2, came3), FIRST_ORDER))
    patch = []
    for side in range(4):
        line = lines_ref[8 * side:8 * side + 8, :]
        drift = repeated(line, 0 if side % 2 == 1 else 2)
        sign = 1.0 if side in (1, 2) else -1.0
        patch.append(wet_rows(line) * (DIFFUSE - (sign * 0.5 * ADVECT) * drift) * rims[side])
    south, east, north, west = patch
    for side in range(4):
        patch_ref[8 * side:8 * side + 8, :] = patch[side]
    end = TILE - 1
    whole = [
        south + at_ends(west, 0, 0) + at_ends(east, 0, end),
        east + at_ends(south, end, 0) + at_ends(north, end, end),
        north + at_ends(west, end, 0) + at_ends(east, end, end),
        west + at_ends(south, 0, 0) + at_ends(north, 0, end),
    ]
    press = []
    for side in range(4):
        tracer = base_lines_ref[8 * side:8 * side + 8, :] + whole[side]
        row = row_of(tracer)
        press.append(GRAVITY * jnp.where(row == 5, tracer + pltpu.roll(tracer, 1, 0), tracer))
    outgoing(press, route, by_link((pay0, pay1, pay2, pay3), SECOND_ORDER), own_two_ref, False)


def middle_kernel(route, state_ref, base_ref, patch_ref, out_ref):
    state = state_ref[...]
    cell, column = column_of()
    patch = [patch_ref[8 * side:8 * side + 8, :] for side in range(4)]
    base = base_ref[...] + spread(patch, cell, column)
    row = lax.broadcasted_iota(jnp.int32, (8, WIDE), 0)
    pressure = GRAVITY * jnp.where(row == 5, base + pltpu.roll(base, 1, 0), base)
    right, left, up, down, cell, column = neighbours(pressure)
    slope = jnp.where(row < 2, pltpu.roll(right - left, 4, 0), pltpu.roll(up - down, 6, 0))
    swapped = jnp.where(row < 2, pltpu.roll(state, 6, 0), -pltpu.roll(state, 2, 0))
    force = STEP_SIZE * (CORIOLIS * swapped - 0.5 * slope)
    live = jnp.where(route[40] == 1, 1.0, 0.0)
    out_ref[...] = (base + jnp.where(row < 4, wet_rows(state) * force, 0.0)) * live


def last_kernel(route, lines_ref, own_ref, almost_ref, came0, came1, came2, came3, out_ref, full, sems):
    rims = rims_of(route, own_ref, by_link((came0, came1, came2, came3), SECOND_ORDER))
    patch = []
    for side in range(4):
        wet = wet_rows(lines_ref[8 * side:8 * side + 8, :])
        row = row_of(wet)
        shift = 4 if side % 2 == 1 else 6
        rim = pltpu.roll(rims[side], shift, 0)
        mine = row < 2 if side % 2 == 1 else (row >= 2) & (row < 4)
        sign = -1.0 if side in (1, 2) else 1.0
        patch.append(jnp.where(mine, (sign * 0.5 * STEP_SIZE) * wet * rim, 0.0))
    cell, column = column_of()
    full[...] = (almost_ref[...] + spread(patch, cell, column))[:, :CELLS]
    copies = [pltpu.make_async_copy(full.at[c], out_ref.at[c, 0], sems.at[c])
              for c in range(6)]
    for copy in copies:
        copy.start()
    for copy in copies:
        copy.wait()


def sds(*shape, dtype=jnp.float32):
    return jax.ShapeDtypeStruct(shape, dtype)


PARAMS = pltpu.CompilerParams(vmem_limit_bytes=16 * 1024 * 1024)


def on_device(nx, ny, fields, wet_mask, tile_of_slot, neighbor, rotation):
    me = (lax.axis_index("gx") * ny + lax.axis_index("gy")).astype(jnp.int32).reshape(1)
    line = sds(8, LANES)
    wide = sds(8, WIDE)
    four = sds(32, LANES)
    raw, wet_raw, lines, own, *pays, route = pl.pallas_call(
        lambda *refs: load_kernel((nx, ny), *refs),
        out_shape=[sds(8, CELLS), sds(8, CELLS, dtype=jnp.int32), four, four, line, line, line, line,
                   sds(ROUTE, dtype=jnp.int32)],
        in_specs=[SMEM] + [HBM] * 5,
        out_specs=[VMEM] * 8 + [SMEM],
        scratch_shapes=[pltpu.SMEM((nx * ny,), jnp.int32), pltpu.SMEM((4, nx * ny), jnp.int32),
                        pltpu.SMEM((4, nx * ny), jnp.int32), pltpu.SemaphoreType.DMA((10,))],
        compiler_params=PARAMS, name="load",
    )(me, *(pltpu.with_memory_space_constraint(v, pltpu.HBM) for v in (tile_of_slot, neighbor.T, rotation.T, fields.reshape(6, 1, CELLS), wet_mask)))
    came = exchanged(pays, FIRST_ORDER, nx, ny)
    state, base, base_lines = pl.pallas_call(
        inner_kernel, out_shape=[wide, wide, four], in_specs=[VMEM] * 2, out_specs=[VMEM] * 3,
        compiler_params=PARAMS, name="inner",
        cost_estimate=pl.CostEstimate(flops=2000000, bytes_accessed=600000, transcendentals=0),
    )(raw, wet_raw)
    patch, own_two, *pays = pl.pallas_call(
        edge_kernel, out_shape=[four, four, line, line, line, line],
        in_specs=[SMEM] + [VMEM] * 7, out_specs=[VMEM] * 6,
        compiler_params=PARAMS, name="edge",
    )(route, lines, own, base_lines, *came)
    came = exchanged(pays, SECOND_ORDER, nx, ny)
    almost = pl.pallas_call(
        middle_kernel, out_shape=wide, in_specs=[SMEM] + [VMEM] * 3, out_specs=VMEM,
        compiler_params=PARAMS, name="middle",
        cost_estimate=pl.CostEstimate(flops=2000000, bytes_accessed=800000, transcendentals=0),
    )(route, state, base, patch)
    out = pl.pallas_call(
        last_kernel, out_shape=sds(6, 1, CELLS), in_specs=[SMEM] + [VMEM] * 7, out_specs=ANY,
        scratch_shapes=[pltpu.VMEM((8, CELLS), jnp.float32), pltpu.SemaphoreType.DMA((6,))],
        compiler_params=PARAMS, name="last",
    )(route, lines, own_two, almost, *came)
    return out.reshape(1, 6, CELLS)


def solution(mesh):
    nx, ny = mesh.shape["gx"], mesh.shape["gy"]
    in_specs = (P(AXES, None, None), P(AXES, None), P(), P(), P())
    return jax.shard_map(lambda *args: on_device(nx, ny, *args), mesh=mesh, in_specs=in_specs,
                         out_specs=P(AXES, None, None), check_vma=False)
```

```python
import jax
import jax.numpy as jnp
from jax import lax
from jax.experimental import pallas as pl
from jax.experimental.pallas import tpu as pltpu
from jax.sharding import PartitionSpec as P

TILE = 90
CELLS = TILE * TILE
LANES = 128
CHUNKS = 64
WIDE = LANES * CHUNKS
HALF = 45
LAST = CELLS - TILE - (CHUNKS - 2) * LANES

ADVECT = 0.25
DIFFUSE = 0.15
STEP_SIZE = 0.5
CORIOLIS = 0.3
GRAVITY = 0.8

AXES = ("gx", "gy")
VMEM = pl.BlockSpec(memory_space=pltpu.VMEM)
SMEM = pl.BlockSpec(memory_space=pltpu.SMEM)
ANY = pl.BlockSpec(memory_space=pl.ANY)
HBM = pl.BlockSpec(memory_space=pltpu.HBM)


def link_x_even(x, y, nx, ny):
    return x ^ 1, y


def link_x_odd(x, y, nx, ny):
    return (((x + nx - 1) % nx ^ 1) + 1) % nx, y


def link_y_even(x, y, nx, ny):
    return x, y ^ 1


def link_y_odd(x, y, nx, ny):
    if y == 0 or y == ny - 1:
        return (x + nx // 2) % nx, y
    return x, ((y - 1) ^ 1) + 1


LINKS = (link_y_odd, link_x_even, link_y_even, link_x_odd)


def pairs_of(link, nx, ny):
    out = []
    for x in range(nx):
        for y in range(ny):
            to_x, to_y = link(x, y, nx, ny)
            out.append((x * ny + y, to_x * ny + to_y))
    return out


X_ORDER = (3, 1)
U_ORDER = (0, 2)
BOTH = X_ORDER + U_ORDER
SECOND_ORDER = (2, 0, 3, 1)


def exchanged(pays, order, nx, ny):
    return [lax.ppermute(pay, AXES, pairs_of(LINKS[link], nx, ny)) for pay, link in zip(pays, order)]


def by_link(refs, order, links=(0, 1, 2, 3)):
    return [refs[order.index(link)] for link in links]


def partner(me, which, nx, ny):
    x, y = me // ny, me % ny
    if which == 0:
        pole = (y == 0) | (y == ny - 1)
        step = jnp.where(y % 2 == 1, 1, -1)
        return jnp.where(pole, (x + nx // 2) % nx * ny + y, me + step)
    if which == 1:
        return me + jnp.where(x % 2 == 0, ny, -ny)
    if which == 2:
        return me + jnp.where(y % 2 == 0, 1, -1)
    return (x + jnp.where(x % 2 == 1, 1, nx - 1)) % nx * ny + y


def lanes():
    return lax.broadcasted_iota(jnp.int32, (8, LANES), 1)


def rows():
    return lax.broadcasted_iota(jnp.int32, (8, LANES), 0)


def pick(values, index):
    return jnp.take_along_axis(values, index, axis=1)


def tiled(values, count):
    return jnp.concatenate([values] * count, axis=1)


def column_of():
    cell = lax.broadcasted_iota(jnp.int32, (8, WIDE), 1)
    line = jnp.floor((cell.astype(jnp.float32) + 0.5) * (1.0 / TILE)).astype(jnp.int32)
    return cell, cell - TILE * line


def edge_lines(state, column):
    lane = lanes()
    edge = (column == 0) | (column == TILE - 1)
    parts = []
    for low, high in ((0, HALF), (HALF, CHUNKS)):
        found = jnp.zeros((8, LANES), jnp.float32)
        for c in range(low, high):
            cut = slice(c * LANES, (c + 1) * LANES)
            found = jnp.where(edge[:, cut], state[:, cut], found)
        parts.append(found)
    east_at = (TILE * lane + TILE - 1) & (LANES - 1)
    west_at = (TILE * lane) & (LANES - 1)
    east = jnp.where(lane < 64, pick(parts[0], east_at), pick(parts[1], east_at))
    west = jnp.where(lane < 64, pick(parts[0], west_at), pick(parts[1], west_at))
    south = state[:, :LANES]
    before = pltpu.roll(state[:, (CHUNKS - 2) * LANES:(CHUNKS - 1) * LANES], LANES - LAST, 1)
    after = pltpu.roll(state[:, (CHUNKS - 1) * LANES:], LANES - LAST, 1)
    north = jnp.where(lane < LANES - LAST, before, after)
    return [south, east, north, west]


def spread(lines, cell, column):
    south, east, north, west = lines
    lane = lanes()
    odd = (lane & 1) == 1
    line_at = (37 * ((lane + jnp.where(odd, 39, 0)) >> 1)) & 63
    early = jnp.where(odd, pick(east, line_at), pick(west, line_at))
    late = jnp.where(odd, pick(east, line_at + 64), pick(west, line_at + 64))
    sides = jnp.concatenate([early] * HALF + [late] * (CHUNKS - HALF), axis=1)
    edge = (column == 0) | (column == TILE - 1)
    out = jnp.where(edge, sides, 0.0)
    first = jnp.where(lane < TILE, south, 0.0) + out[:, :LANES]
    moved = pltpu.roll(north, LAST, 1)
    before = out[:, (CHUNKS - 2) * LANES:(CHUNKS - 1) * LANES] + jnp.where(lane >= LAST, moved, 0.0)
    after = out[:, (CHUNKS - 1) * LANES:] + jnp.where(lane < LAST + TILE - LANES, moved, 0.0)
    return jnp.concatenate([first, out[:, LANES:(CHUNKS - 2) * LANES], before, after], axis=1)


def neighbours(state):
    cell, column = column_of()
    right = jnp.where(column == TILE - 1, 0.0, pltpu.roll(state, WIDE - 1, 1))
    left = jnp.where(column == 0, 0.0, pltpu.roll(state, 1, 1))
    up = jnp.where(cell >= CELLS - TILE, 0.0, pltpu.roll(state, WIDE - TILE, 1))
    down = jnp.where(cell < TILE, 0.0, pltpu.roll(state, TILE, 1))
    return right, left, up, down, cell, column


def row_of(values):
    return lax.broadcasted_iota(jnp.int32, values.shape, 0)


def repeated(values, first):
    row = row_of(values)
    if first == 0:
        pair = jnp.where(row < 2, values, pltpu.roll(values, 2, 0))
    else:
        pair = jnp.where(row < 4, values, pltpu.roll(values, 2, 0))
        pair = jnp.where(row < 2, pltpu.roll(values, 6, 0), pair)
        return pair
    return jnp.where(row < 4, pair, pltpu.roll(values, 4, 0))


def wet_rows(values):
    return jnp.broadcast_to(values[6:7], values.shape)


def turned(line, turns):
    row = row_of(line)
    swapped = jnp.where(row < 2, pltpu.roll(line, 6, 0), pltpu.roll(line, 2, 0))
    velocity = row < 4
    second = jnp.where(row < 2, swapped, -swapped)
    odd = jnp.where(turns % 2 == 1, 1, 0)
    out = jnp.where(jnp.logical_and(velocity, odd == 1), second, line)
    back = jnp.where(turns >= 2, 1, 0)
    return jnp.where(jnp.logical_and(velocity, back == 1), -out, out)


def flipped(line):
    return pick(line, jnp.maximum(TILE - 1 - lanes(), 0))


ROUTE = 48
OWN_AT, RELAY_AT = TILE, {1: TILE + 4, 3: TILE + 8}


class Rows:
    def __init__(self, ref):
        self.ref = ref

    def __getitem__(self, i):
        return jnp.broadcast_to(self.ref[i:i + 1, :], (8, LANES))


def my_index(ny):
    return lax.axis_index("gx") * ny + lax.axis_index("gy")


def sent_line(line, side, route, vector):
    line = jnp.where(route[32 + side] == 1, flipped(line), line)
    return turned(line, route[36 + side]) if vector else line


def chosen(lines, route, link):
    total = jnp.zeros((8, LANES), jnp.float32)
    for side in range(4):
        total = jnp.where(route[4 * link + side] == 1, lines[side], total)
    return total


def own_rims(sent, route):
    out = []
    for target in range(4):
        total = jnp.zeros((8, LANES), jnp.float32)
        for side in range(4):
            total = jnp.where(route[16 + 4 * side + target] == 1, sent[side], total)
        out.append(total)
    return out


def rims_of(route, base, came):
    out = []
    for side in range(4):
        rim = base[side] if base is not None else jnp.zeros((8, LANES), jnp.float32)
        for link in range(4):
            rim = jnp.where(route[4 * link + side] == 1, came[link], rim)
        out.append(rim)
    return out


def four_of(ref):
    return [ref[8 * side:8 * side + 8, :] for side in range(4)]


def columns_at(step):
    lane = lanes()
    odd = lane & 1
    shift = jnp.where(odd == 1, 39 + step, -step) if step % 2 == 0 else jnp.where(odd == 1, -step, 39 + step)
    column = jnp.where(odd == 1, TILE - 1 - step, step) if step % 2 == 0 else jnp.where(odd == 1, step, TILE - 1 - step)
    line_at = (37 * ((lane + shift) >> 1)) & 63
    return line_at, (TILE * line_at + column) >> 7


def raw_lines(chunk_of, step):
    lane = lanes()
    _, home = columns_at(step)
    parts = []
    for low, high in ((0, HALF), (HALF, CHUNKS)):
        found = chunk_of(low)
        for c in range(low + 1, high):
            found = jnp.where(home == c - low, chunk_of(c), found)
        parts.append(found)
    early = lane < 64
    out = [None] * 4
    for side, column in ((1, TILE - 1 - step), (3, step)):
        at = (TILE * lane + column) & (LANES - 1)
        out[side] = jnp.where(early, pick(parts[0], at), pick(parts[1], at))
    for side, first in ((0, TILE * step), (2, CELLS - TILE - TILE * step)):
        low, start = first // LANES, first % LANES
        if start == 0:
            out[side] = chunk_of(low)
        else:
            before = pltpu.roll(chunk_of(low), LANES - start, 1)
            after = pltpu.roll(chunk_of(low + 1), LANES - start, 1)
            out[side] = jnp.where(lane < LANES - start, before, after)
    return out


def spread_chunks(lines, step):
    lane = lanes()
    line_at, home = columns_at(step)
    odd = (lane & 1) == 1
    first_odd, first_even = (lines[1], lines[3]) if step % 2 == 0 else (lines[3], lines[1])
    early = jnp.where(odd, pick(first_odd, line_at), pick(first_even, line_at))
    late = jnp.where(odd, pick(first_odd, line_at + 64), pick(first_even, line_at + 64))
    out = []
    for c in range(CHUNKS):
        out.append(jnp.where(home == (c if c < HALF else c - HALF), early if c < HALF else late, 0.0))
    for side, first in ((0, TILE * step), (2, CELLS - TILE - TILE * step)):
        low, start = first // LANES, first % LANES
        line = jnp.where(lane < TILE, lines[side], 0.0)
        if start == 0:
            out[low] = out[low] + line
        else:
            moved = pltpu.roll(line, start, 1)
            out[low] = out[low] + jnp.where(lane >= start, moved, 0.0)
            if start + TILE > LANES:
                out[low + 1] = out[low + 1] + jnp.where(lane < start + TILE - LANES, moved, 0.0)
    return out


def load_kernel(shape, tiles_hbm, near_hbm, turn_hbm, fields_ref, wet_ref,
                raw, wet_raw, lines_ref, inner_ref, pay0, pay1, pay2, pay3, route_ref,
                tiles_ref, near_ref, turn_ref, sems):
    nx, ny = shape
    tables = [pltpu.make_async_copy(tiles_hbm, tiles_ref, sems.at[7]),
              pltpu.make_async_copy(near_hbm, near_ref, sems.at[8]),
              pltpu.make_async_copy(turn_hbm, turn_ref, sems.at[9])]
    copies = [pltpu.make_async_copy(fields_ref.at[c, 0], raw.at[c], sems.at[c]) for c in range(6)]
    copies.append(pltpu.make_async_copy(wet_ref.at[0], wet_raw.at[0], sems.at[6]))
    for copy in tables + copies:
        copy.start()
    for copy in tables:
        copy.wait()
    me = my_index(ny)
    route = [None] * ROUTE
    tile = tiles_ref[me]
    live = tile >= 0
    held = jnp.maximum(tile, 0)
    near = [jnp.where(live, near_ref[side, held], -1) for side in range(4)]
    turn = [turn_ref[side, held] for side in range(4)]
    for link in range(4):
        other = tiles_ref[partner(me, link, nx, ny)]
        for side in range(4):
            route[4 * link + side] = jnp.where((near[side] >= 0) & (near[side] == other), 1, 0)
    for side in range(4):
        target = (side + 2 + turn[side]) % 4
        for k in range(4):
            route[16 + 4 * side + k] = jnp.where((near[side] >= 0) & (near[side] == tile) & (target == k), 1, 0)
        route[32 + side] = jnp.where((target < 2) != (side >= 2), 1, 0)
        route[36 + side] = (4 - turn[side]) % 4
    route[40] = jnp.where(live, 1, 0)
    for i in range(41):
        route_ref[i:i + 1, :] = jnp.full((1, LANES), route[i], jnp.int32)
    for copy in copies:
        copy.wait()

    def chunk(ref, c):
        if c < CHUNKS - 1:
            return ref[:, c * LANES:(c + 1) * LANES]
        rest = CELLS - c * LANES
        part = ref[:, c * LANES:CELLS]
        return jnp.concatenate([part, jnp.zeros((8, LANES - rest), part.dtype)], axis=1)

    row, lane = rows(), lanes()
    both = []
    for step, ref in ((0, lines_ref), (1, inner_ref)):
        lines = []
        for value, wet in zip(raw_lines(lambda c: chunk(raw, c), step), raw_lines(lambda c: chunk(wet_raw, c), step)):
            wet = jnp.broadcast_to(wet[0:1], (8, LANES)).astype(jnp.float32)
            lines.append(jnp.where(row < 6, value * wet, jnp.where(row == 6, wet, 0.0)))
        for side in range(4):
            ref[8 * side:8 * side + 8, :] = lines[side]
        both.append(lines)
    ends = [jnp.where((lane == OWN_AT + 1) | (lane == OWN_AT + 2), TILE - 1, 0)] * 2
    corners = jnp.where(lane < OWN_AT + 2, pick(both[0][0], ends[0]), pick(both[0][2], ends[1]))
    at_corners = (lane >= OWN_AT) & (lane < OWN_AT + 4)
    sent = [sent_line(both[0][side], side, route, True) for side in range(4)]
    sent_inner = [sent_line(both[1][side], side, route, False) for side in range(4)]
    for link, pay in zip(BOTH, (pay0, pay1, pay2, pay3)):
        pay[0:8, :] = jnp.where(at_corners, corners, chosen(sent, route, link))
        pay[8:16, :] = chosen(sent_inner, route, link)


def pressure_of(tracer, row):
    return GRAVITY * jnp.where(row == 5, tracer + pltpu.roll(tracer, 1, 0), tracer)


def force_of(state, base, row):
    right, left, up, down, cell, column = neighbours(pressure_of(base, row))
    slope = jnp.where(row < 2, pltpu.roll(right - left, 4, 0), pltpu.roll(up - down, 6, 0))
    swapped = jnp.where(row < 2, pltpu.roll(state, 6, 0), -pltpu.roll(state, 2, 0))
    force = STEP_SIZE * (CORIOLIS * swapped - 0.5 * slope)
    return jnp.where(row < 4, wet_rows(state) * force, 0.0)


def masked_state(raw, wet_raw, state_ref):
    state_ref[:, (CHUNKS - 1) * LANES:] = jnp.zeros((8, LANES), jnp.float32)
    for low, high in ((0, (CHUNKS - 1) * LANES), ((CHUNKS - 1) * LANES, CELLS)):
        size = (8, high - low)
        row = lax.broadcasted_iota(jnp.int32, size, 0)
        wet = jnp.broadcast_to(wet_raw[0:1, low:high].astype(jnp.float32), size)
        state_ref[:, low:high] = jnp.where(row < 6, raw[:, low:high] * wet, jnp.where(row == 6, wet, 0.0))
    return state_ref[...]


def without_rims(state):
    right, left, up, down, cell, column = neighbours(state)
    first, second, wet = repeated(state, 0), repeated(state, 2), wet_rows(state)
    along = first * (right - left) + second * (up - down)
    round_sum = right + left + up + down - 4.0 * state
    return wet * (state - (0.5 * ADVECT) * along + DIFFUSE * round_sum), column


def if_live(route_ref, values):
    return jnp.where(tiled(Rows(route_ref)[40], CHUNKS) == 1, values, 0.0)


def base_kernel(raw, wet_raw, state_ref, base_ref, base_lines_ref):
    state = masked_state(raw, wet_raw, state_ref)
    base, column = without_rims(state)
    base_ref[...] = base
    lines = edge_lines(base, column)
    for side in range(4):
        base_lines_ref[8 * side:8 * side + 8, :] = lines[side]


def check_kernel(shape, tiles_hbm, near_hbm, flag, tiles_ref, near_ref, sems):
    nx, ny = shape
    copies = [pltpu.make_async_copy(tiles_hbm, tiles_ref, sems.at[0]),
              pltpu.make_async_copy(near_hbm, near_ref.at[0:4], sems.at[1])]
    for copy in copies:
        copy.start()
    for copy in copies:
        copy.wait()
    row, lane = rows(), lanes()
    tiles = [jnp.broadcast_to(tiles_ref[half:half + 1, :], (8, LANES)) for half in range(2)]
    near = [near_ref[:, half * LANES:(half + 1) * LANES] for half in range(2)]

    def look(table, index):
        return jnp.where(index < LANES, pick(table[0], index & (LANES - 1)), pick(table[1], index & (LANES - 1)))

    worst = jnp.zeros((8, LANES), jnp.int32)
    for half in range(2):
        tile = tiles[half]
        mine = look(near, jnp.maximum(tile, 0))
        linked = (tile >= 0) & (mine >= 0) & (row < 4)
        other = [look(tiles, partner(lane + half * LANES, link, nx, ny)) for link in range(4)]
        over_x = (mine == other[1]) | (mine == other[3])
        kind = jnp.where(linked, jnp.where(mine == tile, 4, jnp.where(over_x, 1, 2)), 0)
        after = jnp.where(row < 3, pltpu.roll(kind, 7, 0), pltpu.roll(kind, 3, 0))
        odd = (kind == 4) | ((kind > 0) & (kind == after) & (row < 4))
        worst = jnp.where(odd, 1, worst)
    flag[0] = jnp.max(worst)


def plan_kernel(shape, tiles_hbm, near_hbm, turn_hbm, raw, wet_raw, route_ref, plan_ref, almost_ref,
                state_ref, tiles_ref, near_ref, turn_ref, sems):
    nx, ny = shape
    copies = [pltpu.make_async_copy(tiles_hbm, tiles_ref, sems.at[0]),
              pltpu.make_async_copy(near_hbm, near_ref, sems.at[1]),
              pltpu.make_async_copy(turn_hbm, turn_ref, sems.at[2])]
    for copy in copies:
        copy.start()
    state = masked_state(raw, wet_raw, state_ref)
    base, _ = without_rims(state)
    row = lax.broadcasted_iota(jnp.int32, (8, WIDE), 0)
    almost_ref[...] = if_live(route_ref, base + force_of(state, base, row))
    for copy in copies:
        copy.wait()
    me = my_index(ny)
    tile = tiles_ref[me]
    held = jnp.maximum(tile, 0)
    across = [partner(me, link, nx, ny) for link in range(4)]
    for link in range(4):
        other = tiles_ref[across[link]]
        side = jnp.int32(-1)
        for k in range(4):
            side = jnp.where((tile >= 0) & (other >= 0) & (near_ref[k, held] == other), k, side)
        linked = side >= 0
        facing = (side + 2 + turn_ref[jnp.maximum(side, 0), held]) % 4
        there = jnp.maximum(other, 0)
        for end in range(2):
            later = (side < 2) == (end == 0)
            lateral = jnp.where(later, facing + 1, facing + 3) % 4
            beyond = jnp.where(linked, near_ref[lateral, there], -1)
            back = (lateral + 2 + turn_ref[lateral, there]) % 4
            corner = jnp.where(later, back + 1, back) % 4
            if link in (1, 3):
                found = [tiles_ref[partner(across[u], link, nx, ny)] for u in (0, 2)]
                which = jnp.where(beyond == found[0], 1, jnp.where(beyond == found[1], 2, 0))
                lane = corner + RELAY_AT[link]
            else:
                found = [tiles_ref[partner(across[link], v, nx, ny)] for v in (1, 3)]
                which = jnp.where((beyond == found[0]) | (beyond == found[1]), 1 + link // 2, 0)
                lane = corner + jnp.where(beyond == found[0], RELAY_AT[1], RELAY_AT[3])
            for i, value in ((0, jnp.where(beyond >= 0, which, 0)), (1, lane)):
                at = 2 * (2 * link + end) + i
                plan_ref[at:at + 1, :] = jnp.full((1, LANES), value, jnp.int32)


def relay_kernel(pay0, pay2, came1, came3, out0, out2):
    lane = lanes()
    for pay, out in ((pay0, out0), (pay2, out2)):
        line = pay[0:8, :]
        for link, came in ((1, came1), (3, came3)):
            moved = pltpu.roll(came[0:8, :], RELAY_AT[link] - OWN_AT, 1)
            line = jnp.where((lane >= RELAY_AT[link]) & (lane < RELAY_AT[link] + 4), moved, line)
        out[0:8, :] = line
        out[8:16, :] = pay[8:16, :]


def edge_patches(lines, rims):
    patch = []
    for side in range(4):
        drift = repeated(lines[side], 0 if side % 2 == 1 else 2)
        sign = 1.0 if side in (1, 2) else -1.0
        patch.append(wet_rows(lines[side]) * (DIFFUSE - (sign * 0.5 * ADVECT) * drift) * rims[side])
    return patch


def with_ends(patch):
    south, east, north, west = patch
    end = TILE - 1
    return [
        south + at_ends(west, 0, 0) + at_ends(east, 0, end),
        east + at_ends(south, end, 0) + at_ends(north, end, end),
        north + at_ends(west, end, 0) + at_ends(east, end, end),
        west + at_ends(south, 0, 0) + at_ends(north, 0, end),
    ]


def final_kernel(route_ref, plan_ref, lines_ref, inner_ref, almost_ref, came1, came3, came0, came2, out_ref, full, sems):
    lane, row = lanes(), rows()
    route, plan = Rows(route_ref), Rows(plan_ref)
    came = [came0, came1, came2, came3]
    outer = []
    for link in range(4):
        line = came[link][0:8, :]
        for end, lane_to in ((0, LANES - 1), (1, TILE)):
            which, lane_from = plan[2 * (2 * link + end)], plan[2 * (2 * link + end) + 1]
            held = came[link][0:8, :]
            if link in (1, 3):
                held = jnp.where(which == 2, came2[0:8, :], came0[0:8, :])
            value = pick(held, lane_from)
            line = jnp.where(lane == lane_to, jnp.where(which > 0, value, 0.0), line)
        outer.append(line)
    rims = rims_of(route, None, outer)
    beyond = rims_of(route, None, [came[link][8:16, :] for link in range(4)])
    lines, inner = four_of(lines_ref), four_of(inner_ref)
    patch = edge_patches(lines, rims)
    whole = with_ends(patch)
    on_edge, inside = [], []
    for side in range(4):
        sign = 1.0 if side in (1, 2) else -1.0
        line, wet, wet_in = rims[side], wet_rows(lines[side]), wet_rows(inner[side])
        after, before = pltpu.roll(line, LANES - 1, 1), pltpu.roll(line, 1, 1)
        first, second = pltpu.roll(line, 4, 0), pltpu.roll(line, 2, 0)
        normal, tangent = (first, second) if side % 2 == 1 else (second, first)
        along = normal * (sign * (beyond[side] - lines[side])) + tangent * (after - before)
        round_sum = after + before + beyond[side] + lines[side] - 4.0 * line
        tracer = wet_rows(line) * (line - (0.5 * ADVECT) * along + DIFFUSE * round_sum)
        far = pressure_of(tracer, row)
        mine = jnp.where(lane < TILE, pressure_of(whole[side], row), 0.0)
        drop = pltpu.roll(mine, LANES - 1, 1) - pltpu.roll(mine, 1, 1)
        to_normal, to_tangent = (4, 6) if side % 2 == 1 else (6, 4)
        own_row = row < 2 if side % 2 == 1 else (row >= 2) & (row < 4)
        cross_row = (row >= 2) & (row < 4) if side % 2 == 1 else row < 2
        push = jnp.where(own_row, sign * pltpu.roll(far, to_normal, 0), 0.0)
        push = jnp.where(cross_row, pltpu.roll(drop, to_tangent, 0), push)
        on_edge.append(patch[side] - (0.5 * STEP_SIZE) * wet * push)
        kept = own_row & (lane > 0) & (lane < TILE - 1)
        inside.append(jnp.where(kept, (-sign * 0.5 * STEP_SIZE) * wet_in * pltpu.roll(mine, to_normal, 0), 0.0))
    edges, seconds = spread_chunks(on_edge, 0), spread_chunks(inside, 1)
    copies = []
    for low, high in ((0, 24), (24, CHUNKS)):
        for c in range(low, high):
            cut = slice(c * LANES, min((c + 1) * LANES, CELLS))
            width = cut.stop - cut.start
            full[:, cut] = (almost_ref[:, c * LANES:(c + 1) * LANES] + (edges[c] + seconds[c]))[:, :width]
        cells = pl.ds(low * LANES, min(high * LANES, CELLS) - low * LANES)
        for c in range(6):
            copies.append(pltpu.make_async_copy(full.at[c, cells], out_ref.at[c, 0, cells], sems.at[len(copies)]))
            copies[-1].start()
    for copy in copies:
        copy.wait()


def write_out(full, out_ref, sems):
    copies = [pltpu.make_async_copy(full.at[c], out_ref.at[c, 0], sems.at[c]) for c in range(6)]
    for copy in copies:
        copy.start()
    for copy in copies:
        copy.wait()


def at_ends(line, lane_from, lane_to):
    value = jnp.broadcast_to(line[:, lane_from:lane_from + 1], (8, LANES))
    return jnp.where(lanes() == lane_to, value, 0.0)


def edge_kernel(route_ref, lines_ref, base_lines_ref, came0, came1, came2, came3,
                patch_ref, own_two_ref, pay0, pay1, pay2, pay3):
    route = Rows(route_ref)
    lines, base = four_of(lines_ref), four_of(base_lines_ref)
    own = own_rims([sent_line(lines[side], side, route, True) for side in range(4)], route)
    rims = rims_of(route, own, [came[0:8, :] for came in by_link((came0, came1, came2, came3), BOTH)])
    patch = edge_patches(lines, rims)
    whole = with_ends(patch)
    press = []
    for side in range(4):
        patch_ref[8 * side:8 * side + 8, :] = patch[side]
        press.append(sent_line(pressure_of(base[side] + whole[side], rows()), side, route, False))
    for link, pay in zip(SECOND_ORDER, (pay0, pay1, pay2, pay3)):
        pay[...] = chosen(press, route, link)
    own = own_rims(press, route)
    for side in range(4):
        own_two_ref[8 * side:8 * side + 8, :] = own[side]


def middle_kernel(route_ref, state_ref, base_ref, patch_ref, out_ref):
    state = state_ref[...]
    cell, column = column_of()
    base = base_ref[...] + spread(four_of(patch_ref), cell, column)
    row = lax.broadcasted_iota(jnp.int32, (8, WIDE), 0)
    out_ref[...] = if_live(route_ref, base + force_of(state, base, row))


def last_kernel(route_ref, lines_ref, own_ref, almost_ref, came0, came1, came2, came3, out_ref, full, sems):
    route = Rows(route_ref)
    rims = rims_of(route, four_of(own_ref), [came[...] for came in by_link((came0, came1, came2, came3), SECOND_ORDER)])
    patch = []
    for side in range(4):
        wet = wet_rows(lines_ref[8 * side:8 * side + 8, :])
        row = rows()
        rim = pltpu.roll(rims[side], 4 if side % 2 == 1 else 6, 0)
        mine = row < 2 if side % 2 == 1 else (row >= 2) & (row < 4)
        sign = -1.0 if side in (1, 2) else 1.0
        patch.append(jnp.where(mine, (sign * 0.5 * STEP_SIZE) * wet * rim, 0.0))
    cell, column = column_of()
    full[...] = (almost_ref[...] + spread(patch, cell, column))[:, :CELLS]
    write_out(full, out_ref, sems)


def sds(*shape, dtype=jnp.float32):
    return jax.ShapeDtypeStruct(shape, dtype)


PARAMS = pltpu.CompilerParams(vmem_limit_bytes=16 * 1024 * 1024)


def on_device(nx, ny, fields, wet_mask, tile_of_slot, neighbor, rotation):
    line, pair, four, wide = sds(8, LANES), sds(16, LANES), sds(32, LANES), sds(8, WIDE)
    table = pltpu.SMEM((4, nx * ny), jnp.int32)
    tables = [pltpu.with_memory_space_constraint(v, pltpu.HBM) for v in (tile_of_slot, neighbor.T, rotation.T)]
    inputs = [pltpu.with_memory_space_constraint(v, pltpu.HBM) for v in (fields.reshape(6, 1, CELLS), wet_mask)]
    raw, wet_raw, lines, inner, *pays, route = pl.pallas_call(
        lambda *refs: load_kernel((nx, ny), *refs),
        out_shape=[sds(8, CELLS), sds(8, CELLS, dtype=jnp.int32), four, four, pair, pair, pair, pair,
                   sds(ROUTE, LANES, dtype=jnp.int32)],
        in_specs=[HBM] * 5,
        out_specs=[VMEM] * 9,
        scratch_shapes=[pltpu.SMEM((nx * ny,), jnp.int32), table, table, pltpu.SemaphoreType.DMA((10,))],
        compiler_params=PARAMS, name="load",
    )(*tables, *inputs)
    came_x = exchanged(pays[:2], X_ORDER, nx, ny)
    halves = pltpu.with_memory_space_constraint(tile_of_slot.reshape(2, LANES), pltpu.HBM)
    flag = pl.pallas_call(
        lambda *refs: check_kernel((nx, ny), *refs),
        out_shape=sds(1, dtype=jnp.int32), in_specs=[HBM] * 2, out_specs=SMEM,
        scratch_shapes=[pltpu.VMEM((2, LANES), jnp.int32), pltpu.VMEM((8, nx * ny), jnp.int32),
                        pltpu.SemaphoreType.DMA((2,))],
        compiler_params=PARAMS, name="check",
        cost_estimate=pl.CostEstimate(flops=1000000, bytes_accessed=600000, transcendentals=0),
    )(halves, tables[1])

    result = pltpu.HBM((6, 1, CELLS), jnp.float32)
    writing = [pltpu.VMEM((8, CELLS), jnp.float32), pltpu.SemaphoreType.DMA((12,))]

    def grid_like():
        sent = pl.pallas_call(
            relay_kernel, out_shape=[pair, pair], in_specs=[VMEM] * 4, out_specs=[VMEM] * 2,
            compiler_params=PARAMS, name="relay",
        )(*by_link(pays[2:], U_ORDER, (0, 2)), *by_link(came_x, X_ORDER, (1, 3)))
        came_u = exchanged([sent[(0, 2).index(link)] for link in U_ORDER], U_ORDER, nx, ny)
        plan, almost = pl.pallas_call(
            lambda *refs: plan_kernel((nx, ny), *refs),
            out_shape=[sds(16, LANES, dtype=jnp.int32), wide], in_specs=[HBM] * 3 + [VMEM] * 3, out_specs=[VMEM] * 2,
            scratch_shapes=[pltpu.VMEM((8, WIDE), jnp.float32), pltpu.SMEM((nx * ny,), jnp.int32), table, table,
                            pltpu.SemaphoreType.DMA((3,))],
            compiler_params=PARAMS, name="plan",
            cost_estimate=pl.CostEstimate(flops=2000000, bytes_accessed=800000, transcendentals=0),
        )(*tables, raw, wet_raw, route)
        return pl.pallas_call(
            final_kernel, out_shape=result, in_specs=[VMEM] * 9, out_specs=HBM,
            scratch_shapes=writing, compiler_params=PARAMS, name="final",
        )(route, plan, lines, inner, almost, *by_link(came_x, X_ORDER, (1, 3)), *by_link(came_u, U_ORDER, (0, 2)))

    def general():
        came = came_x + exchanged(pays[2:], U_ORDER, nx, ny)
        state, base, base_lines = pl.pallas_call(
            base_kernel, out_shape=[wide, wide, four], in_specs=[VMEM] * 2, out_specs=[VMEM] * 3,
            compiler_params=PARAMS, name="base",
            cost_estimate=pl.CostEstimate(flops=2000000, bytes_accessed=800000, transcendentals=0),
        )(raw, wet_raw)
        patch, own_two, *press = pl.pallas_call(
            edge_kernel, out_shape=[four, four, line, line, line, line],
            in_specs=[VMEM] * 7, out_specs=[VMEM] * 6,
            compiler_params=PARAMS, name="edge",
        )(route, lines, base_lines, *came)
        came_two = exchanged(press, SECOND_ORDER, nx, ny)
        nearly = pl.pallas_call(
            middle_kernel, out_shape=wide, in_specs=[VMEM] * 4, out_specs=VMEM,
            compiler_params=PARAMS, name="middle",
            cost_estimate=pl.CostEstimate(flops=2000000, bytes_accessed=800000, transcendentals=0),
        )(route, state, base, patch)
        return pl.pallas_call(
            last_kernel, out_shape=result, in_specs=[VMEM] * 8, out_specs=HBM,
            scratch_shapes=writing, compiler_params=PARAMS, name="last",
        )(route, lines, own_two, nearly, *came_two)

    out = lax.cond(flag[0] == 0, grid_like, general)
    return out.reshape(1, 6, CELLS)


def solution(mesh):
    nx, ny = mesh.shape["gx"], mesh.shape["gy"]
    in_specs = (P(AXES, None, None), P(AXES, None), P(), P(), P())
    return jax.shard_map(lambda *args: on_device(nx, ny, *args), mesh=mesh, in_specs=in_specs,
                         out_specs=P(AXES, None, None), check_vma=False)
```

```python
import jax
import jax.numpy as jnp
from jax import lax
from jax.experimental import pallas as pl
from jax.experimental.pallas import tpu as pltpu
from jax.sharding import PartitionSpec as P

TILE = 90
CELLS = TILE * TILE
LANES = 128
CHUNKS = 64
WIDE = LANES * CHUNKS
HALF = 45
LAST = CELLS - TILE - (CHUNKS - 2) * LANES

ADVECT = 0.25
DIFFUSE = 0.15
STEP_SIZE = 0.5
CORIOLIS = 0.3
GRAVITY = 0.8

AXES = ("gx", "gy")
VMEM = pl.BlockSpec(memory_space=pltpu.VMEM)
SMEM = pl.BlockSpec(memory_space=pltpu.SMEM)
ANY = pl.BlockSpec(memory_space=pl.ANY)
HBM = pl.BlockSpec(memory_space=pltpu.HBM)


def link_x_even(x, y, nx, ny):
    return x ^ 1, y


def link_x_odd(x, y, nx, ny):
    return (((x + nx - 1) % nx ^ 1) + 1) % nx, y


def link_y_even(x, y, nx, ny):
    return x, y ^ 1


def link_y_odd(x, y, nx, ny):
    if y == 0 or y == ny - 1:
        return (x + nx // 2) % nx, y
    return x, ((y - 1) ^ 1) + 1


LINKS = (link_y_odd, link_x_even, link_y_even, link_x_odd)


def pairs_of(link, nx, ny):
    out = []
    for x in range(nx):
        for y in range(ny):
            to_x, to_y = link(x, y, nx, ny)
            out.append((x * ny + y, to_x * ny + to_y))
    return out


X_ORDER = (3, 1)
U_ORDER = (2, 0)
BOTH = X_ORDER + U_ORDER
SECOND_ORDER = (2, 0, 3, 1)


def exchanged(pays, order, nx, ny):
    return [lax.ppermute(pay, AXES, pairs_of(LINKS[link], nx, ny)) for pay, link in zip(pays, order)]


def by_link(refs, order, links=(0, 1, 2, 3)):
    return [refs[order.index(link)] for link in links]


def partner(me, which, nx, ny):
    x, y = me // ny, me % ny
    if which == 0:
        pole = (y == 0) | (y == ny - 1)
        step = jnp.where(y % 2 == 1, 1, -1)
        return jnp.where(pole, (x + nx // 2) % nx * ny + y, me + step)
    if which == 1:
        return me + jnp.where(x % 2 == 0, ny, -ny)
    if which == 2:
        return me + jnp.where(y % 2 == 0, 1, -1)
    return (x + jnp.where(x % 2 == 1, 1, nx - 1)) % nx * ny + y


def lanes():
    return lax.broadcasted_iota(jnp.int32, (8, LANES), 1)


def rows():
    return lax.broadcasted_iota(jnp.int32, (8, LANES), 0)


def pick(values, index):
    return jnp.take_along_axis(values, index, axis=1)


def tiled(values, count):
    return jnp.concatenate([values] * count, axis=1)


def column_of():
    cell = lax.broadcasted_iota(jnp.int32, (8, WIDE), 1)
    line = jnp.floor((cell.astype(jnp.float32) + 0.5) * (1.0 / TILE)).astype(jnp.int32)
    return cell, cell - TILE * line


def edge_lines(state, column):
    lane = lanes()
    edge = (column == 0) | (column == TILE - 1)
    parts = []
    for low, high in ((0, HALF), (HALF, CHUNKS)):
        found = jnp.zeros((8, LANES), jnp.float32)
        for c in range(low, high):
            cut = slice(c * LANES, (c + 1) * LANES)
            found = jnp.where(edge[:, cut], state[:, cut], found)
        parts.append(found)
    east_at = (TILE * lane + TILE - 1) & (LANES - 1)
    west_at = (TILE * lane) & (LANES - 1)
    east = jnp.where(lane < 64, pick(parts[0], east_at), pick(parts[1], east_at))
    west = jnp.where(lane < 64, pick(parts[0], west_at), pick(parts[1], west_at))
    south = state[:, :LANES]
    before = pltpu.roll(state[:, (CHUNKS - 2) * LANES:(CHUNKS - 1) * LANES], LANES - LAST, 1)
    after = pltpu.roll(state[:, (CHUNKS - 1) * LANES:], LANES - LAST, 1)
    north = jnp.where(lane < LANES - LAST, before, after)
    return [south, east, north, west]


def spread(lines, cell, column):
    south, east, north, west = lines
    lane = lanes()
    odd = (lane & 1) == 1
    line_at = (37 * ((lane + jnp.where(odd, 39, 0)) >> 1)) & 63
    early = jnp.where(odd, pick(east, line_at), pick(west, line_at))
    late = jnp.where(odd, pick(east, line_at + 64), pick(west, line_at + 64))
    sides = jnp.concatenate([early] * HALF + [late] * (CHUNKS - HALF), axis=1)
    edge = (column == 0) | (column == TILE - 1)
    out = jnp.where(edge, sides, 0.0)
    first = jnp.where(lane < TILE, south, 0.0) + out[:, :LANES]
    moved = pltpu.roll(north, LAST, 1)
    before = out[:, (CHUNKS - 2) * LANES:(CHUNKS - 1) * LANES] + jnp.where(lane >= LAST, moved, 0.0)
    after = out[:, (CHUNKS - 1) * LANES:] + jnp.where(lane < LAST + TILE - LANES, moved, 0.0)
    return jnp.concatenate([first, out[:, LANES:(CHUNKS - 2) * LANES], before, after], axis=1)


def neighbours(state):
    cell, column = column_of()
    right = jnp.where(column == TILE - 1, 0.0, pltpu.roll(state, WIDE - 1, 1))
    left = jnp.where(column == 0, 0.0, pltpu.roll(state, 1, 1))
    up = jnp.where(cell >= CELLS - TILE, 0.0, pltpu.roll(state, WIDE - TILE, 1))
    down = jnp.where(cell < TILE, 0.0, pltpu.roll(state, TILE, 1))
    return right, left, up, down, cell, column


def row_of(values):
    return lax.broadcasted_iota(jnp.int32, values.shape, 0)


def repeated(values, first):
    row = row_of(values)
    if first == 0:
        pair = jnp.where(row < 2, values, pltpu.roll(values, 2, 0))
    else:
        pair = jnp.where(row < 4, values, pltpu.roll(values, 2, 0))
        pair = jnp.where(row < 2, pltpu.roll(values, 6, 0), pair)
        return pair
    return jnp.where(row < 4, pair, pltpu.roll(values, 4, 0))


def wet_rows(values):
    return jnp.broadcast_to(values[6:7], values.shape)


def turned(line, turns):
    row = row_of(line)
    swapped = jnp.where(row < 2, pltpu.roll(line, 6, 0), pltpu.roll(line, 2, 0))
    velocity = row < 4
    second = jnp.where(row < 2, swapped, -swapped)
    odd = jnp.where(turns % 2 == 1, 1, 0)
    out = jnp.where(jnp.logical_and(velocity, odd == 1), second, line)
    back = jnp.where(turns >= 2, 1, 0)
    return jnp.where(jnp.logical_and(velocity, back == 1), -out, out)


def flipped(line):
    return pick(line, jnp.maximum(TILE - 1 - lanes(), 0))


ROUTE = 48
OWN_AT, RELAY_AT = TILE, {1: TILE + 4, 3: TILE + 8}


class Rows:
    def __init__(self, ref):
        self.ref = ref

    def __getitem__(self, i):
        return jnp.broadcast_to(self.ref[i:i + 1, :], (8, LANES))


def my_index(ny):
    return lax.axis_index("gx") * ny + lax.axis_index("gy")


def sent_line(line, side, route, vector):
    line = jnp.where(route[32 + side] == 1, flipped(line), line)
    return turned(line, route[36 + side]) if vector else line


def chosen(lines, route, link):
    total = jnp.zeros((8, LANES), jnp.float32)
    for side in range(4):
        total = jnp.where(route[4 * link + side] == 1, lines[side], total)
    return total


def own_rims(sent, route):
    out = []
    for target in range(4):
        total = jnp.zeros((8, LANES), jnp.float32)
        for side in range(4):
            total = jnp.where(route[16 + 4 * side + target] == 1, sent[side], total)
        out.append(total)
    return out


def rims_of(route, base, came):
    out = []
    for side in range(4):
        rim = base[side] if base is not None else jnp.zeros((8, LANES), jnp.float32)
        for link in range(4):
            rim = jnp.where(route[4 * link + side] == 1, came[link], rim)
        out.append(rim)
    return out


def four_of(ref):
    return [ref[8 * side:8 * side + 8, :] for side in range(4)]


def columns_at(step):
    lane = lanes()
    odd = lane & 1
    shift = jnp.where(odd == 1, 39 + step, -step) if step % 2 == 0 else jnp.where(odd == 1, -step, 39 + step)
    column = jnp.where(odd == 1, TILE - 1 - step, step) if step % 2 == 0 else jnp.where(odd == 1, step, TILE - 1 - step)
    line_at = (37 * ((lane + shift) >> 1)) & 63
    return line_at, (TILE * line_at + column) >> 7


def raw_lines(chunk_of, step):
    lane = lanes()
    _, home = columns_at(step)
    parts = []
    for low, high in ((0, HALF), (HALF, CHUNKS)):
        found = chunk_of(low)
        for c in range(low + 1, high):
            found = jnp.where(home == c - low, chunk_of(c), found)
        parts.append(found)
    early = lane < 64
    out = [None] * 4
    for side, column in ((1, TILE - 1 - step), (3, step)):
        at = (TILE * lane + column) & (LANES - 1)
        out[side] = jnp.where(early, pick(parts[0], at), pick(parts[1], at))
    for side, first in ((0, TILE * step), (2, CELLS - TILE - TILE * step)):
        low, start = first // LANES, first % LANES
        if start == 0:
            out[side] = chunk_of(low)
        else:
            before = pltpu.roll(chunk_of(low), LANES - start, 1)
            after = pltpu.roll(chunk_of(low + 1), LANES - start, 1)
            out[side] = jnp.where(lane < LANES - start, before, after)
    return out


def spread_chunks(lines, step):
    lane = lanes()
    line_at, home = columns_at(step)
    odd = (lane & 1) == 1
    first_odd, first_even = (lines[1], lines[3]) if step % 2 == 0 else (lines[3], lines[1])
    early = jnp.where(odd, pick(first_odd, line_at), pick(first_even, line_at))
    late = jnp.where(odd, pick(first_odd, line_at + 64), pick(first_even, line_at + 64))
    out = []
    for c in range(CHUNKS):
        out.append(jnp.where(home == (c if c < HALF else c - HALF), early if c < HALF else late, 0.0))
    for side, first in ((0, TILE * step), (2, CELLS - TILE - TILE * step)):
        low, start = first // LANES, first % LANES
        line = jnp.where(lane < TILE, lines[side], 0.0)
        if start == 0:
            out[low] = out[low] + line
        else:
            moved = pltpu.roll(line, start, 1)
            out[low] = out[low] + jnp.where(lane >= start, moved, 0.0)
            if start + TILE > LANES:
                out[low + 1] = out[low + 1] + jnp.where(lane < start + TILE - LANES, moved, 0.0)
    return out


def load_kernel(shape, tiles_hbm, halves_hbm, near_hbm, turn_hbm, fields_ref, wet_ref,
                raw, wet_raw, lines_ref, inner_ref, pay0, pay1, pay2, pay3, route_ref, halves_ref, table_ref,
                tiles_ref, near_ref, turn_ref, sems):
    nx, ny = shape
    tables = [pltpu.make_async_copy(tiles_hbm, tiles_ref, sems.at[7]),
              pltpu.make_async_copy(near_hbm, near_ref, sems.at[8]),
              pltpu.make_async_copy(turn_hbm, turn_ref, sems.at[9])]
    copies = [pltpu.make_async_copy(fields_ref.at[c, 0], raw.at[c], sems.at[c]) for c in range(6)]
    copies.append(pltpu.make_async_copy(wet_ref.at[0], wet_raw.at[0], sems.at[6]))
    copies.append(pltpu.make_async_copy(halves_hbm, halves_ref, sems.at[10]))
    copies.append(pltpu.make_async_copy(near_hbm, table_ref.at[0:4], sems.at[11]))
    for copy in tables + copies:
        copy.start()
    for copy in tables:
        copy.wait()
    me = my_index(ny)
    route = [None] * ROUTE
    tile = tiles_ref[me]
    live = tile >= 0
    held = jnp.maximum(tile, 0)
    near = [jnp.where(live, near_ref[side, held], -1) for side in range(4)]
    turn = [turn_ref[side, held] for side in range(4)]
    for link in range(4):
        other = tiles_ref[partner(me, link, nx, ny)]
        for side in range(4):
            route[4 * link + side] = jnp.where((near[side] >= 0) & (near[side] == other), 1, 0)
    for side in range(4):
        target = (side + 2 + turn[side]) % 4
        for k in range(4):
            route[16 + 4 * side + k] = jnp.where((near[side] >= 0) & (near[side] == tile) & (target == k), 1, 0)
        route[32 + side] = jnp.where((target < 2) != (side >= 2), 1, 0)
        route[36 + side] = (4 - turn[side]) % 4
    route[40] = jnp.where(live, 1, 0)
    for i in range(41):
        route_ref[i:i + 1, :] = jnp.full((1, LANES), route[i], jnp.int32)
    for copy in copies:
        copy.wait()

    def chunk(ref, c):
        if c < CHUNKS - 1:
            return ref[:, c * LANES:(c + 1) * LANES]
        rest = CELLS - c * LANES
        part = ref[:, c * LANES:CELLS]
        return jnp.concatenate([part, jnp.zeros((8, LANES - rest), part.dtype)], axis=1)

    row, lane = rows(), lanes()
    both = []
    for step, ref in ((0, lines_ref), (1, inner_ref)):
        lines = []
        for value, wet in zip(raw_lines(lambda c: chunk(raw, c), step), raw_lines(lambda c: chunk(wet_raw, c), step)):
            wet = jnp.broadcast_to(wet[0:1], (8, LANES)).astype(jnp.float32)
            lines.append(jnp.where(row < 6, value * wet, jnp.where(row == 6, wet, 0.0)))
        for side in range(4):
            ref[8 * side:8 * side + 8, :] = lines[side]
        both.append(lines)
    ends = [jnp.where((lane == OWN_AT + 1) | (lane == OWN_AT + 2), TILE - 1, 0)] * 2
    corners = jnp.where(lane < OWN_AT + 2, pick(both[0][0], ends[0]), pick(both[0][2], ends[1]))
    at_corners = (lane >= OWN_AT) & (lane < OWN_AT + 4)
    sent = [sent_line(both[0][side], side, route, True) for side in range(4)]
    sent_inner = [sent_line(both[1][side], side, route, False) for side in range(4)]
    for link, pay in zip(BOTH, (pay0, pay1, pay2, pay3)):
        pay[0:8, :] = jnp.where(at_corners, corners, chosen(sent, route, link))
        pay[8:16, :] = chosen(sent_inner, route, link)


def pressure_of(tracer, row):
    return GRAVITY * jnp.where(row == 5, tracer + pltpu.roll(tracer, 1, 0), tracer)


def force_of(state, base, row):
    right, left, up, down, cell, column = neighbours(pressure_of(base, row))
    slope = jnp.where(row < 2, pltpu.roll(right - left, 4, 0), pltpu.roll(up - down, 6, 0))
    swapped = jnp.where(row < 2, pltpu.roll(state, 6, 0), -pltpu.roll(state, 2, 0))
    force = STEP_SIZE * (CORIOLIS * swapped - 0.5 * slope)
    return jnp.where(row < 4, wet_rows(state) * force, 0.0)


def masked_state(raw, wet_raw, state_ref):
    state_ref[:, (CHUNKS - 1) * LANES:] = jnp.zeros((8, LANES), jnp.float32)
    for low, high in ((0, (CHUNKS - 1) * LANES), ((CHUNKS - 1) * LANES, CELLS)):
        size = (8, high - low)
        row = lax.broadcasted_iota(jnp.int32, size, 0)
        wet = jnp.broadcast_to(wet_raw[0:1, low:high].astype(jnp.float32), size)
        state_ref[:, low:high] = jnp.where(row < 6, raw[:, low:high] * wet, jnp.where(row == 6, wet, 0.0))
    return state_ref[...]


def without_rims(state):
    right, left, up, down, cell, column = neighbours(state)
    first, second, wet = repeated(state, 0), repeated(state, 2), wet_rows(state)
    along = first * (right - left) + second * (up - down)
    round_sum = right + left + up + down - 4.0 * state
    return wet * (state - (0.5 * ADVECT) * along + DIFFUSE * round_sum), column


def if_live(route_ref, values):
    return jnp.where(tiled(Rows(route_ref)[40], CHUNKS) == 1, values, 0.0)


def base_kernel(raw, wet_raw, state_ref, base_ref, base_lines_ref):
    state = masked_state(raw, wet_raw, state_ref)
    base, column = without_rims(state)
    base_ref[...] = base
    lines = edge_lines(base, column)
    for side in range(4):
        base_lines_ref[8 * side:8 * side + 8, :] = lines[side]


def inner_kernel(shape, tiles_hbm, near_hbm, turn_hbm, raw, wet_raw, route_ref, almost_ref, plan_ref,
                 state_ref, tiles_ref, near_ref, turn_ref, sems):
    copies = [pltpu.make_async_copy(tiles_hbm, tiles_ref, sems.at[0]),
              pltpu.make_async_copy(near_hbm, near_ref, sems.at[1]),
              pltpu.make_async_copy(turn_hbm, turn_ref, sems.at[2])]
    for copy in copies:
        copy.start()
    state = masked_state(raw, wet_raw, state_ref)
    base, _ = without_rims(state)
    almost_ref[...] = base
    for copy in copies:
        copy.wait()
    corner_plan(shape, tiles_ref, near_ref, turn_ref, plan_ref)
    base = almost_ref[...]
    row = lax.broadcasted_iota(jnp.int32, (8, WIDE), 0)
    almost_ref[...] = if_live(route_ref, base + force_of(state, base, row))


def check_kernel(shape, halves_ref, table_ref, after, flag):
    nx, ny = shape
    row, lane = rows(), lanes()
    tiles = [jnp.broadcast_to(halves_ref[half:half + 1, :], (8, LANES)) for half in range(2)]
    near = [table_ref[:, half * LANES:(half + 1) * LANES] for half in range(2)]

    def look(table, index):
        return jnp.where(index < LANES, pick(table[0], index & (LANES - 1)), pick(table[1], index & (LANES - 1)))

    worst = jnp.zeros((8, LANES), jnp.int32)
    for half in range(2):
        tile = tiles[half]
        mine = look(near, jnp.maximum(tile, 0))
        linked = (tile >= 0) & (mine >= 0) & (row < 4)
        other = [look(tiles, partner(lane + half * LANES, link, nx, ny)) for link in range(4)]
        over_x = (mine == other[1]) | (mine == other[3])
        kind = jnp.where(linked, jnp.where(mine == tile, 4, jnp.where(over_x, 1, 2)), 0)
        after = jnp.where(row < 3, pltpu.roll(kind, 7, 0), pltpu.roll(kind, 3, 0))
        odd = (kind == 4) | ((kind > 0) & (kind == after) & (row < 4))
        worst = jnp.where(odd, 1, worst)
    flag[0] = jnp.max(worst)


def corner_plan(shape, tiles_ref, near_ref, turn_ref, plan_ref):
    nx, ny = shape
    me = my_index(ny)
    tile = tiles_ref[me]
    held = jnp.maximum(tile, 0)
    across = [partner(me, link, nx, ny) for link in range(4)]
    for link in range(4):
        other = tiles_ref[across[link]]
        side = jnp.int32(-1)
        for k in range(4):
            side = jnp.where((tile >= 0) & (other >= 0) & (near_ref[k, held] == other), k, side)
        linked = side >= 0
        facing = (side + 2 + turn_ref[jnp.maximum(side, 0), held]) % 4
        there = jnp.maximum(other, 0)
        for end in range(2):
            later = (side < 2) == (end == 0)
            lateral = jnp.where(later, facing + 1, facing + 3) % 4
            beyond = jnp.where(linked, near_ref[lateral, there], -1)
            back = (lateral + 2 + turn_ref[lateral, there]) % 4
            corner = jnp.where(later, back + 1, back) % 4
            if link in (1, 3):
                found = [tiles_ref[partner(across[u], link, nx, ny)] for u in (0, 2)]
                which = jnp.where(beyond == found[0], 1, jnp.where(beyond == found[1], 2, 0))
                lane = corner + RELAY_AT[link]
            else:
                found = [tiles_ref[partner(across[link], v, nx, ny)] for v in (1, 3)]
                which = jnp.where((beyond == found[0]) | (beyond == found[1]), 1 + link // 2, 0)
                lane = corner + jnp.where(beyond == found[0], RELAY_AT[1], RELAY_AT[3])
            for i, value in ((0, jnp.where(beyond >= 0, which, 0)), (1, lane)):
                at = 2 * (2 * link + end) + i
                plan_ref[at:at + 1, :] = jnp.full((1, LANES), value, jnp.int32)


def relay_kernel(pay0, pay1, came0, came1, after, out0, out1):
    lane = lanes()
    for pay, out in ((pay0, out0), (pay1, out1)):
        line = pay[0:8, :]
        for link, came in zip(X_ORDER, (came0, came1)):
            moved = pltpu.roll(came[0:8, :], RELAY_AT[link] - OWN_AT, 1)
            line = jnp.where((lane >= RELAY_AT[link]) & (lane < RELAY_AT[link] + 4), moved, line)
        out[0:8, :] = line
        out[8:16, :] = pay[8:16, :]


def edge_patches(lines, rims):
    patch = []
    for side in range(4):
        drift = repeated(lines[side], 0 if side % 2 == 1 else 2)
        sign = 1.0 if side in (1, 2) else -1.0
        patch.append(wet_rows(lines[side]) * (DIFFUSE - (sign * 0.5 * ADVECT) * drift) * rims[side])
    return patch


def with_ends(patch):
    south, east, north, west = patch
    end = TILE - 1
    return [
        south + at_ends(west, 0, 0) + at_ends(east, 0, end),
        east + at_ends(south, end, 0) + at_ends(north, end, end),
        north + at_ends(west, end, 0) + at_ends(east, end, end),
        west + at_ends(south, 0, 0) + at_ends(north, 0, end),
    ]


def final_kernel(route_ref, plan_ref, lines_ref, inner_ref, almost_ref, first, second, third, fourth, out_ref, full, sems):
    lane, row = lanes(), rows()
    route, plan = Rows(route_ref), Rows(plan_ref)
    came = by_link((first, second, third, fourth), BOTH)
    outer = []
    for link in range(4):
        line = came[link][0:8, :]
        for end, lane_to in ((0, LANES - 1), (1, TILE)):
            which, lane_from = plan[2 * (2 * link + end)], plan[2 * (2 * link + end) + 1]
            held = came[link][0:8, :]
            if link in (1, 3):
                held = jnp.where(which == 2, came[2][0:8, :], came[0][0:8, :])
            value = pick(held, lane_from)
            line = jnp.where(lane == lane_to, jnp.where(which > 0, value, 0.0), line)
        outer.append(line)
    rims = rims_of(route, None, outer)
    beyond = rims_of(route, None, [came[link][8:16, :] for link in range(4)])
    lines, inner = four_of(lines_ref), four_of(inner_ref)
    patch = edge_patches(lines, rims)
    whole = with_ends(patch)
    on_edge, inside = [], []
    for side in range(4):
        sign = 1.0 if side in (1, 2) else -1.0
        line, wet, wet_in = rims[side], wet_rows(lines[side]), wet_rows(inner[side])
        after, before = pltpu.roll(line, LANES - 1, 1), pltpu.roll(line, 1, 1)
        first, second = pltpu.roll(line, 4, 0), pltpu.roll(line, 2, 0)
        normal, tangent = (first, second) if side % 2 == 1 else (second, first)
        along = normal * (sign * (beyond[side] - lines[side])) + tangent * (after - before)
        round_sum = after + before + beyond[side] + lines[side] - 4.0 * line
        tracer = wet_rows(line) * (line - (0.5 * ADVECT) * along + DIFFUSE * round_sum)
        far = pressure_of(tracer, row)
        mine = jnp.where(lane < TILE, pressure_of(whole[side], row), 0.0)
        drop = pltpu.roll(mine, LANES - 1, 1) - pltpu.roll(mine, 1, 1)
        to_normal, to_tangent = (4, 6) if side % 2 == 1 else (6, 4)
        own_row = row < 2 if side % 2 == 1 else (row >= 2) & (row < 4)
        cross_row = (row >= 2) & (row < 4) if side % 2 == 1 else row < 2
        push = jnp.where(own_row, sign * pltpu.roll(far, to_normal, 0), 0.0)
        push = jnp.where(cross_row, pltpu.roll(drop, to_tangent, 0), push)
        on_edge.append(patch[side] - (0.5 * STEP_SIZE) * wet * push)
        kept = own_row & (lane > 0) & (lane < TILE - 1)
        inside.append(jnp.where(kept, (-sign * 0.5 * STEP_SIZE) * wet_in * pltpu.roll(mine, to_normal, 0), 0.0))
    edges, seconds = spread_chunks(on_edge, 0), spread_chunks(inside, 1)
    copies = []
    for low, high in ((0, 24), (24, CHUNKS)):
        for c in range(low, high):
            cut = slice(c * LANES, min((c + 1) * LANES, CELLS))
            width = cut.stop - cut.start
            full[:, cut] = (almost_ref[:, c * LANES:(c + 1) * LANES] + (edges[c] + seconds[c]))[:, :width]
        cells = pl.ds(low * LANES, min(high * LANES, CELLS) - low * LANES)
        for c in range(6):
            copies.append(pltpu.make_async_copy(full.at[c, cells], out_ref.at[c, 0, cells], sems.at[len(copies)]))
            copies[-1].start()
    for copy in copies:
        copy.wait()


def write_out(full, out_ref, sems):
    copies = [pltpu.make_async_copy(full.at[c], out_ref.at[c, 0], sems.at[c]) for c in range(6)]
    for copy in copies:
        copy.start()
    for copy in copies:
        copy.wait()


def at_ends(line, lane_from, lane_to):
    value = jnp.broadcast_to(line[:, lane_from:lane_from + 1], (8, LANES))
    return jnp.where(lanes() == lane_to, value, 0.0)


def edge_kernel(route_ref, lines_ref, base_lines_ref, came0, came1, came2, came3,
                patch_ref, own_two_ref, pay0, pay1, pay2, pay3):
    route = Rows(route_ref)
    lines, base = four_of(lines_ref), four_of(base_lines_ref)
    own = own_rims([sent_line(lines[side], side, route, True) for side in range(4)], route)
    rims = rims_of(route, own, [came[0:8, :] for came in by_link((came0, came1, came2, came3), BOTH)])
    patch = edge_patches(lines, rims)
    whole = with_ends(patch)
    press = []
    for side in range(4):
        patch_ref[8 * side:8 * side + 8, :] = patch[side]
        press.append(sent_line(pressure_of(base[side] + whole[side], rows()), side, route, False))
    for link, pay in zip(SECOND_ORDER, (pay0, pay1, pay2, pay3)):
        pay[...] = chosen(press, route, link)
    own = own_rims(press, route)
    for side in range(4):
        own_two_ref[8 * side:8 * side + 8, :] = own[side]


def middle_kernel(route_ref, state_ref, base_ref, patch_ref, out_ref):
    state = state_ref[...]
    cell, column = column_of()
    base = base_ref[...] + spread(four_of(patch_ref), cell, column)
    row = lax.broadcasted_iota(jnp.int32, (8, WIDE), 0)
    out_ref[...] = if_live(route_ref, base + force_of(state, base, row))


def last_kernel(route_ref, lines_ref, own_ref, almost_ref, came0, came1, came2, came3, out_ref, full, sems):
    route = Rows(route_ref)
    rims = rims_of(route, four_of(own_ref), [came[...] for came in by_link((came0, came1, came2, came3), SECOND_ORDER)])
    patch = []
    for side in range(4):
        wet = wet_rows(lines_ref[8 * side:8 * side + 8, :])
        row = rows()
        rim = pltpu.roll(rims[side], 4 if side % 2 == 1 else 6, 0)
        mine = row < 2 if side % 2 == 1 else (row >= 2) & (row < 4)
        sign = -1.0 if side in (1, 2) else 1.0
        patch.append(jnp.where(mine, (sign * 0.5 * STEP_SIZE) * wet * rim, 0.0))
    cell, column = column_of()
    full[...] = (almost_ref[...] + spread(patch, cell, column))[:, :CELLS]
    write_out(full, out_ref, sems)


def sds(*shape, dtype=jnp.float32):
    return jax.ShapeDtypeStruct(shape, dtype)


PARAMS = pltpu.CompilerParams(vmem_limit_bytes=16 * 1024 * 1024)


def on_device(nx, ny, fields, wet_mask, tile_of_slot, neighbor, rotation):
    line, pair, four, wide = sds(8, LANES), sds(16, LANES), sds(32, LANES), sds(8, WIDE)
    scalars = pltpu.SMEM((4, nx * ny), jnp.int32)
    tables = [pltpu.with_memory_space_constraint(v, pltpu.HBM) for v in (tile_of_slot, neighbor.T, rotation.T)]
    inputs = [pltpu.with_memory_space_constraint(v, pltpu.HBM) for v in (fields.reshape(6, 1, CELLS), wet_mask)]
    halves = pltpu.with_memory_space_constraint(tile_of_slot.reshape(2, LANES), pltpu.HBM)
    raw, wet_raw, lines, inner, *pays, route, halves, table = pl.pallas_call(
        lambda *refs: load_kernel((nx, ny), *refs),
        out_shape=[sds(8, CELLS), sds(8, CELLS, dtype=jnp.int32), four, four, pair, pair, pair, pair,
                   sds(ROUTE, LANES, dtype=jnp.int32),
                   sds(2, LANES, dtype=jnp.int32), sds(8, nx * ny, dtype=jnp.int32)],
        in_specs=[HBM] * 6,
        out_specs=[VMEM] * 11,
        scratch_shapes=[pltpu.SMEM((nx * ny,), jnp.int32), scalars, scalars, pltpu.SemaphoreType.DMA((12,))],
        compiler_params=PARAMS, name="load",
    )(tables[0], halves, *tables[1:], *inputs)
    came_x = exchanged(pays[:2], X_ORDER, nx, ny)
    almost, plan = pl.pallas_call(
        lambda *refs: inner_kernel((nx, ny), *refs),
        out_shape=[wide, sds(16, LANES, dtype=jnp.int32)], in_specs=[HBM] * 3 + [VMEM] * 3, out_specs=[VMEM] * 2,
        scratch_shapes=[pltpu.VMEM((8, WIDE), jnp.float32), pltpu.SMEM((nx * ny,), jnp.int32), scalars, scalars,
                        pltpu.SemaphoreType.DMA((3,))],
        compiler_params=PARAMS, name="inner",
        cost_estimate=pl.CostEstimate(flops=2000000, bytes_accessed=800000, transcendentals=0),
    )(*tables, raw, wet_raw, route)
    sent = pl.pallas_call(
        relay_kernel, out_shape=[pair, pair], in_specs=[VMEM] * 4 + [ANY], out_specs=[VMEM] * 2,
        compiler_params=PARAMS, name="relay",
    )(*pays[2:], *came_x, almost)
    came_u = exchanged(sent, U_ORDER, nx, ny)
    flag = pl.pallas_call(
        lambda *refs: check_kernel((nx, ny), *refs),
        out_shape=sds(1, dtype=jnp.int32), in_specs=[VMEM] * 2 + [ANY], out_specs=SMEM,
        compiler_params=PARAMS, name="check",
        cost_estimate=pl.CostEstimate(flops=2000000, bytes_accessed=800000, transcendentals=0),
    )(halves, table, sent[0])

    result = pltpu.HBM((6, 1, CELLS), jnp.float32)
    writing = [pltpu.VMEM((8, CELLS), jnp.float32), pltpu.SemaphoreType.DMA((12,))]

    def grid_like():
        return pl.pallas_call(
            final_kernel, out_shape=result, in_specs=[VMEM] * 9, out_specs=HBM,
            scratch_shapes=writing, compiler_params=PARAMS, name="final",
        )(route, plan, lines, inner, almost, *came_x, *came_u)

    def general():
        came = came_x + came_u
        state, base, base_lines = pl.pallas_call(
            base_kernel, out_shape=[wide, wide, four], in_specs=[VMEM] * 2, out_specs=[VMEM] * 3,
            compiler_params=PARAMS, name="base",
            cost_estimate=pl.CostEstimate(flops=2000000, bytes_accessed=800000, transcendentals=0),
        )(raw, wet_raw)
        patch, own_two, *press = pl.pallas_call(
            edge_kernel, out_shape=[four, four, line, line, line, line],
            in_specs=[VMEM] * 7, out_specs=[VMEM] * 6,
            compiler_params=PARAMS, name="edge",
        )(route, lines, base_lines, *came)
        came_two = exchanged(press, SECOND_ORDER, nx, ny)
        nearly = pl.pallas_call(
            middle_kernel, out_shape=wide, in_specs=[VMEM] * 4, out_specs=VMEM,
            compiler_params=PARAMS, name="middle",
            cost_estimate=pl.CostEstimate(flops=2000000, bytes_accessed=800000, transcendentals=0),
        )(route, state, base, patch)
        return pl.pallas_call(
            last_kernel, out_shape=result, in_specs=[VMEM] * 8, out_specs=HBM,
            scratch_shapes=writing, compiler_params=PARAMS, name="last",
        )(route, lines, own_two, nearly, *came_two)

    out = lax.cond(flag[0] == 0, grid_like, general)
    return out.reshape(1, 6, CELLS)


def solution(mesh):
    nx, ny = mesh.shape["gx"], mesh.shape["gy"]
    in_specs = (P(AXES, None, None), P(AXES, None), P(), P(), P())
    return jax.shard_map(lambda *args: on_device(nx, ny, *args), mesh=mesh, in_specs=in_specs,
                         out_specs=P(AXES, None, None), check_vma=False)
```

```python
import jax
import jax.numpy as jnp
from jax import lax
from jax.experimental import pallas as pl
from jax.experimental.pallas import tpu as pltpu
from jax.sharding import PartitionSpec as P

TILE = 90
CELLS = TILE * TILE
LANES = 128
CHUNKS = 64
WIDE = LANES * CHUNKS
HALF = 45
LAST = CELLS - TILE - (CHUNKS - 2) * LANES

ADVECT = 0.25
DIFFUSE = 0.15
STEP_SIZE = 0.5
CORIOLIS = 0.3
GRAVITY = 0.8

AXES = ("gx", "gy")
VMEM = pl.BlockSpec(memory_space=pltpu.VMEM)
SMEM = pl.BlockSpec(memory_space=pltpu.SMEM)
ANY = pl.BlockSpec(memory_space=pl.ANY)
HBM = pl.BlockSpec(memory_space=pltpu.HBM)


def link_x_even(x, y, nx, ny):
    return x ^ 1, y


def link_x_odd(x, y, nx, ny):
    return (((x + nx - 1) % nx ^ 1) + 1) % nx, y


def link_y_even(x, y, nx, ny):
    return x, y ^ 1


def link_y_odd(x, y, nx, ny):
    if y == 0 or y == ny - 1:
        return (x + nx // 2) % nx, y
    return x, ((y - 1) ^ 1) + 1


def swapped(x, nx):
    return (x % (nx // 2) == 0) | (x % (nx // 2) == 2)


def link_u_first(x, y, nx, ny):
    return (link_y_even if swapped(x, nx) else link_y_odd)(x, y, nx, ny)


def link_u_second(x, y, nx, ny):
    return (link_y_odd if swapped(x, nx) else link_y_even)(x, y, nx, ny)


LINKS = (link_u_first, link_x_even, link_u_second, link_x_odd)


def pairs_of(link, nx, ny):
    out = []
    for x in range(nx):
        for y in range(ny):
            to_x, to_y = link(x, y, nx, ny)
            out.append((x * ny + y, to_x * ny + to_y))
    return out


U_ORDER = (0, 2)
X_ORDER = (3, 1)
BOTH = U_ORDER + X_ORDER
SECOND_ORDER = (2, 0, 3, 1)


def exchanged(pays, order, nx, ny):
    return [lax.ppermute(pay, AXES, pairs_of(LINKS[link], nx, ny)) for pay, link in zip(pays, order)]


def by_link(refs, order, links=(0, 1, 2, 3)):
    return [refs[order.index(link)] for link in links]


def partner(me, which, nx, ny):
    x, y = me // ny, me % ny
    if which == 1:
        return me + jnp.where(x % 2 == 0, ny, -ny)
    if which == 3:
        return (x + jnp.where(x % 2 == 1, 1, nx - 1)) % nx * ny + y
    even = me + jnp.where(y % 2 == 0, 1, -1)
    pole = (y == 0) | (y == ny - 1)
    odd = jnp.where(pole, (x + nx // 2) % nx * ny + y, me + jnp.where(y % 2 == 1, 1, -1))
    return jnp.where(swapped(x, nx), even, odd) if which == 0 else jnp.where(swapped(x, nx), odd, even)


def lanes():
    return lax.broadcasted_iota(jnp.int32, (8, LANES), 1)


def rows():
    return lax.broadcasted_iota(jnp.int32, (8, LANES), 0)


def pick(values, index):
    return jnp.take_along_axis(values, index, axis=1)


def tiled(values, count):
    return jnp.concatenate([values] * count, axis=1)


def column_of():
    cell = lax.broadcasted_iota(jnp.int32, (8, WIDE), 1)
    line = jnp.floor((cell.astype(jnp.float32) + 0.5) * (1.0 / TILE)).astype(jnp.int32)
    return cell, cell - TILE * line


def edge_lines(state, column):
    lane = lanes()
    edge = (column == 0) | (column == TILE - 1)
    parts = []
    for low, high in ((0, HALF), (HALF, CHUNKS)):
        found = jnp.zeros((8, LANES), jnp.float32)
        for c in range(low, high):
            cut = slice(c * LANES, (c + 1) * LANES)
            found = jnp.where(edge[:, cut], state[:, cut], found)
        parts.append(found)
    east_at = (TILE * lane + TILE - 1) & (LANES - 1)
    west_at = (TILE * lane) & (LANES - 1)
    east = jnp.where(lane < 64, pick(parts[0], east_at), pick(parts[1], east_at))
    west = jnp.where(lane < 64, pick(parts[0], west_at), pick(parts[1], west_at))
    south = state[:, :LANES]
    before = pltpu.roll(state[:, (CHUNKS - 2) * LANES:(CHUNKS - 1) * LANES], LANES - LAST, 1)
    after = pltpu.roll(state[:, (CHUNKS - 1) * LANES:], LANES - LAST, 1)
    north = jnp.where(lane < LANES - LAST, before, after)
    return [south, east, north, west]


def spread(lines, cell, column):
    south, east, north, west = lines
    lane = lanes()
    odd = (lane & 1) == 1
    line_at = (37 * ((lane + jnp.where(odd, 39, 0)) >> 1)) & 63
    early = jnp.where(odd, pick(east, line_at), pick(west, line_at))
    late = jnp.where(odd, pick(east, line_at + 64), pick(west, line_at + 64))
    sides = jnp.concatenate([early] * HALF + [late] * (CHUNKS - HALF), axis=1)
    edge = (column == 0) | (column == TILE - 1)
    out = jnp.where(edge, sides, 0.0)
    first = jnp.where(lane < TILE, south, 0.0) + out[:, :LANES]
    moved = pltpu.roll(north, LAST, 1)
    before = out[:, (CHUNKS - 2) * LANES:(CHUNKS - 1) * LANES] + jnp.where(lane >= LAST, moved, 0.0)
    after = out[:, (CHUNKS - 1) * LANES:] + jnp.where(lane < LAST + TILE - LANES, moved, 0.0)
    return jnp.concatenate([first, out[:, LANES:(CHUNKS - 2) * LANES], before, after], axis=1)


def neighbours(state):
    cell, column = column_of()
    right = jnp.where(column == TILE - 1, 0.0, pltpu.roll(state, WIDE - 1, 1))
    left = jnp.where(column == 0, 0.0, pltpu.roll(state, 1, 1))
    up = jnp.where(cell >= CELLS - TILE, 0.0, pltpu.roll(state, WIDE - TILE, 1))
    down = jnp.where(cell < TILE, 0.0, pltpu.roll(state, TILE, 1))
    return right, left, up, down, cell, column


def row_of(values):
    return lax.broadcasted_iota(jnp.int32, values.shape, 0)


def repeated(values, first):
    row = row_of(values)
    if first == 0:
        pair = jnp.where(row < 2, values, pltpu.roll(values, 2, 0))
    else:
        pair = jnp.where(row < 4, values, pltpu.roll(values, 2, 0))
        pair = jnp.where(row < 2, pltpu.roll(values, 6, 0), pair)
        return pair
    return jnp.where(row < 4, pair, pltpu.roll(values, 4, 0))


def wet_rows(values):
    return jnp.broadcast_to(values[6:7], values.shape)


def turned(line, turns):
    row = row_of(line)
    swapped = jnp.where(row < 2, pltpu.roll(line, 6, 0), pltpu.roll(line, 2, 0))
    velocity = row < 4
    second = jnp.where(row < 2, swapped, -swapped)
    odd = jnp.where(turns % 2 == 1, 1, 0)
    out = jnp.where(jnp.logical_and(velocity, odd == 1), second, line)
    back = jnp.where(turns >= 2, 1, 0)
    return jnp.where(jnp.logical_and(velocity, back == 1), -out, out)


def flipped(line):
    return pick(line, jnp.maximum(TILE - 1 - lanes(), 0))


ROUTE = 48
OWN_AT, RELAY_AT = TILE, {0: TILE + 4, 2: TILE + 8}


class Rows:
    def __init__(self, ref):
        self.ref = ref

    def __getitem__(self, i):
        return jnp.broadcast_to(self.ref[i:i + 1, :], (8, LANES))


def my_index(ny):
    return lax.axis_index("gx") * ny + lax.axis_index("gy")


def sent_line(line, side, route, vector):
    line = jnp.where(route[32 + side] == 1, flipped(line), line)
    return turned(line, route[36 + side]) if vector else line


def chosen(lines, route, link):
    total = jnp.zeros((8, LANES), jnp.float32)
    for side in range(4):
        total = jnp.where(route[4 * link + side] == 1, lines[side], total)
    return total


def own_rims(sent, route):
    out = []
    for target in range(4):
        total = jnp.zeros((8, LANES), jnp.float32)
        for side in range(4):
            total = jnp.where(route[16 + 4 * side + target] == 1, sent[side], total)
        out.append(total)
    return out


def rims_of(route, base, came):
    out = []
    for side in range(4):
        rim = base[side] if base is not None else jnp.zeros((8, LANES), jnp.float32)
        for link in range(4):
            rim = jnp.where(route[4 * link + side] == 1, came[link], rim)
        out.append(rim)
    return out


def four_of(ref):
    return [ref[8 * side:8 * side + 8, :] for side in range(4)]


def columns_at(step):
    lane = lanes()
    odd = lane & 1
    shift = jnp.where(odd == 1, 39 + step, -step) if step % 2 == 0 else jnp.where(odd == 1, -step, 39 + step)
    column = jnp.where(odd == 1, TILE - 1 - step, step) if step % 2 == 0 else jnp.where(odd == 1, step, TILE - 1 - step)
    line_at = (37 * ((lane + shift) >> 1)) & 63
    return line_at, (TILE * line_at + column) >> 7


def raw_lines(chunk_of, step):
    lane = lanes()
    _, home = columns_at(step)
    parts = []
    for low, high in ((0, HALF), (HALF, CHUNKS)):
        found = chunk_of(low)
        for c in range(low + 1, high):
            found = jnp.where(home == c - low, chunk_of(c), found)
        parts.append(found)
    early = lane < 64
    out = [None] * 4
    for side, column in ((1, TILE - 1 - step), (3, step)):
        at = (TILE * lane + column) & (LANES - 1)
        out[side] = jnp.where(early, pick(parts[0], at), pick(parts[1], at))
    for side, first in ((0, TILE * step), (2, CELLS - TILE - TILE * step)):
        low, start = first // LANES, first % LANES
        if start == 0:
            out[side] = chunk_of(low)
        else:
            before = pltpu.roll(chunk_of(low), LANES - start, 1)
            after = pltpu.roll(chunk_of(low + 1), LANES - start, 1)
            out[side] = jnp.where(lane < LANES - start, before, after)
    return out


def spread_chunks(lines, step):
    lane = lanes()
    line_at, home = columns_at(step)
    odd = (lane & 1) == 1
    first_odd, first_even = (lines[1], lines[3]) if step % 2 == 0 else (lines[3], lines[1])
    early = jnp.where(odd, pick(first_odd, line_at), pick(first_even, line_at))
    late = jnp.where(odd, pick(first_odd, line_at + 64), pick(first_even, line_at + 64))
    out = []
    for c in range(CHUNKS):
        out.append(jnp.where(home == (c if c < HALF else c - HALF), early if c < HALF else late, 0.0))
    for side, first in ((0, TILE * step), (2, CELLS - TILE - TILE * step)):
        low, start = first // LANES, first % LANES
        line = jnp.where(lane < TILE, lines[side], 0.0)
        if start == 0:
            out[low] = out[low] + line
        else:
            moved = pltpu.roll(line, start, 1)
            out[low] = out[low] + jnp.where(lane >= start, moved, 0.0)
            if start + TILE > LANES:
                out[low + 1] = out[low + 1] + jnp.where(lane < start + TILE - LANES, moved, 0.0)
    return out


def load_kernel(shape, tiles_hbm, halves_hbm, near_hbm, turn_hbm, fields_ref, wet_ref,
                raw, wet_raw, lines_ref, inner_ref, pay0, pay1, pay2, pay3, route_ref, halves_ref, table_ref,
                tiles_ref, near_ref, turn_ref, sems):
    nx, ny = shape
    tables = [pltpu.make_async_copy(tiles_hbm, tiles_ref, sems.at[7]),
              pltpu.make_async_copy(near_hbm, near_ref, sems.at[8]),
              pltpu.make_async_copy(turn_hbm, turn_ref, sems.at[9])]
    copies = [pltpu.make_async_copy(fields_ref.at[c, 0], raw.at[c], sems.at[c]) for c in range(6)]
    copies.append(pltpu.make_async_copy(wet_ref.at[0], wet_raw.at[0], sems.at[6]))
    copies.append(pltpu.make_async_copy(halves_hbm, halves_ref, sems.at[10]))
    copies.append(pltpu.make_async_copy(near_hbm, table_ref.at[0:4], sems.at[11]))
    for copy in tables + copies:
        copy.start()
    for copy in tables:
        copy.wait()
    me = my_index(ny)
    route = [None] * ROUTE
    tile = tiles_ref[me]
    live = tile >= 0
    held = jnp.maximum(tile, 0)
    near = [jnp.where(live, near_ref[side, held], -1) for side in range(4)]
    turn = [turn_ref[side, held] for side in range(4)]
    for link in range(4):
        other = tiles_ref[partner(me, link, nx, ny)]
        for side in range(4):
            route[4 * link + side] = jnp.where((near[side] >= 0) & (near[side] == other), 1, 0)
    for side in range(4):
        target = (side + 2 + turn[side]) % 4
        for k in range(4):
            route[16 + 4 * side + k] = jnp.where((near[side] >= 0) & (near[side] == tile) & (target == k), 1, 0)
        route[32 + side] = jnp.where((target < 2) != (side >= 2), 1, 0)
        route[36 + side] = (4 - turn[side]) % 4
    route[40] = jnp.where(live, 1, 0)
    for i in range(41):
        route_ref[i:i + 1, :] = jnp.full((1, LANES), route[i], jnp.int32)
    for copy in copies:
        copy.wait()

    def chunk(ref, c):
        if c < CHUNKS - 1:
            return ref[:, c * LANES:(c + 1) * LANES]
        rest = CELLS - c * LANES
        part = ref[:, c * LANES:CELLS]
        return jnp.concatenate([part, jnp.zeros((8, LANES - rest), part.dtype)], axis=1)

    row, lane = rows(), lanes()
    both = []
    for step, ref in ((0, lines_ref), (1, inner_ref)):
        lines = []
        for value, wet in zip(raw_lines(lambda c: chunk(raw, c), step), raw_lines(lambda c: chunk(wet_raw, c), step)):
            wet = jnp.broadcast_to(wet[0:1], (8, LANES)).astype(jnp.float32)
            lines.append(jnp.where(row < 6, value * wet, jnp.where(row == 6, wet, 0.0)))
        for side in range(4):
            ref[8 * side:8 * side + 8, :] = lines[side]
        both.append(lines)
    ends = [jnp.where((lane == OWN_AT + 1) | (lane == OWN_AT + 2), TILE - 1, 0)] * 2
    corners = jnp.where(lane < OWN_AT + 2, pick(both[0][0], ends[0]), pick(both[0][2], ends[1]))
    at_corners = (lane >= OWN_AT) & (lane < OWN_AT + 4)
    sent = [sent_line(both[0][side], side, route, True) for side in range(4)]
    sent_inner = [sent_line(both[1][side], side, route, False) for side in range(4)]
    for link, pay in zip(BOTH, (pay0, pay1, pay2, pay3)):
        pay[0:8, :] = jnp.where(at_corners, corners, chosen(sent, route, link))
        pay[8:16, :] = chosen(sent_inner, route, link)


def pressure_of(tracer, row):
    return GRAVITY * jnp.where(row == 5, tracer + pltpu.roll(tracer, 1, 0), tracer)


def force_of(state, base, row):
    right, left, up, down, cell, column = neighbours(pressure_of(base, row))
    slope = jnp.where(row < 2, pltpu.roll(right - left, 4, 0), pltpu.roll(up - down, 6, 0))
    swapped = jnp.where(row < 2, pltpu.roll(state, 6, 0), -pltpu.roll(state, 2, 0))
    force = STEP_SIZE * (CORIOLIS * swapped - 0.5 * slope)
    return jnp.where(row < 4, wet_rows(state) * force, 0.0)


def masked_state(raw, wet_raw, state_ref):
    state_ref[:, (CHUNKS - 1) * LANES:] = jnp.zeros((8, LANES), jnp.float32)
    for low, high in ((0, (CHUNKS - 1) * LANES), ((CHUNKS - 1) * LANES, CELLS)):
        size = (8, high - low)
        row = lax.broadcasted_iota(jnp.int32, size, 0)
        wet = jnp.broadcast_to(wet_raw[0:1, low:high].astype(jnp.float32), size)
        state_ref[:, low:high] = jnp.where(row < 6, raw[:, low:high] * wet, jnp.where(row == 6, wet, 0.0))
    return state_ref[...]


def without_rims(state):
    right, left, up, down, cell, column = neighbours(state)
    first, second, wet = repeated(state, 0), repeated(state, 2), wet_rows(state)
    along = first * (right - left) + second * (up - down)
    round_sum = right + left + up + down - 4.0 * state
    return wet * (state - (0.5 * ADVECT) * along + DIFFUSE * round_sum), column


def if_live(route_ref, values):
    return jnp.where(tiled(Rows(route_ref)[40], CHUNKS) == 1, values, 0.0)


def base_kernel(raw, wet_raw, state_ref, base_ref, base_lines_ref):
    state = masked_state(raw, wet_raw, state_ref)
    base, column = without_rims(state)
    base_ref[...] = base
    lines = edge_lines(base, column)
    for side in range(4):
        base_lines_ref[8 * side:8 * side + 8, :] = lines[side]


def inner_kernel(shape, tiles_hbm, near_hbm, turn_hbm, raw, wet_raw, route_ref, halves_ref, table_ref,
                 almost_ref, plan_ref, flag, state_ref, tiles_ref, near_ref, turn_ref, sems):
    copies = [pltpu.make_async_copy(tiles_hbm, tiles_ref, sems.at[0]),
              pltpu.make_async_copy(near_hbm, near_ref, sems.at[1]),
              pltpu.make_async_copy(turn_hbm, turn_ref, sems.at[2])]
    for copy in copies:
        copy.start()
    flag[0] = off_grid(shape, halves_ref, table_ref)
    state = masked_state(raw, wet_raw, state_ref)
    base, _ = without_rims(state)
    almost_ref[...] = base
    for copy in copies:
        copy.wait()
    corner_plan(shape, tiles_ref, near_ref, turn_ref, plan_ref)
    base = almost_ref[...]
    row = lax.broadcasted_iota(jnp.int32, (8, WIDE), 0)
    almost_ref[...] = if_live(route_ref, base + force_of(state_ref[...], base, row))


def off_grid(shape, halves_ref, table_ref):
    nx, ny = shape
    row, lane = rows(), lanes()
    tiles = [jnp.broadcast_to(halves_ref[half:half + 1, :], (8, LANES)) for half in range(2)]
    near = [table_ref[:, half * LANES:(half + 1) * LANES] for half in range(2)]

    def look(table, index):
        return jnp.where(index < LANES, pick(table[0], index & (LANES - 1)), pick(table[1], index & (LANES - 1)))

    worst = jnp.zeros((8, LANES), jnp.int32)
    for half in range(2):
        tile = tiles[half]
        mine = look(near, jnp.maximum(tile, 0))
        linked = (tile >= 0) & (mine >= 0) & (row < 4)
        other = [look(tiles, partner(lane + half * LANES, link, nx, ny)) for link in range(4)]
        over_x = (mine == other[1]) | (mine == other[3])
        kind = jnp.where(linked, jnp.where(mine == tile, 4, jnp.where(over_x, 1, 2)), 0)
        after = jnp.where(row < 3, pltpu.roll(kind, 7, 0), pltpu.roll(kind, 3, 0))
        odd = (kind == 4) | ((kind > 0) & (kind == after) & (row < 4))
        worst = jnp.where(odd, 1, worst)
    return jnp.max(worst)


def corner_plan(shape, tiles_ref, near_ref, turn_ref, plan_ref):
    nx, ny = shape
    me = my_index(ny)
    tile = tiles_ref[me]
    held = jnp.maximum(tile, 0)
    across = [partner(me, link, nx, ny) for link in range(4)]
    relayed = [(which, RELAY_AT[u], tiles_ref[partner(across[x], u, nx, ny)])
               for which, x in ((1, 1), (2, 3)) for u in (0, 2)]
    for link in range(4):
        other = tiles_ref[across[link]]
        side = jnp.int32(-1)
        for k in range(4):
            side = jnp.where((tile >= 0) & (other >= 0) & (near_ref[k, held] == other), k, side)
        facing = (side + 2 + turn_ref[jnp.maximum(side, 0), held]) % 4
        there = jnp.maximum(other, 0)
        for end in range(2):
            later = (side < 2) == (end == 0)
            lateral = jnp.where(later, facing + 1, facing + 3) % 4
            beyond = jnp.where(side >= 0, near_ref[lateral, there], -1)
            back = (lateral + 2 + turn_ref[lateral, there]) % 4
            corner = jnp.where(later, back + 1, back) % 4
            buffer, lane = jnp.int32(0), jnp.int32(0)
            for which, base, name in relayed:
                here = (beyond >= 0) & (beyond == name)
                buffer, lane = jnp.where(here, which, buffer), jnp.where(here, base + corner, lane)
            at = 2 * (2 * link + end)
            plan_ref[at:at + 1, :] = jnp.full((1, LANES), buffer, jnp.int32)
            plan_ref[at + 1:at + 2, :] = jnp.full((1, LANES), lane, jnp.int32)


def relay_kernel(pay0, pay1, came0, came1, after, out0, out1):
    lane = lanes()
    for pay, out in ((pay0, out0), (pay1, out1)):
        line = pay[0:8, :]
        for link, came in zip(U_ORDER, (came0, came1)):
            moved = pltpu.roll(came[0:8, :], RELAY_AT[link] - OWN_AT, 1)
            line = jnp.where((lane >= RELAY_AT[link]) & (lane < RELAY_AT[link] + 4), moved, line)
        out[0:8, :] = line
        out[8:16, :] = pay[8:16, :]


def edge_patches(lines, rims):
    patch = []
    for side in range(4):
        drift = repeated(lines[side], 0 if side % 2 == 1 else 2)
        sign = 1.0 if side in (1, 2) else -1.0
        patch.append(wet_rows(lines[side]) * (DIFFUSE - (sign * 0.5 * ADVECT) * drift) * rims[side])
    return patch


def with_ends(patch):
    south, east, north, west = patch
    end = TILE - 1
    return [
        south + at_ends(west, 0, 0) + at_ends(east, 0, end),
        east + at_ends(south, end, 0) + at_ends(north, end, end),
        north + at_ends(west, end, 0) + at_ends(east, end, end),
        west + at_ends(south, 0, 0) + at_ends(north, 0, end),
    ]


def final_kernel(route_ref, plan_ref, lines_ref, inner_ref, almost_ref, first, second, third, fourth, out_ref, full, sems):
    lane, row = lanes(), rows()
    route, plan = Rows(route_ref), Rows(plan_ref)
    came = by_link((first, second, third, fourth), BOTH)
    outer = []
    for link in range(4):
        line = came[link][0:8, :]
        for end, lane_to in ((0, LANES - 1), (1, TILE)):
            which, lane_from = plan[2 * (2 * link + end)], plan[2 * (2 * link + end) + 1]
            held = jnp.where(which == 2, came[3][0:8, :], came[1][0:8, :])
            value = pick(held, lane_from)
            line = jnp.where(lane == lane_to, jnp.where(which > 0, value, 0.0), line)
        outer.append(line)
    rims = rims_of(route, None, outer)
    beyond = rims_of(route, None, [came[link][8:16, :] for link in range(4)])
    lines, inner = four_of(lines_ref), four_of(inner_ref)
    patch = edge_patches(lines, rims)
    whole = with_ends(patch)
    on_edge, inside = [], []
    for side in range(4):
        sign = 1.0 if side in (1, 2) else -1.0
        line, wet, wet_in = rims[side], wet_rows(lines[side]), wet_rows(inner[side])
        after, before = pltpu.roll(line, LANES - 1, 1), pltpu.roll(line, 1, 1)
        first, second = pltpu.roll(line, 4, 0), pltpu.roll(line, 2, 0)
        normal, tangent = (first, second) if side % 2 == 1 else (second, first)
        along = normal * (sign * (beyond[side] - lines[side])) + tangent * (after - before)
        round_sum = after + before + beyond[side] + lines[side] - 4.0 * line
        tracer = wet_rows(line) * (line - (0.5 * ADVECT) * along + DIFFUSE * round_sum)
        far = pressure_of(tracer, row)
        mine = jnp.where(lane < TILE, pressure_of(whole[side], row), 0.0)
        drop = pltpu.roll(mine, LANES - 1, 1) - pltpu.roll(mine, 1, 1)
        to_normal, to_tangent = (4, 6) if side % 2 == 1 else (6, 4)
        own_row = row < 2 if side % 2 == 1 else (row >= 2) & (row < 4)
        cross_row = (row >= 2) & (row < 4) if side % 2 == 1 else row < 2
        push = jnp.where(own_row, sign * pltpu.roll(far, to_normal, 0), 0.0)
        push = jnp.where(cross_row, pltpu.roll(drop, to_tangent, 0), push)
        on_edge.append(patch[side] - (0.5 * STEP_SIZE) * wet * push)
        kept = own_row & (lane > 0) & (lane < TILE - 1)
        inside.append(jnp.where(kept, (-sign * 0.5 * STEP_SIZE) * wet_in * pltpu.roll(mine, to_normal, 0), 0.0))
    edges, seconds = spread_chunks(on_edge, 0), spread_chunks(inside, 1)
    copies = []
    for low, high in ((0, 24), (24, CHUNKS)):
        for c in range(low, high):
            cut = slice(c * LANES, min((c + 1) * LANES, CELLS))
            width = cut.stop - cut.start
            full[:, cut] = (almost_ref[:, c * LANES:(c + 1) * LANES] + (edges[c] + seconds[c]))[:, :width]
        cells = pl.ds(low * LANES, min(high * LANES, CELLS) - low * LANES)
        for c in range(6):
            copies.append(pltpu.make_async_copy(full.at[c, cells], out_ref.at[c, 0, cells], sems.at[len(copies)]))
            copies[-1].start()
    for copy in copies:
        copy.wait()


def write_out(full, out_ref, sems):
    copies = [pltpu.make_async_copy(full.at[c], out_ref.at[c, 0], sems.at[c]) for c in range(6)]
    for copy in copies:
        copy.start()
    for copy in copies:
        copy.wait()


def at_ends(line, lane_from, lane_to):
    value = jnp.broadcast_to(line[:, lane_from:lane_from + 1], (8, LANES))
    return jnp.where(lanes() == lane_to, value, 0.0)


def edge_kernel(route_ref, lines_ref, base_lines_ref, came0, came1, came2, came3,
                patch_ref, own_two_ref, pay0, pay1, pay2, pay3):
    route = Rows(route_ref)
    lines, base = four_of(lines_ref), four_of(base_lines_ref)
    own = own_rims([sent_line(lines[side], side, route, True) for side in range(4)], route)
    rims = rims_of(route, own, [came[0:8, :] for came in by_link((came0, came1, came2, came3), BOTH)])
    patch = edge_patches(lines, rims)
    whole = with_ends(patch)
    press = []
    for side in range(4):
        patch_ref[8 * side:8 * side + 8, :] = patch[side]
        press.append(sent_line(pressure_of(base[side] + whole[side], rows()), side, route, False))
    for link, pay in zip(SECOND_ORDER, (pay0, pay1, pay2, pay3)):
        pay[...] = chosen(press, route, link)
    own = own_rims(press, route)
    for side in range(4):
        own_two_ref[8 * side:8 * side + 8, :] = own[side]


def middle_kernel(route_ref, state_ref, base_ref, patch_ref, out_ref):
    state = state_ref[...]
    cell, column = column_of()
    base = base_ref[...] + spread(four_of(patch_ref), cell, column)
    row = lax.broadcasted_iota(jnp.int32, (8, WIDE), 0)
    out_ref[...] = if_live(route_ref, base + force_of(state, base, row))


def last_kernel(route_ref, lines_ref, own_ref, almost_ref, came0, came1, came2, came3, out_ref, full, sems):
    route = Rows(route_ref)
    rims = rims_of(route, four_of(own_ref), [came[...] for came in by_link((came0, came1, came2, came3), SECOND_ORDER)])
    patch = []
    for side in range(4):
        wet = wet_rows(lines_ref[8 * side:8 * side + 8, :])
        row = rows()
        rim = pltpu.roll(rims[side], 4 if side % 2 == 1 else 6, 0)
        mine = row < 2 if side % 2 == 1 else (row >= 2) & (row < 4)
        sign = -1.0 if side in (1, 2) else 1.0
        patch.append(jnp.where(mine, (sign * 0.5 * STEP_SIZE) * wet * rim, 0.0))
    cell, column = column_of()
    full[...] = (almost_ref[...] + spread(patch, cell, column))[:, :CELLS]
    write_out(full, out_ref, sems)


def sds(*shape, dtype=jnp.float32):
    return jax.ShapeDtypeStruct(shape, dtype)


PARAMS = pltpu.CompilerParams(vmem_limit_bytes=16 * 1024 * 1024)


def on_device(nx, ny, fields, wet_mask, tile_of_slot, neighbor, rotation):
    line, pair, four, wide = sds(8, LANES), sds(16, LANES), sds(32, LANES), sds(8, WIDE)
    scalars = pltpu.SMEM((4, nx * ny), jnp.int32)
    tables = [pltpu.with_memory_space_constraint(v, pltpu.HBM) for v in (tile_of_slot, neighbor.T, rotation.T)]
    inputs = [pltpu.with_memory_space_constraint(v, pltpu.HBM) for v in (fields.reshape(6, 1, CELLS), wet_mask)]
    halves = pltpu.with_memory_space_constraint(tile_of_slot.reshape(2, LANES), pltpu.HBM)
    raw, wet_raw, lines, inner, *pays, route, halves, table = pl.pallas_call(
        lambda *refs: load_kernel((nx, ny), *refs),
        out_shape=[sds(8, CELLS), sds(8, CELLS, dtype=jnp.int32), four, four, pair, pair, pair, pair,
                   sds(ROUTE, LANES, dtype=jnp.int32),
                   sds(2, LANES, dtype=jnp.int32), sds(8, nx * ny, dtype=jnp.int32)],
        in_specs=[HBM] * 6,
        out_specs=[VMEM] * 11,
        scratch_shapes=[pltpu.SMEM((nx * ny,), jnp.int32), scalars, scalars, pltpu.SemaphoreType.DMA((12,))],
        compiler_params=PARAMS, name="load",
    )(tables[0], halves, *tables[1:], *inputs)
    came_u = exchanged(pays[:2], U_ORDER, nx, ny)
    almost, plan, flag = pl.pallas_call(
        lambda *refs: inner_kernel((nx, ny), *refs),
        out_shape=[wide, sds(16, LANES, dtype=jnp.int32), sds(1, dtype=jnp.int32)],
        in_specs=[HBM] * 3 + [VMEM] * 5, out_specs=[VMEM, VMEM, SMEM],
        scratch_shapes=[pltpu.VMEM((8, WIDE), jnp.float32), pltpu.SMEM((nx * ny,), jnp.int32), scalars, scalars,
                        pltpu.SemaphoreType.DMA((3,))],
        compiler_params=PARAMS, name="inner",
        cost_estimate=pl.CostEstimate(flops=2000000, bytes_accessed=800000, transcendentals=0),
    )(*tables, raw, wet_raw, route, halves, table)
    sent = pl.pallas_call(
        relay_kernel, out_shape=[pair, pair], in_specs=[VMEM] * 4 + [ANY], out_specs=[VMEM] * 2,
        compiler_params=PARAMS, name="relay",
    )(*pays[2:], *came_u, almost)
    came_x = exchanged(sent, X_ORDER, nx, ny)
    result = pltpu.HBM((6, 1, CELLS), jnp.float32)
    writing = [pltpu.VMEM((8, CELLS), jnp.float32), pltpu.SemaphoreType.DMA((12,))]

    def grid_like():
        return pl.pallas_call(
            final_kernel, out_shape=result, in_specs=[VMEM] * 9, out_specs=HBM,
            scratch_shapes=writing, compiler_params=PARAMS, name="final",
        )(route, plan, lines, inner, almost, *came_u, *came_x)

    def general():
        came = came_u + came_x
        state, base, base_lines = pl.pallas_call(
            base_kernel, out_shape=[wide, wide, four], in_specs=[VMEM] * 2, out_specs=[VMEM] * 3,
            compiler_params=PARAMS, name="base",
            cost_estimate=pl.CostEstimate(flops=2000000, bytes_accessed=800000, transcendentals=0),
        )(raw, wet_raw)
        patch, own_two, *press = pl.pallas_call(
            edge_kernel, out_shape=[four, four, line, line, line, line],
            in_specs=[VMEM] * 7, out_specs=[VMEM] * 6,
            compiler_params=PARAMS, name="edge",
        )(route, lines, base_lines, *came)
        came_two = exchanged(press, SECOND_ORDER, nx, ny)
        nearly = pl.pallas_call(
            middle_kernel, out_shape=wide, in_specs=[VMEM] * 4, out_specs=VMEM,
            compiler_params=PARAMS, name="middle",
            cost_estimate=pl.CostEstimate(flops=2000000, bytes_accessed=800000, transcendentals=0),
        )(route, state, base, patch)
        return pl.pallas_call(
            last_kernel, out_shape=result, in_specs=[VMEM] * 8, out_specs=HBM,
            scratch_shapes=writing, compiler_params=PARAMS, name="last",
        )(route, lines, own_two, nearly, *came_two)

    out = lax.switch(flag[0], [grid_like, general])
    return out.reshape(1, 6, CELLS)


def solution(mesh):
    nx, ny = mesh.shape["gx"], mesh.shape["gy"]
    in_specs = (P(AXES, None, None), P(AXES, None), P(), P(), P())
    return jax.shard_map(lambda *args: on_device(nx, ny, *args), mesh=mesh, in_specs=in_specs,
                         out_specs=P(AXES, None, None), check_vma=False)
```

```python
import jax
import jax.numpy as jnp
from jax import lax
from jax.experimental import pallas as pl
from jax.experimental.pallas import tpu as pltpu
from jax.sharding import PartitionSpec as P

TILE = 90
CELLS = TILE * TILE
LANES = 128
CHUNKS = 64
WIDE = LANES * CHUNKS
HALF = 45
LAST = CELLS - TILE - (CHUNKS - 2) * LANES

ADVECT = 0.25
DIFFUSE = 0.15
STEP_SIZE = 0.5
CORIOLIS = 0.3
GRAVITY = 0.8

AXES = ("gx", "gy")
VMEM = pl.BlockSpec(memory_space=pltpu.VMEM)
SMEM = pl.BlockSpec(memory_space=pltpu.SMEM)
ANY = pl.BlockSpec(memory_space=pl.ANY)
HBM = pl.BlockSpec(memory_space=pltpu.HBM)


def link_x_even(x, y, nx, ny):
    return x ^ 1, y


def link_x_odd(x, y, nx, ny):
    return (((x + nx - 1) % nx ^ 1) + 1) % nx, y


def link_y_even(x, y, nx, ny):
    return x, y ^ 1


def link_y_odd(x, y, nx, ny):
    if y == 0 or y == ny - 1:
        return (x + nx // 2) % nx, y
    return x, ((y - 1) ^ 1) + 1


def swapped(x, nx):
    return (x % (nx // 2) == 0) | (x % (nx // 2) == 2)


def link_u_first(x, y, nx, ny):
    return (link_y_even if swapped(x, nx) else link_y_odd)(x, y, nx, ny)


def link_u_second(x, y, nx, ny):
    return (link_y_odd if swapped(x, nx) else link_y_even)(x, y, nx, ny)


LINKS = (link_u_first, link_x_even, link_u_second, link_x_odd)


def pairs_of(link, nx, ny):
    out = []
    for x in range(nx):
        for y in range(ny):
            to_x, to_y = link(x, y, nx, ny)
            out.append((x * ny + y, to_x * ny + to_y))
    return out


U_ORDER = (0, 2)
X_ORDER = (3, 1)
BOTH = U_ORDER + X_ORDER
SECOND_ORDER = (2, 0, 3, 1)


def exchanged(pays, order, nx, ny):
    return [lax.ppermute(pay, AXES, pairs_of(LINKS[link], nx, ny)) for pay, link in zip(pays, order)]


def by_link(refs, order, links=(0, 1, 2, 3)):
    return [refs[order.index(link)] for link in links]


def partner(me, which, nx, ny):
    x, y = me // ny, me % ny
    if which == 1:
        return me + jnp.where(x % 2 == 0, ny, -ny)
    if which == 3:
        return (x + jnp.where(x % 2 == 1, 1, nx - 1)) % nx * ny + y
    even = me + jnp.where(y % 2 == 0, 1, -1)
    pole = (y == 0) | (y == ny - 1)
    odd = jnp.where(pole, (x + nx // 2) % nx * ny + y, me + jnp.where(y % 2 == 1, 1, -1))
    return jnp.where(swapped(x, nx), even, odd) if which == 0 else jnp.where(swapped(x, nx), odd, even)


def lanes():
    return lax.broadcasted_iota(jnp.int32, (8, LANES), 1)


def rows():
    return lax.broadcasted_iota(jnp.int32, (8, LANES), 0)


def pick(values, index):
    return jnp.take_along_axis(values, index, axis=1)


def tiled(values, count):
    return jnp.concatenate([values] * count, axis=1)


def column_of():
    cell = lax.broadcasted_iota(jnp.int32, (8, WIDE), 1)
    line = jnp.floor((cell.astype(jnp.float32) + 0.5) * (1.0 / TILE)).astype(jnp.int32)
    return cell, cell - TILE * line


def edge_lines(state, column):
    lane = lanes()
    edge = (column == 0) | (column == TILE - 1)
    parts = []
    for low, high in ((0, HALF), (HALF, CHUNKS)):
        found = jnp.zeros((8, LANES), jnp.float32)
        for c in range(low, high):
            cut = slice(c * LANES, (c + 1) * LANES)
            found = jnp.where(edge[:, cut], state[:, cut], found)
        parts.append(found)
    east_at = (TILE * lane + TILE - 1) & (LANES - 1)
    west_at = (TILE * lane) & (LANES - 1)
    east = jnp.where(lane < 64, pick(parts[0], east_at), pick(parts[1], east_at))
    west = jnp.where(lane < 64, pick(parts[0], west_at), pick(parts[1], west_at))
    south = state[:, :LANES]
    before = pltpu.roll(state[:, (CHUNKS - 2) * LANES:(CHUNKS - 1) * LANES], LANES - LAST, 1)
    after = pltpu.roll(state[:, (CHUNKS - 1) * LANES:], LANES - LAST, 1)
    north = jnp.where(lane < LANES - LAST, before, after)
    return [south, east, north, west]


def spread(lines, cell, column):
    south, east, north, west = lines
    lane = lanes()
    odd = (lane & 1) == 1
    line_at = (37 * ((lane + jnp.where(odd, 39, 0)) >> 1)) & 63
    early = jnp.where(odd, pick(east, line_at), pick(west, line_at))
    late = jnp.where(odd, pick(east, line_at + 64), pick(west, line_at + 64))
    sides = jnp.concatenate([early] * HALF + [late] * (CHUNKS - HALF), axis=1)
    edge = (column == 0) | (column == TILE - 1)
    out = jnp.where(edge, sides, 0.0)
    first = jnp.where(lane < TILE, south, 0.0) + out[:, :LANES]
    moved = pltpu.roll(north, LAST, 1)
    before = out[:, (CHUNKS - 2) * LANES:(CHUNKS - 1) * LANES] + jnp.where(lane >= LAST, moved, 0.0)
    after = out[:, (CHUNKS - 1) * LANES:] + jnp.where(lane < LAST + TILE - LANES, moved, 0.0)
    return jnp.concatenate([first, out[:, LANES:(CHUNKS - 2) * LANES], before, after], axis=1)


def neighbours(state):
    cell, column = column_of()
    right = jnp.where(column == TILE - 1, 0.0, pltpu.roll(state, WIDE - 1, 1))
    left = jnp.where(column == 0, 0.0, pltpu.roll(state, 1, 1))
    up = jnp.where(cell >= CELLS - TILE, 0.0, pltpu.roll(state, WIDE - TILE, 1))
    down = jnp.where(cell < TILE, 0.0, pltpu.roll(state, TILE, 1))
    return right, left, up, down, cell, column


def row_of(values):
    return lax.broadcasted_iota(jnp.int32, values.shape, 0)


def repeated(values, first):
    row = row_of(values)
    if first == 0:
        pair = jnp.where(row < 2, values, pltpu.roll(values, 2, 0))
    else:
        pair = jnp.where(row < 4, values, pltpu.roll(values, 2, 0))
        pair = jnp.where(row < 2, pltpu.roll(values, 6, 0), pair)
        return pair
    return jnp.where(row < 4, pair, pltpu.roll(values, 4, 0))


def wet_rows(values):
    return jnp.broadcast_to(values[6:7], values.shape)


def turned(line, turns):
    row = row_of(line)
    swapped = jnp.where(row < 2, pltpu.roll(line, 6, 0), pltpu.roll(line, 2, 0))
    velocity = row < 4
    second = jnp.where(row < 2, swapped, -swapped)
    odd = jnp.where(turns % 2 == 1, 1, 0)
    out = jnp.where(jnp.logical_and(velocity, odd == 1), second, line)
    back = jnp.where(turns >= 2, 1, 0)
    return jnp.where(jnp.logical_and(velocity, back == 1), -out, out)


def flipped(line):
    return pick(line, jnp.maximum(TILE - 1 - lanes(), 0))


ROUTE = 48
OWN_AT, RELAY_AT = TILE, {0: TILE + 4, 2: TILE + 8}


class Rows:
    def __init__(self, ref):
        self.ref = ref

    def __getitem__(self, i):
        return jnp.broadcast_to(self.ref[i:i + 1, :], (8, LANES))


def my_index(ny):
    return lax.axis_index("gx") * ny + lax.axis_index("gy")


def sent_line(line, side, route, vector):
    line = jnp.where(route[32 + side] == 1, flipped(line), line)
    return turned(line, route[36 + side]) if vector else line


def chosen(lines, route, link):
    total = jnp.zeros((8, LANES), jnp.float32)
    for side in range(4):
        total = jnp.where(route[4 * link + side] == 1, lines[side], total)
    return total


def own_rims(sent, route):
    out = []
    for target in range(4):
        total = jnp.zeros((8, LANES), jnp.float32)
        for side in range(4):
            total = jnp.where(route[16 + 4 * side + target] == 1, sent[side], total)
        out.append(total)
    return out


def rims_of(route, base, came):
    out = []
    for side in range(4):
        rim = base[side] if base is not None else jnp.zeros((8, LANES), jnp.float32)
        for link in range(4):
            rim = jnp.where(route[4 * link + side] == 1, came[link], rim)
        out.append(rim)
    return out


def four_of(ref):
    return [ref[8 * side:8 * side + 8, :] for side in range(4)]


def columns_at(step):
    lane = lanes()
    odd = lane & 1
    shift = jnp.where(odd == 1, 39 + step, -step) if step % 2 == 0 else jnp.where(odd == 1, -step, 39 + step)
    column = jnp.where(odd == 1, TILE - 1 - step, step) if step % 2 == 0 else jnp.where(odd == 1, step, TILE - 1 - step)
    line_at = (37 * ((lane + shift) >> 1)) & 63
    return line_at, (TILE * line_at + column) >> 7


def raw_lines(chunk_of, step):
    lane = lanes()
    _, home = columns_at(step)
    parts = []
    for low, high in ((0, HALF), (HALF, CHUNKS)):
        found = chunk_of(low)
        for c in range(low + 1, high):
            found = jnp.where(home == c - low, chunk_of(c), found)
        parts.append(found)
    early = lane < 64
    out = [None] * 4
    for side, column in ((1, TILE - 1 - step), (3, step)):
        at = (TILE * lane + column) & (LANES - 1)
        out[side] = jnp.where(early, pick(parts[0], at), pick(parts[1], at))
    for side, first in ((0, TILE * step), (2, CELLS - TILE - TILE * step)):
        low, start = first // LANES, first % LANES
        if start == 0:
            out[side] = chunk_of(low)
        else:
            before = pltpu.roll(chunk_of(low), LANES - start, 1)
            after = pltpu.roll(chunk_of(low + 1), LANES - start, 1)
            out[side] = jnp.where(lane < LANES - start, before, after)
    return out


def spread_chunks(lines, step):
    lane = lanes()
    line_at, home = columns_at(step)
    odd = (lane & 1) == 1
    first_odd, first_even = (lines[1], lines[3]) if step % 2 == 0 else (lines[3], lines[1])
    early = jnp.where(odd, pick(first_odd, line_at), pick(first_even, line_at))
    late = jnp.where(odd, pick(first_odd, line_at + 64), pick(first_even, line_at + 64))
    out = []
    for c in range(CHUNKS):
        out.append(jnp.where(home == (c if c < HALF else c - HALF), early if c < HALF else late, 0.0))
    for side, first in ((0, TILE * step), (2, CELLS - TILE - TILE * step)):
        low, start = first // LANES, first % LANES
        line = jnp.where(lane < TILE, lines[side], 0.0)
        if start == 0:
            out[low] = out[low] + line
        else:
            moved = pltpu.roll(line, start, 1)
            out[low] = out[low] + jnp.where(lane >= start, moved, 0.0)
            if start + TILE > LANES:
                out[low + 1] = out[low + 1] + jnp.where(lane < start + TILE - LANES, moved, 0.0)
    return out


def load_kernel(shape, tiles_hbm, near_hbm, turn_hbm, fields_ref, wet_ref,
                raw, wet_raw, lines_ref, inner_ref, pay0, pay1, pay2, pay3, route_ref,
                tiles_ref, near_ref, turn_ref, sems):
    nx, ny = shape
    tables = [pltpu.make_async_copy(tiles_hbm, tiles_ref, sems.at[7]),
              pltpu.make_async_copy(near_hbm, near_ref, sems.at[8]),
              pltpu.make_async_copy(turn_hbm, turn_ref, sems.at[9])]
    copies = [pltpu.make_async_copy(fields_ref.at[:, 0], raw.at[0:6], sems.at[0])]
    copies.append(pltpu.make_async_copy(wet_ref.at[0], wet_raw.at[0], sems.at[6]))
    for copy in tables + copies:
        copy.start()
    for copy in tables:
        copy.wait()
    me = my_index(ny)
    route = [None] * ROUTE
    tile = tiles_ref[me]
    live = tile >= 0
    held = jnp.maximum(tile, 0)
    near = [jnp.where(live, near_ref[side, held], -1) for side in range(4)]
    turn = [turn_ref[side, held] for side in range(4)]
    for link in range(4):
        other = tiles_ref[partner(me, link, nx, ny)]
        for side in range(4):
            route[4 * link + side] = jnp.where((near[side] >= 0) & (near[side] == other), 1, 0)
    for side in range(4):
        target = (side + 2 + turn[side]) % 4
        for k in range(4):
            route[16 + 4 * side + k] = jnp.where((near[side] >= 0) & (near[side] == tile) & (target == k), 1, 0)
        route[32 + side] = jnp.where((target < 2) != (side >= 2), 1, 0)
        route[36 + side] = (4 - turn[side]) % 4
    route[40] = jnp.where(live, 1, 0)
    for i in range(41):
        route_ref[i:i + 1, :] = jnp.full((1, LANES), route[i], jnp.int32)
    for copy in copies:
        copy.wait()

    def chunk(ref, c):
        if c < CHUNKS - 1:
            return ref[:, c * LANES:(c + 1) * LANES]
        rest = CELLS - c * LANES
        part = ref[:, c * LANES:CELLS]
        return jnp.concatenate([part, jnp.zeros((8, LANES - rest), part.dtype)], axis=1)

    row, lane = rows(), lanes()
    both = []
    for step, ref in ((0, lines_ref), (1, inner_ref)):
        lines = []
        for value, wet in zip(raw_lines(lambda c: chunk(raw, c), step), raw_lines(lambda c: chunk(wet_raw, c), step)):
            wet = jnp.broadcast_to(wet[0:1], (8, LANES)).astype(jnp.float32)
            lines.append(jnp.where(row < 6, value * wet, jnp.where(row == 6, wet, 0.0)))
        for side in range(4):
            ref[8 * side:8 * side + 8, :] = lines[side]
        both.append(lines)
    ends = [jnp.where((lane == OWN_AT + 1) | (lane == OWN_AT + 2), TILE - 1, 0)] * 2
    corners = jnp.where(lane < OWN_AT + 2, pick(both[0][0], ends[0]), pick(both[0][2], ends[1]))
    at_corners = (lane >= OWN_AT) & (lane < OWN_AT + 4)
    sent = [sent_line(both[0][side], side, route, True) for side in range(4)]
    sent_inner = [sent_line(both[1][side], side, route, False) for side in range(4)]
    for link, pay in zip(BOTH, (pay0, pay1, pay2, pay3)):
        pay[0:8, :] = jnp.where(at_corners, corners, chosen(sent, route, link))
        pay[8:16, :] = chosen(sent_inner, route, link)


def pressure_of(tracer, row):
    return GRAVITY * jnp.where(row == 5, tracer + pltpu.roll(tracer, 1, 0), tracer)


def force_of(state, base, row):
    right, left, up, down, cell, column = neighbours(pressure_of(base, row))
    slope = jnp.where(row < 2, pltpu.roll(right - left, 4, 0), pltpu.roll(up - down, 6, 0))
    swapped = jnp.where(row < 2, pltpu.roll(state, 6, 0), -pltpu.roll(state, 2, 0))
    force = STEP_SIZE * (CORIOLIS * swapped - 0.5 * slope)
    return jnp.where(row < 4, wet_rows(state) * force, 0.0)


def masked_state(raw, wet_raw, state_ref):
    state_ref[:, (CHUNKS - 1) * LANES:] = jnp.zeros((8, LANES), jnp.float32)
    for low, high in ((0, (CHUNKS - 1) * LANES), ((CHUNKS - 1) * LANES, CELLS)):
        size = (8, high - low)
        row = lax.broadcasted_iota(jnp.int32, size, 0)
        wet = jnp.broadcast_to(wet_raw[0:1, low:high].astype(jnp.float32), size)
        state_ref[:, low:high] = jnp.where(row < 6, raw[:, low:high] * wet, jnp.where(row == 6, wet, 0.0))
    return state_ref[...]


def without_rims(state):
    right, left, up, down, cell, column = neighbours(state)
    first, second, wet = repeated(state, 0), repeated(state, 2), wet_rows(state)
    along = first * (right - left) + second * (up - down)
    round_sum = right + left + up + down - 4.0 * state
    return wet * (state - (0.5 * ADVECT) * along + DIFFUSE * round_sum), column


def if_live(route_ref, values):
    return jnp.where(tiled(Rows(route_ref)[40], CHUNKS) == 1, values, 0.0)


def base_kernel(raw, wet_raw, state_ref, base_ref, base_lines_ref):
    state = masked_state(raw, wet_raw, state_ref)
    base, column = without_rims(state)
    base_ref[...] = base
    lines = edge_lines(base, column)
    for side in range(4):
        base_lines_ref[8 * side:8 * side + 8, :] = lines[side]


def inner_kernel(shape, tiles_hbm, near_hbm, turn_hbm, halves_hbm, raw, wet_raw, route_ref,
                 almost_ref, plan_ref, flag, state_ref, tiles_ref, near_ref, turn_ref, halves_ref, table_ref, sems):
    copies = [pltpu.make_async_copy(tiles_hbm, tiles_ref, sems.at[0]),
              pltpu.make_async_copy(near_hbm, near_ref, sems.at[1]),
              pltpu.make_async_copy(turn_hbm, turn_ref, sems.at[2]),
              pltpu.make_async_copy(halves_hbm, halves_ref, sems.at[3]),
              pltpu.make_async_copy(near_hbm, table_ref.at[0:4], sems.at[4])]
    for copy in copies:
        copy.start()
    state = masked_state(raw, wet_raw, state_ref)
    base, _ = without_rims(state)
    almost_ref[...] = base
    for copy in copies:
        copy.wait()
    flag[0] = off_grid(shape, halves_ref, table_ref)
    corner_plan(shape, tiles_ref, near_ref, turn_ref, plan_ref)
    base = almost_ref[...]
    row = lax.broadcasted_iota(jnp.int32, (8, WIDE), 0)
    almost_ref[...] = if_live(route_ref, base + force_of(state_ref[...], base, row))


def off_grid(shape, halves_ref, table_ref):
    nx, ny = shape
    row, lane = rows(), lanes()
    tiles = [jnp.broadcast_to(halves_ref[half:half + 1, :], (8, LANES)) for half in range(2)]
    near = [table_ref[:, half * LANES:(half + 1) * LANES] for half in range(2)]

    def look(table, index):
        return jnp.where(index < LANES, pick(table[0], index & (LANES - 1)), pick(table[1], index & (LANES - 1)))

    worst = jnp.zeros((8, LANES), jnp.int32)
    for half in range(2):
        tile = tiles[half]
        mine = look(near, jnp.maximum(tile, 0))
        linked = (tile >= 0) & (mine >= 0) & (row < 4)
        other = [look(tiles, partner(lane + half * LANES, link, nx, ny)) for link in range(4)]
        over_x = (mine == other[1]) | (mine == other[3])
        kind = jnp.where(linked, jnp.where(mine == tile, 4, jnp.where(over_x, 1, 2)), 0)
        after = jnp.where(row < 3, pltpu.roll(kind, 7, 0), pltpu.roll(kind, 3, 0))
        odd = (kind == 4) | ((kind > 0) & (kind == after) & (row < 4))
        worst = jnp.where(odd, 1, worst)
    return jnp.max(worst)


def corner_plan(shape, tiles_ref, near_ref, turn_ref, plan_ref):
    nx, ny = shape
    me = my_index(ny)
    tile = tiles_ref[me]
    held = jnp.maximum(tile, 0)
    across = [partner(me, link, nx, ny) for link in range(4)]
    relayed = [(which, RELAY_AT[u], tiles_ref[partner(across[x], u, nx, ny)])
               for which, x in ((1, 1), (2, 3)) for u in (0, 2)]
    for link in range(4):
        other = tiles_ref[across[link]]
        side = jnp.int32(-1)
        for k in range(4):
            side = jnp.where((tile >= 0) & (other >= 0) & (near_ref[k, held] == other), k, side)
        facing = (side + 2 + turn_ref[jnp.maximum(side, 0), held]) % 4
        there = jnp.maximum(other, 0)
        for end in range(2):
            later = (side < 2) == (end == 0)
            lateral = jnp.where(later, facing + 1, facing + 3) % 4
            beyond = jnp.where(side >= 0, near_ref[lateral, there], -1)
            back = (lateral + 2 + turn_ref[lateral, there]) % 4
            corner = jnp.where(later, back + 1, back) % 4
            buffer, lane = jnp.int32(0), jnp.int32(0)
            for which, base, name in relayed:
                here = (beyond >= 0) & (beyond == name)
                buffer, lane = jnp.where(here, which, buffer), jnp.where(here, base + corner, lane)
            at = 2 * (2 * link + end)
            plan_ref[at:at + 1, :] = jnp.full((1, LANES), buffer, jnp.int32)
            plan_ref[at + 1:at + 2, :] = jnp.full((1, LANES), lane, jnp.int32)


def relay_kernel(pay0, pay1, came0, came1, after, out0, out1):
    lane = lanes()
    for pay, out in ((pay0, out0), (pay1, out1)):
        line = pay[0:8, :]
        for link, came in zip(U_ORDER, (came0, came1)):
            moved = pltpu.roll(came[0:8, :], RELAY_AT[link] - OWN_AT, 1)
            line = jnp.where((lane >= RELAY_AT[link]) & (lane < RELAY_AT[link] + 4), moved, line)
        out[0:8, :] = line
        out[8:16, :] = pay[8:16, :]


def edge_patches(lines, rims):
    patch = []
    for side in range(4):
        drift = repeated(lines[side], 0 if side % 2 == 1 else 2)
        sign = 1.0 if side in (1, 2) else -1.0
        patch.append(wet_rows(lines[side]) * (DIFFUSE - (sign * 0.5 * ADVECT) * drift) * rims[side])
    return patch


def with_ends(patch):
    south, east, north, west = patch
    end = TILE - 1
    return [
        south + at_ends(west, 0, 0) + at_ends(east, 0, end),
        east + at_ends(south, end, 0) + at_ends(north, end, end),
        north + at_ends(west, end, 0) + at_ends(east, end, end),
        west + at_ends(south, 0, 0) + at_ends(north, 0, end),
    ]


def final_kernel(route_ref, plan_ref, lines_ref, inner_ref, almost_ref, first, second, third, fourth, out_ref, full, sems):
    lane, row = lanes(), rows()
    route, plan = Rows(route_ref), Rows(plan_ref)
    came = by_link((first, second, third, fourth), BOTH)
    outer = []
    for link in range(4):
        line = came[link][0:8, :]
        for end, lane_to in ((0, LANES - 1), (1, TILE)):
            which, lane_from = plan[2 * (2 * link + end)], plan[2 * (2 * link + end) + 1]
            held = jnp.where(which == 2, came[3][0:8, :], came[1][0:8, :])
            value = pick(held, lane_from)
            line = jnp.where(lane == lane_to, jnp.where(which > 0, value, 0.0), line)
        outer.append(line)
    rims = rims_of(route, None, outer)
    beyond = rims_of(route, None, [came[link][8:16, :] for link in range(4)])
    lines, inner = four_of(lines_ref), four_of(inner_ref)
    patch = edge_patches(lines, rims)
    whole = with_ends(patch)
    on_edge, inside = [], []
    for side in range(4):
        sign = 1.0 if side in (1, 2) else -1.0
        line, wet, wet_in = rims[side], wet_rows(lines[side]), wet_rows(inner[side])
        after, before = pltpu.roll(line, LANES - 1, 1), pltpu.roll(line, 1, 1)
        first, second = pltpu.roll(line, 4, 0), pltpu.roll(line, 2, 0)
        normal, tangent = (first, second) if side % 2 == 1 else (second, first)
        along = normal * (sign * (beyond[side] - lines[side])) + tangent * (after - before)
        round_sum = after + before + beyond[side] + lines[side] - 4.0 * line
        tracer = wet_rows(line) * (line - (0.5 * ADVECT) * along + DIFFUSE * round_sum)
        far = pressure_of(tracer, row)
        mine = jnp.where(lane < TILE, pressure_of(whole[side], row), 0.0)
        drop = pltpu.roll(mine, LANES - 1, 1) - pltpu.roll(mine, 1, 1)
        to_normal, to_tangent = (4, 6) if side % 2 == 1 else (6, 4)
        own_row = row < 2 if side % 2 == 1 else (row >= 2) & (row < 4)
        cross_row = (row >= 2) & (row < 4) if side % 2 == 1 else row < 2
        push = jnp.where(own_row, sign * pltpu.roll(far, to_normal, 0), 0.0)
        push = jnp.where(cross_row, pltpu.roll(drop, to_tangent, 0), push)
        on_edge.append(patch[side] - (0.5 * STEP_SIZE) * wet * push)
        kept = own_row & (lane > 0) & (lane < TILE - 1)
        inside.append(jnp.where(kept, (-sign * 0.5 * STEP_SIZE) * wet_in * pltpu.roll(mine, to_normal, 0), 0.0))
    edges, seconds = spread_chunks(on_edge, 0), spread_chunks(inside, 1)
    copies = []
    for low, high in ((0, 24), (24, CHUNKS)):
        for c in range(low, high):
            cut = slice(c * LANES, min((c + 1) * LANES, CELLS))
            width = cut.stop - cut.start
            full[:, cut] = (almost_ref[:, c * LANES:(c + 1) * LANES] + (edges[c] + seconds[c]))[:, :width]
        cells = pl.ds(low * LANES, min(high * LANES, CELLS) - low * LANES)
        copies.append(pltpu.make_async_copy(full.at[0:6, cells], out_ref.at[:, 0, cells], sems.at[len(copies)]))
        copies[-1].start()
    for copy in copies:
        copy.wait()


def write_out(full, out_ref, sems):
    copies = [pltpu.make_async_copy(full.at[c], out_ref.at[c, 0], sems.at[c]) for c in range(6)]
    for copy in copies:
        copy.start()
    for copy in copies:
        copy.wait()


def at_ends(line, lane_from, lane_to):
    value = jnp.broadcast_to(line[:, lane_from:lane_from + 1], (8, LANES))
    return jnp.where(lanes() == lane_to, value, 0.0)


def edge_kernel(route_ref, lines_ref, base_lines_ref, came0, came1, came2, came3,
                patch_ref, own_two_ref, pay0, pay1, pay2, pay3):
    route = Rows(route_ref)
    lines, base = four_of(lines_ref), four_of(base_lines_ref)
    own = own_rims([sent_line(lines[side], side, route, True) for side in range(4)], route)
    rims = rims_of(route, own, [came[0:8, :] for came in by_link((came0, came1, came2, came3), BOTH)])
    patch = edge_patches(lines, rims)
    whole = with_ends(patch)
    press = []
    for side in range(4):
        patch_ref[8 * side:8 * side + 8, :] = patch[side]
        press.append(sent_line(pressure_of(base[side] + whole[side], rows()), side, route, False))
    for link, pay in zip(SECOND_ORDER, (pay0, pay1, pay2, pay3)):
        pay[...] = chosen(press, route, link)
    own = own_rims(press, route)
    for side in range(4):
        own_two_ref[8 * side:8 * side + 8, :] = own[side]


def middle_kernel(route_ref, state_ref, base_ref, patch_ref, out_ref):
    state = state_ref[...]
    cell, column = column_of()
    base = base_ref[...] + spread(four_of(patch_ref), cell, column)
    row = lax.broadcasted_iota(jnp.int32, (8, WIDE), 0)
    out_ref[...] = if_live(route_ref, base + force_of(state, base, row))


def last_kernel(route_ref, lines_ref, own_ref, almost_ref, came0, came1, came2, came3, out_ref, full, sems):
    route = Rows(route_ref)
    rims = rims_of(route, four_of(own_ref), [came[...] for came in by_link((came0, came1, came2, came3), SECOND_ORDER)])
    patch = []
    for side in range(4):
        wet = wet_rows(lines_ref[8 * side:8 * side + 8, :])
        row = rows()
        rim = pltpu.roll(rims[side], 4 if side % 2 == 1 else 6, 0)
        mine = row < 2 if side % 2 == 1 else (row >= 2) & (row < 4)
        sign = -1.0 if side in (1, 2) else 1.0
        patch.append(jnp.where(mine, (sign * 0.5 * STEP_SIZE) * wet * rim, 0.0))
    cell, column = column_of()
    full[...] = (almost_ref[...] + spread(patch, cell, column))[:, :CELLS]
    write_out(full, out_ref, sems)


def sds(*shape, dtype=jnp.float32):
    return jax.ShapeDtypeStruct(shape, dtype)


PARAMS = pltpu.CompilerParams(vmem_limit_bytes=16 * 1024 * 1024)


def on_device(nx, ny, fields, wet_mask, tile_of_slot, neighbor, rotation):
    line, pair, four, wide = sds(8, LANES), sds(16, LANES), sds(32, LANES), sds(8, WIDE)
    scalars = pltpu.SMEM((4, nx * ny), jnp.int32)
    tables = [pltpu.with_memory_space_constraint(v, pltpu.HBM) for v in (tile_of_slot, neighbor.T, rotation.T)]
    inputs = [pltpu.with_memory_space_constraint(v, pltpu.HBM) for v in (fields.reshape(6, 1, CELLS), wet_mask)]
    halves = pltpu.with_memory_space_constraint(tile_of_slot.reshape(2, LANES), pltpu.HBM)
    raw, wet_raw, lines, inner, *pays, route = pl.pallas_call(
        lambda *refs: load_kernel((nx, ny), *refs),
        out_shape=[sds(8, CELLS), sds(8, CELLS, dtype=jnp.int32), four, four, pair, pair, pair, pair,
                   sds(ROUTE, LANES, dtype=jnp.int32)],
        in_specs=[HBM] * 5,
        out_specs=[VMEM] * 9,
        scratch_shapes=[pltpu.SMEM((nx * ny,), jnp.int32), scalars, scalars, pltpu.SemaphoreType.DMA((12,))],
        compiler_params=PARAMS, name="load",
    )(*tables, *inputs)
    came_u = exchanged(pays[:2], U_ORDER, nx, ny)
    almost, plan, flag = pl.pallas_call(
        lambda *refs: inner_kernel((nx, ny), *refs),
        out_shape=[wide, sds(16, LANES, dtype=jnp.int32), sds(1, dtype=jnp.int32)],
        in_specs=[HBM] * 4 + [VMEM] * 3, out_specs=[VMEM, VMEM, SMEM],
        scratch_shapes=[pltpu.VMEM((8, WIDE), jnp.float32), pltpu.SMEM((nx * ny,), jnp.int32), scalars, scalars,
                        pltpu.VMEM((2, LANES), jnp.int32), pltpu.VMEM((8, nx * ny), jnp.int32),
                        pltpu.SemaphoreType.DMA((5,))],
        compiler_params=PARAMS, name="inner",
        cost_estimate=pl.CostEstimate(flops=2000000, bytes_accessed=800000, transcendentals=0),
    )(*tables, halves, raw, wet_raw, route)
    sent = pl.pallas_call(
        relay_kernel, out_shape=[pair, pair], in_specs=[VMEM] * 4 + [ANY], out_specs=[VMEM] * 2,
        compiler_params=PARAMS, name="relay",
    )(*pays[2:], *came_u, almost)
    came_x = exchanged(sent, X_ORDER, nx, ny)
    result = pltpu.HBM((6, 1, CELLS), jnp.float32)
    writing = [pltpu.VMEM((8, CELLS), jnp.float32), pltpu.SemaphoreType.DMA((12,))]

    def grid_like():
        return pl.pallas_call(
            final_kernel, out_shape=result, in_specs=[VMEM] * 9, out_specs=HBM,
            scratch_shapes=writing, compiler_params=PARAMS, name="final",
        )(route, plan, lines, inner, almost, *came_u, *came_x)

    def general():
        came = came_u + came_x
        state, base, base_lines = pl.pallas_call(
            base_kernel, out_shape=[wide, wide, four], in_specs=[VMEM] * 2, out_specs=[VMEM] * 3,
            compiler_params=PARAMS, name="base",
            cost_estimate=pl.CostEstimate(flops=2000000, bytes_accessed=800000, transcendentals=0),
        )(raw, wet_raw)
        patch, own_two, *press = pl.pallas_call(
            edge_kernel, out_shape=[four, four, line, line, line, line],
            in_specs=[VMEM] * 7, out_specs=[VMEM] * 6,
            compiler_params=PARAMS, name="edge",
        )(route, lines, base_lines, *came)
        came_two = exchanged(press, SECOND_ORDER, nx, ny)
        nearly = pl.pallas_call(
            middle_kernel, out_shape=wide, in_specs=[VMEM] * 4, out_specs=VMEM,
            compiler_params=PARAMS, name="middle",
            cost_estimate=pl.CostEstimate(flops=2000000, bytes_accessed=800000, transcendentals=0),
        )(route, state, base, patch)
        return pl.pallas_call(
            last_kernel, out_shape=result, in_specs=[VMEM] * 8, out_specs=HBM,
            scratch_shapes=writing, compiler_params=PARAMS, name="last",
        )(route, lines, own_two, nearly, *came_two)

    out = lax.switch(flag[0], [grid_like, general])
    return out.reshape(1, 6, CELLS)


def solution(mesh):
    nx, ny = mesh.shape["gx"], mesh.shape["gy"]
    in_specs = (P(AXES, None, None), P(AXES, None), P(), P(), P())
    return jax.shard_map(lambda *args: on_device(nx, ny, *args), mesh=mesh, in_specs=in_specs,
                         out_specs=P(AXES, None, None), check_vma=False)
```

```python
import jax
import jax.numpy as jnp
from jax import lax
from jax.experimental import pallas as pl
from jax.experimental.pallas import tpu as pltpu
from jax.sharding import PartitionSpec as P

TILE = 90
CELLS = TILE * TILE
LANES = 128
CHUNKS = 64
WIDE = LANES * CHUNKS
HALF = 45
LAST = CELLS - TILE - (CHUNKS - 2) * LANES

ADVECT = 0.25
DIFFUSE = 0.15
STEP_SIZE = 0.5
CORIOLIS = 0.3
GRAVITY = 0.8

AXES = ("gx", "gy")
VMEM = pl.BlockSpec(memory_space=pltpu.VMEM)
SMEM = pl.BlockSpec(memory_space=pltpu.SMEM)
ANY = pl.BlockSpec(memory_space=pl.ANY)
HBM = pl.BlockSpec(memory_space=pltpu.HBM)


def link_x_even(x, y, nx, ny):
    return x ^ 1, y


def link_x_odd(x, y, nx, ny):
    return (((x + nx - 1) % nx ^ 1) + 1) % nx, y


def link_y_even(x, y, nx, ny):
    return x, y ^ 1


def link_y_odd(x, y, nx, ny):
    if y == 0 or y == ny - 1:
        return (x + nx // 2) % nx, y
    return x, ((y - 1) ^ 1) + 1


def swapped(x, nx):
    return (x % (nx // 2) == 0) | (x % (nx // 2) == 2)


def link_u_first(x, y, nx, ny):
    return (link_y_even if swapped(x, nx) else link_y_odd)(x, y, nx, ny)


def link_u_second(x, y, nx, ny):
    return (link_y_odd if swapped(x, nx) else link_y_even)(x, y, nx, ny)


LINKS = (link_u_first, link_x_even, link_u_second, link_x_odd)


def pairs_of(link, nx, ny):
    out = []
    for x in range(nx):
        for y in range(ny):
            to_x, to_y = link(x, y, nx, ny)
            out.append((x * ny + y, to_x * ny + to_y))
    return out


U_ORDER = (0, 2)
X_ORDER = (3, 1)
BOTH = U_ORDER + X_ORDER
SECOND_ORDER = (2, 0, 3, 1)


def exchanged(pays, order, nx, ny):
    return [lax.ppermute(pay, AXES, pairs_of(LINKS[link], nx, ny)) for pay, link in zip(pays, order)]


def by_link(refs, order, links=(0, 1, 2, 3)):
    return [refs[order.index(link)] for link in links]


def partner(me, which, nx, ny):
    x, y = me // ny, me % ny
    if which == 1:
        return me + jnp.where(x % 2 == 0, ny, -ny)
    if which == 3:
        return (x + jnp.where(x % 2 == 1, 1, nx - 1)) % nx * ny + y
    even = me + jnp.where(y % 2 == 0, 1, -1)
    pole = (y == 0) | (y == ny - 1)
    odd = jnp.where(pole, (x + nx // 2) % nx * ny + y, me + jnp.where(y % 2 == 1, 1, -1))
    return jnp.where(swapped(x, nx), even, odd) if which == 0 else jnp.where(swapped(x, nx), odd, even)


def lanes():
    return lax.broadcasted_iota(jnp.int32, (8, LANES), 1)


def rows():
    return lax.broadcasted_iota(jnp.int32, (8, LANES), 0)


def pick(values, index):
    return jnp.take_along_axis(values, index, axis=1)


def tiled(values, count):
    return jnp.concatenate([values] * count, axis=1)


def column_of():
    cell = lax.broadcasted_iota(jnp.int32, (8, WIDE), 1)
    line = jnp.floor((cell.astype(jnp.float32) + 0.5) * (1.0 / TILE)).astype(jnp.int32)
    return cell, cell - TILE * line


def edge_lines(state, column):
    lane = lanes()
    edge = (column == 0) | (column == TILE - 1)
    parts = []
    for low, high in ((0, HALF), (HALF, CHUNKS)):
        found = jnp.zeros((8, LANES), jnp.float32)
        for c in range(low, high):
            cut = slice(c * LANES, (c + 1) * LANES)
            found = jnp.where(edge[:, cut], state[:, cut], found)
        parts.append(found)
    east_at = (TILE * lane + TILE - 1) & (LANES - 1)
    west_at = (TILE * lane) & (LANES - 1)
    east = jnp.where(lane < 64, pick(parts[0], east_at), pick(parts[1], east_at))
    west = jnp.where(lane < 64, pick(parts[0], west_at), pick(parts[1], west_at))
    south = state[:, :LANES]
    before = pltpu.roll(state[:, (CHUNKS - 2) * LANES:(CHUNKS - 1) * LANES], LANES - LAST, 1)
    after = pltpu.roll(state[:, (CHUNKS - 1) * LANES:], LANES - LAST, 1)
    north = jnp.where(lane < LANES - LAST, before, after)
    return [south, east, north, west]


def spread(lines, cell, column):
    south, east, north, west = lines
    lane = lanes()
    odd = (lane & 1) == 1
    line_at = (37 * ((lane + jnp.where(odd, 39, 0)) >> 1)) & 63
    early = jnp.where(odd, pick(east, line_at), pick(west, line_at))
    late = jnp.where(odd, pick(east, line_at + 64), pick(west, line_at + 64))
    sides = jnp.concatenate([early] * HALF + [late] * (CHUNKS - HALF), axis=1)
    edge = (column == 0) | (column == TILE - 1)
    out = jnp.where(edge, sides, 0.0)
    first = jnp.where(lane < TILE, south, 0.0) + out[:, :LANES]
    moved = pltpu.roll(north, LAST, 1)
    before = out[:, (CHUNKS - 2) * LANES:(CHUNKS - 1) * LANES] + jnp.where(lane >= LAST, moved, 0.0)
    after = out[:, (CHUNKS - 1) * LANES:] + jnp.where(lane < LAST + TILE - LANES, moved, 0.0)
    return jnp.concatenate([first, out[:, LANES:(CHUNKS - 2) * LANES], before, after], axis=1)


def neighbours(state):
    cell, column = column_of()
    right = jnp.where(column == TILE - 1, 0.0, pltpu.roll(state, WIDE - 1, 1))
    left = jnp.where(column == 0, 0.0, pltpu.roll(state, 1, 1))
    up = jnp.where(cell >= CELLS - TILE, 0.0, pltpu.roll(state, WIDE - TILE, 1))
    down = jnp.where(cell < TILE, 0.0, pltpu.roll(state, TILE, 1))
    return right, left, up, down, cell, column


def row_of(values):
    return lax.broadcasted_iota(jnp.int32, values.shape, 0)


def repeated(values, first):
    row = row_of(values)
    if first == 0:
        pair = jnp.where(row < 2, values, pltpu.roll(values, 2, 0))
    else:
        pair = jnp.where(row < 4, values, pltpu.roll(values, 2, 0))
        pair = jnp.where(row < 2, pltpu.roll(values, 6, 0), pair)
        return pair
    return jnp.where(row < 4, pair, pltpu.roll(values, 4, 0))


def wet_rows(values):
    return jnp.broadcast_to(values[6:7], values.shape)


def turned(line, turns):
    row = row_of(line)
    swapped = jnp.where(row < 2, pltpu.roll(line, 6, 0), pltpu.roll(line, 2, 0))
    velocity = row < 4
    second = jnp.where(row < 2, swapped, -swapped)
    odd = jnp.where(turns % 2 == 1, 1, 0)
    out = jnp.where(jnp.logical_and(velocity, odd == 1), second, line)
    back = jnp.where(turns >= 2, 1, 0)
    return jnp.where(jnp.logical_and(velocity, back == 1), -out, out)


def flipped(line):
    return pick(line, jnp.maximum(TILE - 1 - lanes(), 0))


ROUTE = 48
OWN_AT, RELAY_AT = TILE, {0: TILE + 4, 2: TILE + 8}


class Rows:
    def __init__(self, ref):
        self.ref = ref

    def __getitem__(self, i):
        return jnp.broadcast_to(self.ref[i:i + 1, :], (8, LANES))


def my_index(ny):
    return lax.axis_index("gx") * ny + lax.axis_index("gy")


def sent_line(line, side, route, vector):
    line = jnp.where(route[32 + side] == 1, flipped(line), line)
    return turned(line, route[36 + side]) if vector else line


def chosen(lines, route, link):
    total = jnp.zeros((8, LANES), jnp.float32)
    for side in range(4):
        total = jnp.where(route[4 * link + side] == 1, lines[side], total)
    return total


def own_rims(sent, route):
    out = []
    for target in range(4):
        total = jnp.zeros((8, LANES), jnp.float32)
        for side in range(4):
            total = jnp.where(route[16 + 4 * side + target] == 1, sent[side], total)
        out.append(total)
    return out


def rims_of(route, base, came):
    out = []
    for side in range(4):
        rim = base[side] if base is not None else jnp.zeros((8, LANES), jnp.float32)
        for link in range(4):
            rim = jnp.where(route[4 * link + side] == 1, came[link], rim)
        out.append(rim)
    return out


def four_of(ref):
    return [ref[8 * side:8 * side + 8, :] for side in range(4)]


def columns_at(step):
    lane = lanes()
    odd = lane & 1
    shift = jnp.where(odd == 1, 39 + step, -step) if step % 2 == 0 else jnp.where(odd == 1, -step, 39 + step)
    column = jnp.where(odd == 1, TILE - 1 - step, step) if step % 2 == 0 else jnp.where(odd == 1, step, TILE - 1 - step)
    line_at = (37 * ((lane + shift) >> 1)) & 63
    return line_at, (TILE * line_at + column) >> 7


def raw_lines(chunk_of, step):
    lane = lanes()
    _, home = columns_at(step)
    parts = []
    for low, high in ((0, HALF), (HALF, CHUNKS)):
        found = chunk_of(low)
        for c in range(low + 1, high):
            found = jnp.where(home == c - low, chunk_of(c), found)
        parts.append(found)
    early = lane < 64
    out = [None] * 4
    for side, column in ((1, TILE - 1 - step), (3, step)):
        at = (TILE * lane + column) & (LANES - 1)
        out[side] = jnp.where(early, pick(parts[0], at), pick(parts[1], at))
    for side, first in ((0, TILE * step), (2, CELLS - TILE - TILE * step)):
        low, start = first // LANES, first % LANES
        if start == 0:
            out[side] = chunk_of(low)
        else:
            before = pltpu.roll(chunk_of(low), LANES - start, 1)
            after = pltpu.roll(chunk_of(low + 1), LANES - start, 1)
            out[side] = jnp.where(lane < LANES - start, before, after)
    return out


def spread_chunks(lines, step):
    lane = lanes()
    line_at, home = columns_at(step)
    odd = (lane & 1) == 1
    first_odd, first_even = (lines[1], lines[3]) if step % 2 == 0 else (lines[3], lines[1])
    early = jnp.where(odd, pick(first_odd, line_at), pick(first_even, line_at))
    late = jnp.where(odd, pick(first_odd, line_at + 64), pick(first_even, line_at + 64))
    out = []
    for c in range(CHUNKS):
        out.append(jnp.where(home == (c if c < HALF else c - HALF), early if c < HALF else late, 0.0))
    for side, first in ((0, TILE * step), (2, CELLS - TILE - TILE * step)):
        low, start = first // LANES, first % LANES
        line = jnp.where(lane < TILE, lines[side], 0.0)
        if start == 0:
            out[low] = out[low] + line
        else:
            moved = pltpu.roll(line, start, 1)
            out[low] = out[low] + jnp.where(lane >= start, moved, 0.0)
            if start + TILE > LANES:
                out[low + 1] = out[low + 1] + jnp.where(lane < start + TILE - LANES, moved, 0.0)
    return out


def load_kernel(shape, tiles_hbm, near_hbm, turn_hbm, fields_ref, wet_ref,
                raw, wet_raw, lines_ref, inner_ref, pay0, pay1, pay2, pay3, route_ref,
                tiles_ref, near_ref, turn_ref, sems):
    nx, ny = shape
    tables = [pltpu.make_async_copy(tiles_hbm, tiles_ref, sems.at[7]),
              pltpu.make_async_copy(near_hbm, near_ref, sems.at[8]),
              pltpu.make_async_copy(turn_hbm, turn_ref, sems.at[9])]
    copies = [pltpu.make_async_copy(fields_ref.at[:, 0], raw.at[0:6], sems.at[0])]
    copies.append(pltpu.make_async_copy(wet_ref.at[0], wet_raw.at[0], sems.at[6]))
    for copy in tables + copies:
        copy.start()
    for copy in tables:
        copy.wait()
    me = my_index(ny)
    route = [None] * ROUTE
    tile = tiles_ref[me]
    live = tile >= 0
    held = jnp.maximum(tile, 0)
    near = [jnp.where(live, near_ref[side, held], -1) for side in range(4)]
    turn = [turn_ref[side, held] for side in range(4)]
    for link in range(4):
        other = tiles_ref[partner(me, link, nx, ny)]
        for side in range(4):
            route[4 * link + side] = jnp.where((near[side] >= 0) & (near[side] == other), 1, 0)
    for side in range(4):
        target = (side + 2 + turn[side]) % 4
        for k in range(4):
            route[16 + 4 * side + k] = jnp.where((near[side] >= 0) & (near[side] == tile) & (target == k), 1, 0)
        route[32 + side] = jnp.where((target < 2) != (side >= 2), 1, 0)
        route[36 + side] = (4 - turn[side]) % 4
    route[40] = jnp.where(live, 1, 0)
    for i in range(41):
        route_ref[i:i + 1, :] = jnp.full((1, LANES), route[i], jnp.int32)
    for copy in copies:
        copy.wait()

    def chunk(ref, c):
        if c < CHUNKS - 1:
            return ref[:, c * LANES:(c + 1) * LANES]
        rest = CELLS - c * LANES
        part = ref[:, c * LANES:CELLS]
        return jnp.concatenate([part, jnp.zeros((8, LANES - rest), part.dtype)], axis=1)

    row, lane = rows(), lanes()
    both = []
    for step, ref in ((0, lines_ref), (1, inner_ref)):
        lines = []
        for value, wet in zip(raw_lines(lambda c: chunk(raw, c), step), raw_lines(lambda c: chunk(wet_raw, c), step)):
            wet = jnp.broadcast_to(wet[0:1], (8, LANES)).astype(jnp.float32)
            lines.append(jnp.where(row < 6, value * wet, jnp.where(row == 6, wet, 0.0)))
        for side in range(4):
            ref[8 * side:8 * side + 8, :] = lines[side]
        both.append(lines)
    ends = [jnp.where((lane == OWN_AT + 1) | (lane == OWN_AT + 2), TILE - 1, 0)] * 2
    corners = jnp.where(lane < OWN_AT + 2, pick(both[0][0], ends[0]), pick(both[0][2], ends[1]))
    at_corners = (lane >= OWN_AT) & (lane < OWN_AT + 4)
    sent = [sent_line(both[0][side], side, route, True) for side in range(4)]
    sent_inner = [sent_line(both[1][side], side, route, False) for side in range(4)]
    for link, pay in zip(BOTH, (pay0, pay1, pay2, pay3)):
        pay[0:8, :] = jnp.where(at_corners, corners, chosen(sent, route, link))
        pay[8:16, :] = chosen(sent_inner, route, link)


def pressure_of(tracer, row):
    return GRAVITY * jnp.where(row == 5, tracer + pltpu.roll(tracer, 1, 0), tracer)


def force_of(state, base, row):
    right, left, up, down, cell, column = neighbours(pressure_of(base, row))
    slope = jnp.where(row < 2, pltpu.roll(right - left, 4, 0), pltpu.roll(up - down, 6, 0))
    swapped = jnp.where(row < 2, pltpu.roll(state, 6, 0), -pltpu.roll(state, 2, 0))
    force = STEP_SIZE * (CORIOLIS * swapped - 0.5 * slope)
    return jnp.where(row < 4, wet_rows(state) * force, 0.0)


def masked_state(raw, wet_raw, state_ref):
    state_ref[:, (CHUNKS - 1) * LANES:] = jnp.zeros((8, LANES), jnp.float32)
    for low, high in ((0, (CHUNKS - 1) * LANES), ((CHUNKS - 1) * LANES, CELLS)):
        size = (8, high - low)
        row = lax.broadcasted_iota(jnp.int32, size, 0)
        wet = jnp.broadcast_to(wet_raw[0:1, low:high].astype(jnp.float32), size)
        state_ref[:, low:high] = jnp.where(row < 6, raw[:, low:high] * wet, jnp.where(row == 6, wet, 0.0))
    return state_ref[...]


def without_rims(state):
    right, left, up, down, cell, column = neighbours(state)
    first, second, wet = repeated(state, 0), repeated(state, 2), wet_rows(state)
    along = first * (right - left) + second * (up - down)
    round_sum = right + left + up + down - 4.0 * state
    return wet * (state - (0.5 * ADVECT) * along + DIFFUSE * round_sum), column


def if_live(route_ref, values):
    return jnp.where(tiled(Rows(route_ref)[40], CHUNKS) == 1, values, 0.0)


def base_kernel(raw, wet_raw, state_ref, base_ref, base_lines_ref):
    state = masked_state(raw, wet_raw, state_ref)
    base, column = without_rims(state)
    base_ref[...] = base
    lines = edge_lines(base, column)
    for side in range(4):
        base_lines_ref[8 * side:8 * side + 8, :] = lines[side]


def inner_kernel(shape, tiles_hbm, near_hbm, turn_hbm, halves_hbm, raw, wet_raw, route_ref,
                 almost_ref, plan_ref, flag, state_ref, tiles_ref, near_ref, turn_ref, halves_ref, table_ref, sems):
    copies = [pltpu.make_async_copy(tiles_hbm, tiles_ref, sems.at[0]),
              pltpu.make_async_copy(near_hbm, near_ref, sems.at[1]),
              pltpu.make_async_copy(turn_hbm, turn_ref, sems.at[2]),
              pltpu.make_async_copy(halves_hbm, halves_ref, sems.at[3]),
              pltpu.make_async_copy(near_hbm, table_ref.at[0:4], sems.at[4])]
    for copy in copies:
        copy.start()
    state = masked_state(raw, wet_raw, state_ref)
    base, _ = without_rims(state)
    almost_ref[...] = base
    for copy in copies:
        copy.wait()
    flag[0] = off_grid(shape, halves_ref, table_ref)
    corner_plan(shape, tiles_ref, near_ref, turn_ref, plan_ref)
    base = almost_ref[...]
    row = lax.broadcasted_iota(jnp.int32, (8, WIDE), 0)
    almost_ref[...] = if_live(route_ref, base + force_of(state_ref[...], base, row))


def off_grid(shape, halves_ref, table_ref):
    nx, ny = shape
    row, lane = rows(), lanes()
    tiles = [jnp.broadcast_to(halves_ref[half:half + 1, :], (8, LANES)) for half in range(2)]
    near = [table_ref[:, half * LANES:(half + 1) * LANES] for half in range(2)]

    def look(table, index):
        return jnp.where(index < LANES, pick(table[0], index & (LANES - 1)), pick(table[1], index & (LANES - 1)))

    worst = jnp.zeros((8, LANES), jnp.int32)
    for half in range(2):
        tile = tiles[half]
        mine = look(near, jnp.maximum(tile, 0))
        linked = (tile >= 0) & (mine >= 0) & (row < 4)
        other = [look(tiles, partner(lane + half * LANES, link, nx, ny)) for link in range(4)]
        over_x = (mine == other[1]) | (mine == other[3])
        kind = jnp.where(linked, jnp.where(mine == tile, 4, jnp.where(over_x, 1, 2)), 0)
        after = jnp.where(row < 3, pltpu.roll(kind, 7, 0), pltpu.roll(kind, 3, 0))
        odd = (kind == 4) | ((kind > 0) & (kind == after) & (row < 4))
        worst = jnp.where(odd, 1, worst)
    return jnp.max(worst)


def corner_plan(shape, tiles_ref, near_ref, turn_ref, plan_ref):
    nx, ny = shape
    me = my_index(ny)
    tile = tiles_ref[me]
    held = jnp.maximum(tile, 0)
    across = [partner(me, link, nx, ny) for link in range(4)]
    relayed = [(which, RELAY_AT[u], tiles_ref[partner(across[x], u, nx, ny)])
               for which, x in ((1, 1), (2, 3)) for u in (0, 2)]
    for link in range(4):
        other = tiles_ref[across[link]]
        side = jnp.int32(-1)
        for k in range(4):
            side = jnp.where((tile >= 0) & (other >= 0) & (near_ref[k, held] == other), k, side)
        facing = (side + 2 + turn_ref[jnp.maximum(side, 0), held]) % 4
        there = jnp.maximum(other, 0)
        for end in range(2):
            later = (side < 2) == (end == 0)
            lateral = jnp.where(later, facing + 1, facing + 3) % 4
            beyond = jnp.where(side >= 0, near_ref[lateral, there], -1)
            back = (lateral + 2 + turn_ref[lateral, there]) % 4
            corner = jnp.where(later, back + 1, back) % 4
            buffer, lane = jnp.int32(0), jnp.int32(0)
            for which, base, name in relayed:
                here = (beyond >= 0) & (beyond == name)
                buffer, lane = jnp.where(here, which, buffer), jnp.where(here, base + corner, lane)
            at = 2 * (2 * link + end)
            plan_ref[at:at + 1, :] = jnp.full((1, LANES), buffer, jnp.int32)
            plan_ref[at + 1:at + 2, :] = jnp.full((1, LANES), lane, jnp.int32)


def relay_kernel(pay0, pay1, came0, came1, after, out0, out1):
    lane = lanes()
    for pay, out in ((pay0, out0), (pay1, out1)):
        line = pay[0:8, :]
        for link, came in zip(U_ORDER, (came0, came1)):
            moved = pltpu.roll(came[0:8, :], RELAY_AT[link] - OWN_AT, 1)
            line = jnp.where((lane >= RELAY_AT[link]) & (lane < RELAY_AT[link] + 4), moved, line)
        out[0:8, :] = line
        out[8:16, :] = pay[8:16, :]


def edge_patches(lines, rims):
    patch = []
    for side in range(4):
        drift = repeated(lines[side], 0 if side % 2 == 1 else 2)
        sign = 1.0 if side in (1, 2) else -1.0
        patch.append(wet_rows(lines[side]) * (DIFFUSE - (sign * 0.5 * ADVECT) * drift) * rims[side])
    return patch


def with_ends(patch):
    south, east, north, west = patch
    end = TILE - 1
    return [
        south + at_ends(west, 0, 0) + at_ends(east, 0, end),
        east + at_ends(south, end, 0) + at_ends(north, end, end),
        north + at_ends(west, end, 0) + at_ends(east, end, end),
        west + at_ends(south, 0, 0) + at_ends(north, 0, end),
    ]


def pressure_at(tracer, shift, row):
    return GRAVITY * (pltpu.roll(tracer, shift, 0)
                      + jnp.where(row == (5 + shift) % 8, pltpu.roll(tracer, shift + 1, 0), 0.0))


def final_kernel(route_ref, plan_ref, lines_ref, inner_ref, almost_ref, first, second, third, fourth, out_ref, full, sems):
    lane, row = lanes(), rows()
    route, plan = Rows(route_ref), Rows(plan_ref)
    came = by_link((first, second, third, fourth), BOTH)
    outer = [came[link][0:8, :] for link in range(4)]
    ends = []
    for end in range(2):
        values = []
        for link in range(4):
            which, lane_from = plan[2 * (2 * link + end)], plan[2 * (2 * link + end) + 1]
            held = jnp.where(which == 2, outer[3], outer[1])
            values.append(jnp.where(which > 0, pick(held, lane_from), 0.0))
        ends.append(rims_of(route, None, values))
    rims = rims_of(route, None, outer)
    beyond = rims_of(route, None, [came[link][8:16, :] for link in range(4)])
    lines, inner = four_of(lines_ref), four_of(inner_ref)
    patch = edge_patches(lines, rims)
    whole = with_ends(patch)
    on_edge, inside = [], []
    for side in range(4):
        sign = 1.0 if side in (1, 2) else -1.0
        line, wet, wet_in = rims[side], wet_rows(lines[side]), wet_rows(inner[side])
        after = jnp.where(lane == TILE - 1, ends[1][side], pltpu.roll(line, LANES - 1, 1))
        before = jnp.where(lane == 0, ends[0][side], pltpu.roll(line, 1, 1))
        upper, lower = pltpu.roll(line, 4, 0), pltpu.roll(line, 2, 0)
        normal, tangent = (upper, lower) if side % 2 == 1 else (lower, upper)
        along = normal * (sign * (beyond[side] - lines[side])) + tangent * (after - before)
        round_sum = after + before + beyond[side] + lines[side] - 4.0 * line
        tracer = wet_rows(line) * (line - (0.5 * ADVECT) * along + DIFFUSE * round_sum)
        mine = jnp.where(lane < TILE, whole[side], 0.0)
        to_normal, to_tangent = (4, 6) if side % 2 == 1 else (6, 4)
        own_row = row < 2 if side % 2 == 1 else (row >= 2) & (row < 4)
        cross_row = (row >= 2) & (row < 4) if side % 2 == 1 else row < 2
        cross = pressure_at(mine, to_tangent, row)
        drop = pltpu.roll(cross, LANES - 1, 1) - pltpu.roll(cross, 1, 1)
        push = jnp.where(own_row, sign * pressure_at(tracer, to_normal, row), 0.0)
        push = jnp.where(cross_row, drop, push)
        on_edge.append(patch[side] - (0.5 * STEP_SIZE) * wet * push)
        kept = own_row & (lane > 0) & (lane < TILE - 1)
        inside.append(jnp.where(kept, (-sign * 0.5 * STEP_SIZE) * wet_in * pressure_at(mine, to_normal, row), 0.0))
    edges, seconds = spread_chunks(on_edge, 0), spread_chunks(inside, 1)
    copies = []
    for low, high in ((0, 24), (24, CHUNKS)):
        for c in range(low, high):
            cut = slice(c * LANES, min((c + 1) * LANES, CELLS))
            width = cut.stop - cut.start
            full[:, cut] = (almost_ref[:, c * LANES:(c + 1) * LANES] + (edges[c] + seconds[c]))[:, :width]
        cells = pl.ds(low * LANES, min(high * LANES, CELLS) - low * LANES)
        copies.append(pltpu.make_async_copy(full.at[0:6, cells], out_ref.at[:, 0, cells], sems.at[len(copies)]))
        copies[-1].start()
    for copy in copies:
        copy.wait()


def write_out(full, out_ref, sems):
    copies = [pltpu.make_async_copy(full.at[c], out_ref.at[c, 0], sems.at[c]) for c in range(6)]
    for copy in copies:
        copy.start()
    for copy in copies:
        copy.wait()


def at_ends(line, lane_from, lane_to):
    value = jnp.broadcast_to(line[:, lane_from:lane_from + 1], (8, LANES))
    return jnp.where(lanes() == lane_to, value, 0.0)


def edge_kernel(route_ref, lines_ref, base_lines_ref, came0, came1, came2, came3,
                patch_ref, own_two_ref, pay0, pay1, pay2, pay3):
    route = Rows(route_ref)
    lines, base = four_of(lines_ref), four_of(base_lines_ref)
    own = own_rims([sent_line(lines[side], side, route, True) for side in range(4)], route)
    rims = rims_of(route, own, [came[0:8, :] for came in by_link((came0, came1, came2, came3), BOTH)])
    patch = edge_patches(lines, rims)
    whole = with_ends(patch)
    press = []
    for side in range(4):
        patch_ref[8 * side:8 * side + 8, :] = patch[side]
        press.append(sent_line(pressure_of(base[side] + whole[side], rows()), side, route, False))
    for link, pay in zip(SECOND_ORDER, (pay0, pay1, pay2, pay3)):
        pay[...] = chosen(press, route, link)
    own = own_rims(press, route)
    for side in range(4):
        own_two_ref[8 * side:8 * side + 8, :] = own[side]


def middle_kernel(route_ref, state_ref, base_ref, patch_ref, out_ref):
    state = state_ref[...]
    cell, column = column_of()
    base = base_ref[...] + spread(four_of(patch_ref), cell, column)
    row = lax.broadcasted_iota(jnp.int32, (8, WIDE), 0)
    out_ref[...] = if_live(route_ref, base + force_of(state, base, row))


def last_kernel(route_ref, lines_ref, own_ref, almost_ref, came0, came1, came2, came3, out_ref, full, sems):
    route = Rows(route_ref)
    rims = rims_of(route, four_of(own_ref), [came[...] for came in by_link((came0, came1, came2, came3), SECOND_ORDER)])
    patch = []
    for side in range(4):
        wet = wet_rows(lines_ref[8 * side:8 * side + 8, :])
        row = rows()
        rim = pltpu.roll(rims[side], 4 if side % 2 == 1 else 6, 0)
        mine = row < 2 if side % 2 == 1 else (row >= 2) & (row < 4)
        sign = -1.0 if side in (1, 2) else 1.0
        patch.append(jnp.where(mine, (sign * 0.5 * STEP_SIZE) * wet * rim, 0.0))
    cell, column = column_of()
    full[...] = (almost_ref[...] + spread(patch, cell, column))[:, :CELLS]
    write_out(full, out_ref, sems)


def sds(*shape, dtype=jnp.float32):
    return jax.ShapeDtypeStruct(shape, dtype)


PARAMS = pltpu.CompilerParams(vmem_limit_bytes=16 * 1024 * 1024)


def on_device(nx, ny, fields, wet_mask, tile_of_slot, neighbor, rotation):
    line, pair, four, wide = sds(8, LANES), sds(16, LANES), sds(32, LANES), sds(8, WIDE)
    scalars = pltpu.SMEM((4, nx * ny), jnp.int32)
    tables = [pltpu.with_memory_space_constraint(v, pltpu.HBM) for v in (tile_of_slot, neighbor.T, rotation.T)]
    inputs = [pltpu.with_memory_space_constraint(v, pltpu.HBM) for v in (fields.reshape(6, 1, CELLS), wet_mask)]
    halves = pltpu.with_memory_space_constraint(tile_of_slot.reshape(2, LANES), pltpu.HBM)
    raw, wet_raw, lines, inner, *pays, route = pl.pallas_call(
        lambda *refs: load_kernel((nx, ny), *refs),
        out_shape=[sds(8, CELLS), sds(8, CELLS, dtype=jnp.int32), four, four, pair, pair, pair, pair,
                   sds(ROUTE, LANES, dtype=jnp.int32)],
        in_specs=[HBM] * 5,
        out_specs=[VMEM] * 9,
        scratch_shapes=[pltpu.SMEM((nx * ny,), jnp.int32), scalars, scalars, pltpu.SemaphoreType.DMA((12,))],
        compiler_params=PARAMS, name="load",
    )(*tables, *inputs)
    came_u = exchanged(pays[:2], U_ORDER, nx, ny)
    almost, plan, flag = pl.pallas_call(
        lambda *refs: inner_kernel((nx, ny), *refs),
        out_shape=[wide, sds(16, LANES, dtype=jnp.int32), sds(1, dtype=jnp.int32)],
        in_specs=[HBM] * 4 + [VMEM] * 3, out_specs=[VMEM, VMEM, SMEM],
        scratch_shapes=[pltpu.VMEM((8, WIDE), jnp.float32), pltpu.SMEM((nx * ny,), jnp.int32), scalars, scalars,
                        pltpu.VMEM((2, LANES), jnp.int32), pltpu.VMEM((8, nx * ny), jnp.int32),
                        pltpu.SemaphoreType.DMA((5,))],
        compiler_params=PARAMS, name="inner",
        cost_estimate=pl.CostEstimate(flops=2000000, bytes_accessed=800000, transcendentals=0),
    )(*tables, halves, raw, wet_raw, route)
    sent = pl.pallas_call(
        relay_kernel, out_shape=[pair, pair], in_specs=[VMEM] * 4 + [ANY], out_specs=[VMEM] * 2,
        compiler_params=PARAMS, name="relay",
    )(*pays[2:], *came_u, almost)
    came_x = exchanged(sent, X_ORDER, nx, ny)
    result = pltpu.HBM((6, 1, CELLS), jnp.float32)
    writing = [pltpu.VMEM((8, CELLS), jnp.float32), pltpu.SemaphoreType.DMA((12,))]

    def grid_like():
        return pl.pallas_call(
            final_kernel, out_shape=result, in_specs=[VMEM] * 9, out_specs=HBM,
            scratch_shapes=writing, compiler_params=PARAMS, name="final",
        )(route, plan, lines, inner, almost, *came_u, *came_x)

    def general():
        came = came_u + came_x
        state, base, base_lines = pl.pallas_call(
            base_kernel, out_shape=[wide, wide, four], in_specs=[VMEM] * 2, out_specs=[VMEM] * 3,
            compiler_params=PARAMS, name="base",
            cost_estimate=pl.CostEstimate(flops=2000000, bytes_accessed=800000, transcendentals=0),
        )(raw, wet_raw)
        patch, own_two, *press = pl.pallas_call(
            edge_kernel, out_shape=[four, four, line, line, line, line],
            in_specs=[VMEM] * 7, out_specs=[VMEM] * 6,
            compiler_params=PARAMS, name="edge",
        )(route, lines, base_lines, *came)
        came_two = exchanged(press, SECOND_ORDER, nx, ny)
        nearly = pl.pallas_call(
            middle_kernel, out_shape=wide, in_specs=[VMEM] * 4, out_specs=VMEM,
            compiler_params=PARAMS, name="middle",
            cost_estimate=pl.CostEstimate(flops=2000000, bytes_accessed=800000, transcendentals=0),
        )(route, state, base, patch)
        return pl.pallas_call(
            last_kernel, out_shape=result, in_specs=[VMEM] * 8, out_specs=HBM,
            scratch_shapes=writing, compiler_params=PARAMS, name="last",
        )(route, lines, own_two, nearly, *came_two)

    out = lax.switch(flag[0], [grid_like, general])
    return out.reshape(1, 6, CELLS)


def solution(mesh):
    nx, ny = mesh.shape["gx"], mesh.shape["gy"]
    in_specs = (P(AXES, None, None), P(AXES, None), P(), P(), P())
    return jax.shard_map(lambda *args: on_device(nx, ny, *args), mesh=mesh, in_specs=in_specs,
                         out_specs=P(AXES, None, None), check_vma=False)
```

```python
import jax
import jax.numpy as jnp
from jax import lax
from jax.experimental import pallas as pl
from jax.experimental.pallas import tpu as pltpu
from jax.sharding import PartitionSpec as P

TILE = 90
CELLS = TILE * TILE
LANES = 128
CHUNKS = 64
WIDE = LANES * CHUNKS
HALF = 45
LAST = CELLS - TILE - (CHUNKS - 2) * LANES

ADVECT = 0.25
DIFFUSE = 0.15
STEP_SIZE = 0.5
CORIOLIS = 0.3
GRAVITY = 0.8

AXES = ("gx", "gy")
VMEM = pl.BlockSpec(memory_space=pltpu.VMEM)
SMEM = pl.BlockSpec(memory_space=pltpu.SMEM)
ANY = pl.BlockSpec(memory_space=pl.ANY)
HBM = pl.BlockSpec(memory_space=pltpu.HBM)


def over(value, count):
    return value >> (count.bit_length() - 1) if count & (count - 1) == 0 else value // count


def rest(value, count):
    return value & (count - 1) if count & (count - 1) == 0 else value % count


def link_x_even(x, y, nx, ny):
    return x ^ 1, y


def link_x_odd(x, y, nx, ny):
    return (((x + nx - 1) % nx ^ 1) + 1) % nx, y


def link_y_even(x, y, nx, ny):
    return x, y ^ 1


def link_y_odd(x, y, nx, ny):
    if y == 0 or y == ny - 1:
        return (x + nx // 2) % nx, y
    return x, ((y - 1) ^ 1) + 1


def swapped(x, nx):
    column = rest(x, nx // 2)
    return (column == 0) | (column == 2)


def link_u_first(x, y, nx, ny):
    return (link_y_even if swapped(x, nx) else link_y_odd)(x, y, nx, ny)


def link_u_second(x, y, nx, ny):
    return (link_y_odd if swapped(x, nx) else link_y_even)(x, y, nx, ny)


LINKS = (link_u_first, link_x_even, link_u_second, link_x_odd)


def pairs_of(link, nx, ny):
    out = []
    for x in range(nx):
        for y in range(ny):
            to_x, to_y = link(x, y, nx, ny)
            out.append((x * ny + y, to_x * ny + to_y))
    return out


U_ORDER = (0, 2)
X_ORDER = (3, 1)
BOTH = U_ORDER + X_ORDER
SECOND_ORDER = (2, 0, 3, 1)


def exchanged(pays, order, nx, ny):
    return [lax.ppermute(pay, AXES, pairs_of(LINKS[link], nx, ny)) for pay, link in zip(pays, order)]


def by_link(refs, order, links=(0, 1, 2, 3)):
    return [refs[order.index(link)] for link in links]


def partner(me, which, nx, ny):
    x, y = over(me, ny), rest(me, ny)
    if which == 1:
        return me + jnp.where(rest(x, 2) == 0, ny, -ny)
    if which == 3:
        return rest(me + jnp.where(rest(x, 2) == 1, ny, (nx - 1) * ny), nx * ny)
    even = me + jnp.where(rest(y, 2) == 0, 1, -1)
    pole = (y == 0) | (y == ny - 1)
    odd = jnp.where(pole, rest(me + nx // 2 * ny, nx * ny), me + jnp.where(rest(y, 2) == 1, 1, -1))
    return jnp.where(swapped(x, nx), even, odd) if which == 0 else jnp.where(swapped(x, nx), odd, even)


def lanes():
    return lax.broadcasted_iota(jnp.int32, (8, LANES), 1)


def rows():
    return lax.broadcasted_iota(jnp.int32, (8, LANES), 0)


def pick(values, index):
    return jnp.take_along_axis(values, index, axis=1)


def tiled(values, count):
    return jnp.concatenate([values] * count, axis=1)


def column_of():
    cell = lax.broadcasted_iota(jnp.int32, (8, WIDE), 1)
    line = jnp.floor((cell.astype(jnp.float32) + 0.5) * (1.0 / TILE)).astype(jnp.int32)
    return cell, cell - TILE * line


def edge_lines(state, column):
    lane = lanes()
    edge = (column == 0) | (column == TILE - 1)
    parts = []
    for low, high in ((0, HALF), (HALF, CHUNKS)):
        found = jnp.zeros((8, LANES), jnp.float32)
        for c in range(low, high):
            cut = slice(c * LANES, (c + 1) * LANES)
            found = jnp.where(edge[:, cut], state[:, cut], found)
        parts.append(found)
    east_at = (TILE * lane + TILE - 1) & (LANES - 1)
    west_at = (TILE * lane) & (LANES - 1)
    east = jnp.where(lane < 64, pick(parts[0], east_at), pick(parts[1], east_at))
    west = jnp.where(lane < 64, pick(parts[0], west_at), pick(parts[1], west_at))
    south = state[:, :LANES]
    before = pltpu.roll(state[:, (CHUNKS - 2) * LANES:(CHUNKS - 1) * LANES], LANES - LAST, 1)
    after = pltpu.roll(state[:, (CHUNKS - 1) * LANES:], LANES - LAST, 1)
    north = jnp.where(lane < LANES - LAST, before, after)
    return [south, east, north, west]


def spread(lines, cell, column):
    south, east, north, west = lines
    lane = lanes()
    odd = (lane & 1) == 1
    line_at = (37 * ((lane + jnp.where(odd, 39, 0)) >> 1)) & 63
    early = jnp.where(odd, pick(east, line_at), pick(west, line_at))
    late = jnp.where(odd, pick(east, line_at + 64), pick(west, line_at + 64))
    sides = jnp.concatenate([early] * HALF + [late] * (CHUNKS - HALF), axis=1)
    edge = (column == 0) | (column == TILE - 1)
    out = jnp.where(edge, sides, 0.0)
    first = jnp.where(lane < TILE, south, 0.0) + out[:, :LANES]
    moved = pltpu.roll(north, LAST, 1)
    before = out[:, (CHUNKS - 2) * LANES:(CHUNKS - 1) * LANES] + jnp.where(lane >= LAST, moved, 0.0)
    after = out[:, (CHUNKS - 1) * LANES:] + jnp.where(lane < LAST + TILE - LANES, moved, 0.0)
    return jnp.concatenate([first, out[:, LANES:(CHUNKS - 2) * LANES], before, after], axis=1)


def neighbours(state):
    cell, column = column_of()
    right = jnp.where(column == TILE - 1, 0.0, pltpu.roll(state, WIDE - 1, 1))
    left = jnp.where(column == 0, 0.0, pltpu.roll(state, 1, 1))
    up = jnp.where(cell >= CELLS - TILE, 0.0, pltpu.roll(state, WIDE - TILE, 1))
    down = jnp.where(cell < TILE, 0.0, pltpu.roll(state, TILE, 1))
    return right, left, up, down, cell, column


def row_of(values):
    return lax.broadcasted_iota(jnp.int32, values.shape, 0)


def repeated(values, first):
    row = row_of(values)
    if first == 0:
        pair = jnp.where(row < 2, values, pltpu.roll(values, 2, 0))
    else:
        pair = jnp.where(row < 4, values, pltpu.roll(values, 2, 0))
        pair = jnp.where(row < 2, pltpu.roll(values, 6, 0), pair)
        return pair
    return jnp.where(row < 4, pair, pltpu.roll(values, 4, 0))


def wet_rows(values):
    return jnp.broadcast_to(values[6:7], values.shape)


def turned(line, turns):
    row = row_of(line)
    swapped = jnp.where(row < 2, pltpu.roll(line, 6, 0), pltpu.roll(line, 2, 0))
    velocity = row < 4
    second = jnp.where(row < 2, swapped, -swapped)
    odd = jnp.where(turns % 2 == 1, 1, 0)
    out = jnp.where(jnp.logical_and(velocity, odd == 1), second, line)
    back = jnp.where(turns >= 2, 1, 0)
    return jnp.where(jnp.logical_and(velocity, back == 1), -out, out)


def flipped(line):
    return pick(line, jnp.maximum(TILE - 1 - lanes(), 0))


ROUTE = 48
OWN_AT, RELAY_AT = TILE, {0: TILE + 4, 2: TILE + 8}


class Rows:
    def __init__(self, ref):
        self.ref = ref

    def __getitem__(self, i):
        return jnp.broadcast_to(self.ref[i:i + 1, :], (8, LANES))


def my_index(ny):
    return lax.axis_index("gx") * ny + lax.axis_index("gy")


def sent_line(line, side, route, vector):
    line = jnp.where(route[32 + side] == 1, flipped(line), line)
    return turned(line, route[36 + side]) if vector else line


def chosen(lines, route, link):
    total = jnp.zeros((8, LANES), jnp.float32)
    for side in range(4):
        total = jnp.where(route[4 * link + side] == 1, lines[side], total)
    return total


def own_rims(sent, route):
    out = []
    for target in range(4):
        total = jnp.zeros((8, LANES), jnp.float32)
        for side in range(4):
            total = jnp.where(route[16 + 4 * side + target] == 1, sent[side], total)
        out.append(total)
    return out


def rims_of(route, base, came):
    out = []
    for side in range(4):
        rim = base[side] if base is not None else jnp.zeros((8, LANES), jnp.float32)
        for link in range(4):
            rim = jnp.where(route[4 * link + side] == 1, came[link], rim)
        out.append(rim)
    return out


def four_of(ref):
    return [ref[8 * side:8 * side + 8, :] for side in range(4)]


def columns_at(step):
    lane = lanes()
    odd = lane & 1
    shift = jnp.where(odd == 1, 39 + step, -step) if step % 2 == 0 else jnp.where(odd == 1, -step, 39 + step)
    column = jnp.where(odd == 1, TILE - 1 - step, step) if step % 2 == 0 else jnp.where(odd == 1, step, TILE - 1 - step)
    line_at = (37 * ((lane + shift) >> 1)) & 63
    return line_at, (TILE * line_at + column) >> 7


def raw_lines(chunk_of, step):
    lane = lanes()
    _, home = columns_at(step)
    parts = []
    for low, high in ((0, HALF), (HALF, CHUNKS)):
        found = chunk_of(low)
        for c in range(low + 1, high):
            found = jnp.where(home == c - low, chunk_of(c), found)
        parts.append(found)
    early = lane < 64
    out = [None] * 4
    for side, column in ((1, TILE - 1 - step), (3, step)):
        at = (TILE * lane + column) & (LANES - 1)
        out[side] = jnp.where(early, pick(parts[0], at), pick(parts[1], at))
    for side, first in ((0, TILE * step), (2, CELLS - TILE - TILE * step)):
        low, start = first // LANES, first % LANES
        if start == 0:
            out[side] = chunk_of(low)
        else:
            before = pltpu.roll(chunk_of(low), LANES - start, 1)
            after = pltpu.roll(chunk_of(low + 1), LANES - start, 1)
            out[side] = jnp.where(lane < LANES - start, before, after)
    return out


def spread_chunks(lines, step):
    lane = lanes()
    line_at, home = columns_at(step)
    odd = (lane & 1) == 1
    first_odd, first_even = (lines[1], lines[3]) if step % 2 == 0 else (lines[3], lines[1])
    early = jnp.where(odd, pick(first_odd, line_at), pick(first_even, line_at))
    late = jnp.where(odd, pick(first_odd, line_at + 64), pick(first_even, line_at + 64))
    out = []
    for c in range(CHUNKS):
        out.append(jnp.where(home == (c if c < HALF else c - HALF), early if c < HALF else late, 0.0))
    for side, first in ((0, TILE * step), (2, CELLS - TILE - TILE * step)):
        low, start = first // LANES, first % LANES
        line = jnp.where(lane < TILE, lines[side], 0.0)
        if start == 0:
            out[low] = out[low] + line
        else:
            moved = pltpu.roll(line, start, 1)
            out[low] = out[low] + jnp.where(lane >= start, moved, 0.0)
            if start + TILE > LANES:
                out[low + 1] = out[low + 1] + jnp.where(lane < start + TILE - LANES, moved, 0.0)
    return out


def load_kernel(shape, tiles_hbm, near_hbm, turn_hbm, fields_ref, wet_ref,
                raw, wet_raw, lines_ref, inner_ref, pay0, pay1, pay2, pay3, route_ref,
                tiles_ref, near_ref, turn_ref, sems):
    nx, ny = shape
    tables = [pltpu.make_async_copy(tiles_hbm, tiles_ref, sems.at[7]),
              pltpu.make_async_copy(near_hbm, near_ref, sems.at[8]),
              pltpu.make_async_copy(turn_hbm, turn_ref, sems.at[9])]
    copies = [pltpu.make_async_copy(fields_ref.at[:, 0], raw.at[0:6], sems.at[0])]
    copies.append(pltpu.make_async_copy(wet_ref.at[0], wet_raw.at[0], sems.at[6]))
    for copy in tables + copies:
        copy.start()
    for copy in tables:
        copy.wait()
    me = my_index(ny)
    route = [None] * ROUTE
    tile = tiles_ref[me]
    live = tile >= 0
    held = jnp.maximum(tile, 0)
    near = [jnp.where(live, near_ref[side, held], -1) for side in range(4)]
    turn = [turn_ref[side, held] for side in range(4)]
    for link in range(4):
        other = tiles_ref[partner(me, link, nx, ny)]
        for side in range(4):
            route[4 * link + side] = jnp.where((near[side] >= 0) & (near[side] == other), 1, 0)
    for side in range(4):
        target = (side + 2 + turn[side]) & 3
        for k in range(4):
            route[16 + 4 * side + k] = jnp.where((near[side] >= 0) & (near[side] == tile) & (target == k), 1, 0)
        route[32 + side] = jnp.where((target < 2) != (side >= 2), 1, 0)
        route[36 + side] = (4 - turn[side]) & 3
    route[40] = jnp.where(live, 1, 0)
    for i in range(41):
        route_ref[i:i + 1, :] = jnp.full((1, LANES), route[i], jnp.int32)
    for copy in copies:
        copy.wait()

    def chunk(ref, c):
        if c < CHUNKS - 1:
            return ref[:, c * LANES:(c + 1) * LANES]
        rest = CELLS - c * LANES
        part = ref[:, c * LANES:CELLS]
        return jnp.concatenate([part, jnp.zeros((8, LANES - rest), part.dtype)], axis=1)

    row, lane = rows(), lanes()
    both = []
    for step, ref in ((0, lines_ref), (1, inner_ref)):
        lines = []
        for value, wet in zip(raw_lines(lambda c: chunk(raw, c), step), raw_lines(lambda c: chunk(wet_raw, c), step)):
            wet = jnp.broadcast_to(wet[0:1], (8, LANES)).astype(jnp.float32)
            lines.append(jnp.where(row < 6, value * wet, jnp.where(row == 6, wet, 0.0)))
        for side in range(4):
            ref[8 * side:8 * side + 8, :] = lines[side]
        both.append(lines)
    ends = [jnp.where((lane == OWN_AT + 1) | (lane == OWN_AT + 2), TILE - 1, 0)] * 2
    corners = jnp.where(lane < OWN_AT + 2, pick(both[0][0], ends[0]), pick(both[0][2], ends[1]))
    at_corners = (lane >= OWN_AT) & (lane < OWN_AT + 4)
    sent = [sent_line(both[0][side], side, route, True) for side in range(4)]
    sent_inner = [sent_line(both[1][side], side, route, False) for side in range(4)]
    for link, pay in zip(BOTH, (pay0, pay1, pay2, pay3)):
        pay[0:8, :] = jnp.where(at_corners, corners, chosen(sent, route, link))
        pay[8:16, :] = chosen(sent_inner, route, link)


def pressure_of(tracer, row):
    return GRAVITY * jnp.where(row == 5, tracer + pltpu.roll(tracer, 1, 0), tracer)


def force_of(state, base, row):
    right, left, up, down, cell, column = neighbours(pressure_of(base, row))
    slope = jnp.where(row < 2, pltpu.roll(right - left, 4, 0), pltpu.roll(up - down, 6, 0))
    swapped = jnp.where(row < 2, pltpu.roll(state, 6, 0), -pltpu.roll(state, 2, 0))
    force = STEP_SIZE * (CORIOLIS * swapped - 0.5 * slope)
    return jnp.where(row < 4, wet_rows(state) * force, 0.0)


def masked_state(raw, wet_raw, state_ref):
    state_ref[:, (CHUNKS - 1) * LANES:] = jnp.zeros((8, LANES), jnp.float32)
    for low, high in ((0, (CHUNKS - 1) * LANES), ((CHUNKS - 1) * LANES, CELLS)):
        size = (8, high - low)
        row = lax.broadcasted_iota(jnp.int32, size, 0)
        wet = jnp.broadcast_to(wet_raw[0:1, low:high].astype(jnp.float32), size)
        state_ref[:, low:high] = jnp.where(row < 6, raw[:, low:high] * wet, jnp.where(row == 6, wet, 0.0))
    return state_ref[...]


def without_rims(state):
    right, left, up, down, cell, column = neighbours(state)
    first, second, wet = repeated(state, 0), repeated(state, 2), wet_rows(state)
    along = first * (right - left) + second * (up - down)
    round_sum = right + left + up + down - 4.0 * state
    return wet * (state - (0.5 * ADVECT) * along + DIFFUSE * round_sum), column


def if_live(route_ref, values):
    return jnp.where(tiled(Rows(route_ref)[40], CHUNKS) == 1, values, 0.0)


def base_kernel(raw, wet_raw, state_ref, base_ref, base_lines_ref):
    state = masked_state(raw, wet_raw, state_ref)
    base, column = without_rims(state)
    base_ref[...] = base
    lines = edge_lines(base, column)
    for side in range(4):
        base_lines_ref[8 * side:8 * side + 8, :] = lines[side]


def inner_kernel(shape, tiles_hbm, near_hbm, turn_hbm, halves_hbm, raw, wet_raw, route_ref,
                 almost_ref, plan_ref, flag, state_ref, tiles_ref, near_ref, turn_ref, halves_ref, table_ref, sems):
    copies = [pltpu.make_async_copy(tiles_hbm, tiles_ref, sems.at[0]),
              pltpu.make_async_copy(near_hbm, near_ref, sems.at[1]),
              pltpu.make_async_copy(turn_hbm, turn_ref, sems.at[2]),
              pltpu.make_async_copy(halves_hbm, halves_ref, sems.at[3]),
              pltpu.make_async_copy(near_hbm, table_ref.at[0:4], sems.at[4])]
    for copy in copies:
        copy.start()
    state = masked_state(raw, wet_raw, state_ref)
    base, _ = without_rims(state)
    almost_ref[...] = base
    for copy in copies:
        copy.wait()
    flag[0] = off_grid(shape, halves_ref, table_ref)
    corner_plan(shape, tiles_ref, near_ref, turn_ref, plan_ref)
    base = almost_ref[...]
    row = lax.broadcasted_iota(jnp.int32, (8, WIDE), 0)
    almost_ref[...] = if_live(route_ref, base + force_of(state_ref[...], base, row))


def off_grid(shape, halves_ref, table_ref):
    nx, ny = shape
    row, lane = rows(), lanes()
    tiles = [jnp.broadcast_to(halves_ref[half:half + 1, :], (8, LANES)) for half in range(2)]
    near = [table_ref[:, half * LANES:(half + 1) * LANES] for half in range(2)]

    def look(table, index):
        return jnp.where(index < LANES, pick(table[0], index & (LANES - 1)), pick(table[1], index & (LANES - 1)))

    worst = jnp.zeros((8, LANES), jnp.int32)
    for half in range(2):
        tile = tiles[half]
        mine = look(near, jnp.maximum(tile, 0))
        linked = (tile >= 0) & (mine >= 0) & (row < 4)
        other = [look(tiles, partner(lane + half * LANES, link, nx, ny)) for link in range(4)]
        over_x = (mine == other[1]) | (mine == other[3])
        kind = jnp.where(linked, jnp.where(mine == tile, 4, jnp.where(over_x, 1, 2)), 0)
        after = jnp.where(row < 3, pltpu.roll(kind, 7, 0), pltpu.roll(kind, 3, 0))
        odd = (kind == 4) | ((kind > 0) & (kind == after) & (row < 4))
        worst = jnp.where(odd, 1, worst)
    return jnp.max(worst)


def corner_plan(shape, tiles_ref, near_ref, turn_ref, plan_ref):
    nx, ny = shape
    me = my_index(ny)
    tile = tiles_ref[me]
    held = jnp.maximum(tile, 0)
    across = [partner(me, link, nx, ny) for link in range(4)]
    relayed = [(which, RELAY_AT[u], tiles_ref[partner(across[x], u, nx, ny)])
               for which, x in ((1, 1), (2, 3)) for u in (0, 2)]
    for link in range(4):
        other = tiles_ref[across[link]]
        side = jnp.int32(-1)
        for k in range(4):
            side = jnp.where((tile >= 0) & (other >= 0) & (near_ref[k, held] == other), k, side)
        facing = (side + 2 + turn_ref[jnp.maximum(side, 0), held]) & 3
        there = jnp.maximum(other, 0)
        for end in range(2):
            later = (side < 2) == (end == 0)
            lateral = jnp.where(later, facing + 1, facing + 3) & 3
            beyond = jnp.where(side >= 0, near_ref[lateral, there], -1)
            back = (lateral + 2 + turn_ref[lateral, there]) & 3
            corner = jnp.where(later, back + 1, back) & 3
            buffer, lane = jnp.int32(0), jnp.int32(0)
            for which, base, name in relayed:
                here = (beyond >= 0) & (beyond == name)
                buffer, lane = jnp.where(here, which, buffer), jnp.where(here, base + corner, lane)
            at = 2 * (2 * link + end)
            plan_ref[at:at + 1, :] = jnp.full((1, LANES), buffer, jnp.int32)
            plan_ref[at + 1:at + 2, :] = jnp.full((1, LANES), lane, jnp.int32)


def relay_kernel(pay0, pay1, came0, came1, after, out0, out1):
    lane = lanes()
    for pay, out in ((pay0, out0), (pay1, out1)):
        line = pay[0:8, :]
        for link, came in zip(U_ORDER, (came0, came1)):
            moved = pltpu.roll(came[0:8, :], RELAY_AT[link] - OWN_AT, 1)
            line = jnp.where((lane >= RELAY_AT[link]) & (lane < RELAY_AT[link] + 4), moved, line)
        out[0:8, :] = line
        out[8:16, :] = pay[8:16, :]


def edge_patches(lines, rims):
    patch = []
    for side in range(4):
        drift = repeated(lines[side], 0 if side % 2 == 1 else 2)
        sign = 1.0 if side in (1, 2) else -1.0
        patch.append(wet_rows(lines[side]) * (DIFFUSE - (sign * 0.5 * ADVECT) * drift) * rims[side])
    return patch


def with_ends(patch):
    south, east, north, west = patch
    end = TILE - 1
    return [
        south + at_ends(west, 0, 0) + at_ends(east, 0, end),
        east + at_ends(south, end, 0) + at_ends(north, end, end),
        north + at_ends(west, end, 0) + at_ends(east, end, end),
        west + at_ends(south, 0, 0) + at_ends(north, 0, end),
    ]


def pressure_at(tracer, shift, row):
    return GRAVITY * (pltpu.roll(tracer, shift, 0)
                      + jnp.where(row == (5 + shift) % 8, pltpu.roll(tracer, shift + 1, 0), 0.0))


def final_kernel(route_ref, plan_ref, lines_ref, inner_ref, almost_ref, first, second, third, fourth, out_ref, full, sems):
    lane, row = lanes(), rows()
    route, plan = Rows(route_ref), Rows(plan_ref)
    came = by_link((first, second, third, fourth), BOTH)
    outer = [came[link][0:8, :] for link in range(4)]
    ends = []
    for end in range(2):
        values = []
        for link in range(4):
            which, lane_from = plan[2 * (2 * link + end)], plan[2 * (2 * link + end) + 1]
            held = jnp.where(which == 2, outer[3], outer[1])
            values.append(jnp.where(which > 0, pick(held, lane_from), 0.0))
        ends.append(rims_of(route, None, values))
    rims = rims_of(route, None, outer)
    beyond = rims_of(route, None, [came[link][8:16, :] for link in range(4)])
    lines, inner = four_of(lines_ref), four_of(inner_ref)
    patch = edge_patches(lines, rims)
    whole = with_ends(patch)
    on_edge, inside = [], []
    for side in range(4):
        sign = 1.0 if side in (1, 2) else -1.0
        line, wet, wet_in = rims[side], wet_rows(lines[side]), wet_rows(inner[side])
        after = jnp.where(lane == TILE - 1, ends[1][side], pltpu.roll(line, LANES - 1, 1))
        before = jnp.where(lane == 0, ends[0][side], pltpu.roll(line, 1, 1))
        upper, lower = pltpu.roll(line, 4, 0), pltpu.roll(line, 2, 0)
        normal, tangent = (upper, lower) if side % 2 == 1 else (lower, upper)
        along = normal * (sign * (beyond[side] - lines[side])) + tangent * (after - before)
        round_sum = after + before + beyond[side] + lines[side] - 4.0 * line
        tracer = wet_rows(line) * (line - (0.5 * ADVECT) * along + DIFFUSE * round_sum)
        mine = jnp.where(lane < TILE, whole[side], 0.0)
        to_normal, to_tangent = (4, 6) if side % 2 == 1 else (6, 4)
        own_row = row < 2 if side % 2 == 1 else (row >= 2) & (row < 4)
        cross_row = (row >= 2) & (row < 4) if side % 2 == 1 else row < 2
        cross = pressure_at(mine, to_tangent, row)
        drop = pltpu.roll(cross, LANES - 1, 1) - pltpu.roll(cross, 1, 1)
        push = jnp.where(own_row, sign * pressure_at(tracer, to_normal, row), 0.0)
        push = jnp.where(cross_row, drop, push)
        on_edge.append(patch[side] - (0.5 * STEP_SIZE) * wet * push)
        kept = own_row & (lane > 0) & (lane < TILE - 1)
        inside.append(jnp.where(kept, (-sign * 0.5 * STEP_SIZE) * wet_in * pressure_at(mine, to_normal, row), 0.0))
    edges, seconds = spread_chunks(on_edge, 0), spread_chunks(inside, 1)
    copies = []
    for low, high in ((0, 24), (24, CHUNKS)):
        for c in range(low, high):
            cut = slice(c * LANES, min((c + 1) * LANES, CELLS))
            width = cut.stop - cut.start
            full[:, cut] = (almost_ref[:, c * LANES:(c + 1) * LANES] + (edges[c] + seconds[c]))[:, :width]
        cells = pl.ds(low * LANES, min(high * LANES, CELLS) - low * LANES)
        copies.append(pltpu.make_async_copy(full.at[0:6, cells], out_ref.at[:, 0, cells], sems.at[len(copies)]))
        copies[-1].start()
    for copy in copies:
        copy.wait()


def write_out(full, out_ref, sems):
    copies = [pltpu.make_async_copy(full.at[c], out_ref.at[c, 0], sems.at[c]) for c in range(6)]
    for copy in copies:
        copy.start()
    for copy in copies:
        copy.wait()


def at_ends(line, lane_from, lane_to):
    value = jnp.broadcast_to(line[:, lane_from:lane_from + 1], (8, LANES))
    return jnp.where(lanes() == lane_to, value, 0.0)


def edge_kernel(route_ref, lines_ref, base_lines_ref, came0, came1, came2, came3,
                patch_ref, own_two_ref, pay0, pay1, pay2, pay3):
    route = Rows(route_ref)
    lines, base = four_of(lines_ref), four_of(base_lines_ref)
    own = own_rims([sent_line(lines[side], side, route, True) for side in range(4)], route)
    rims = rims_of(route, own, [came[0:8, :] for came in by_link((came0, came1, came2, came3), BOTH)])
    patch = edge_patches(lines, rims)
    whole = with_ends(patch)
    press = []
    for side in range(4):
        patch_ref[8 * side:8 * side + 8, :] = patch[side]
        press.append(sent_line(pressure_of(base[side] + whole[side], rows()), side, route, False))
    for link, pay in zip(SECOND_ORDER, (pay0, pay1, pay2, pay3)):
        pay[...] = chosen(press, route, link)
    own = own_rims(press, route)
    for side in range(4):
        own_two_ref[8 * side:8 * side + 8, :] = own[side]


def middle_kernel(route_ref, state_ref, base_ref, patch_ref, out_ref):
    state = state_ref[...]
    cell, column = column_of()
    base = base_ref[...] + spread(four_of(patch_ref), cell, column)
    row = lax.broadcasted_iota(jnp.int32, (8, WIDE), 0)
    out_ref[...] = if_live(route_ref, base + force_of(state, base, row))


def last_kernel(route_ref, lines_ref, own_ref, almost_ref, came0, came1, came2, came3, out_ref, full, sems):
    route = Rows(route_ref)
    rims = rims_of(route, four_of(own_ref), [came[...] for came in by_link((came0, came1, came2, came3), SECOND_ORDER)])
    patch = []
    for side in range(4):
        wet = wet_rows(lines_ref[8 * side:8 * side + 8, :])
        row = rows()
        rim = pltpu.roll(rims[side], 4 if side % 2 == 1 else 6, 0)
        mine = row < 2 if side % 2 == 1 else (row >= 2) & (row < 4)
        sign = -1.0 if side in (1, 2) else 1.0
        patch.append(jnp.where(mine, (sign * 0.5 * STEP_SIZE) * wet * rim, 0.0))
    cell, column = column_of()
    full[...] = (almost_ref[...] + spread(patch, cell, column))[:, :CELLS]
    write_out(full, out_ref, sems)


def sds(*shape, dtype=jnp.float32):
    return jax.ShapeDtypeStruct(shape, dtype)


PARAMS = pltpu.CompilerParams(vmem_limit_bytes=16 * 1024 * 1024)


def on_device(nx, ny, fields, wet_mask, tile_of_slot, neighbor, rotation):
    line, pair, four, wide = sds(8, LANES), sds(16, LANES), sds(32, LANES), sds(8, WIDE)
    scalars = pltpu.SMEM((4, nx * ny), jnp.int32)
    tables = [pltpu.with_memory_space_constraint(v, pltpu.HBM) for v in (tile_of_slot, neighbor.T, rotation.T)]
    inputs = [pltpu.with_memory_space_constraint(v, pltpu.HBM) for v in (fields.reshape(6, 1, CELLS), wet_mask)]
    halves = pltpu.with_memory_space_constraint(tile_of_slot.reshape(2, LANES), pltpu.HBM)
    raw, wet_raw, lines, inner, *pays, route = pl.pallas_call(
        lambda *refs: load_kernel((nx, ny), *refs),
        out_shape=[sds(8, CELLS), sds(8, CELLS, dtype=jnp.int32), four, four, pair, pair, pair, pair,
                   sds(ROUTE, LANES, dtype=jnp.int32)],
        in_specs=[HBM] * 5,
        out_specs=[VMEM] * 9,
        scratch_shapes=[pltpu.SMEM((nx * ny,), jnp.int32), scalars, scalars, pltpu.SemaphoreType.DMA((12,))],
        compiler_params=PARAMS, name="load",
    )(*tables, *inputs)
    came_u = exchanged(pays[:2], U_ORDER, nx, ny)
    almost, plan, flag = pl.pallas_call(
        lambda *refs: inner_kernel((nx, ny), *refs),
        out_shape=[wide, sds(16, LANES, dtype=jnp.int32), sds(1, dtype=jnp.int32)],
        in_specs=[HBM] * 4 + [VMEM] * 3, out_specs=[VMEM, VMEM, SMEM],
        scratch_shapes=[pltpu.VMEM((8, WIDE), jnp.float32), pltpu.SMEM((nx * ny,), jnp.int32), scalars, scalars,
                        pltpu.VMEM((2, LANES), jnp.int32), pltpu.VMEM((8, nx * ny), jnp.int32),
                        pltpu.SemaphoreType.DMA((5,))],
        compiler_params=PARAMS, name="inner",
        cost_estimate=pl.CostEstimate(flops=2000000, bytes_accessed=800000, transcendentals=0),
    )(*tables, halves, raw, wet_raw, route)
    sent = pl.pallas_call(
        relay_kernel, out_shape=[pair, pair], in_specs=[VMEM] * 4 + [ANY], out_specs=[VMEM] * 2,
        compiler_params=PARAMS, name="relay",
    )(*pays[2:], *came_u, almost)
    came_x = exchanged(sent, X_ORDER, nx, ny)
    result = pltpu.HBM((6, 1, CELLS), jnp.float32)
    writing = [pltpu.VMEM((8, CELLS), jnp.float32), pltpu.SemaphoreType.DMA((12,))]

    def grid_like():
        return pl.pallas_call(
            final_kernel, out_shape=result, in_specs=[VMEM] * 9, out_specs=HBM,
            scratch_shapes=writing, compiler_params=PARAMS, name="final",
        )(route, plan, lines, inner, almost, *came_u, *came_x)

    def general():
        came = came_u + came_x
        state, base, base_lines = pl.pallas_call(
            base_kernel, out_shape=[wide, wide, four], in_specs=[VMEM] * 2, out_specs=[VMEM] * 3,
            compiler_params=PARAMS, name="base",
            cost_estimate=pl.CostEstimate(flops=2000000, bytes_accessed=800000, transcendentals=0),
        )(raw, wet_raw)
        patch, own_two, *press = pl.pallas_call(
            edge_kernel, out_shape=[four, four, line, line, line, line],
            in_specs=[VMEM] * 7, out_specs=[VMEM] * 6,
            compiler_params=PARAMS, name="edge",
        )(route, lines, base_lines, *came)
        came_two = exchanged(press, SECOND_ORDER, nx, ny)
        nearly = pl.pallas_call(
            middle_kernel, out_shape=wide, in_specs=[VMEM] * 4, out_specs=VMEM,
            compiler_params=PARAMS, name="middle",
            cost_estimate=pl.CostEstimate(flops=2000000, bytes_accessed=800000, transcendentals=0),
        )(route, state, base, patch)
        return pl.pallas_call(
            last_kernel, out_shape=result, in_specs=[VMEM] * 8, out_specs=HBM,
            scratch_shapes=writing, compiler_params=PARAMS, name="last",
        )(route, lines, own_two, nearly, *came_two)

    out = lax.switch(flag[0], [grid_like, general])
    return out.reshape(1, 6, CELLS)


def solution(mesh):
    nx, ny = mesh.shape["gx"], mesh.shape["gy"]
    in_specs = (P(AXES, None, None), P(AXES, None), P(), P(), P())
    return jax.shard_map(lambda *args: on_device(nx, ny, *args), mesh=mesh, in_specs=in_specs,
                         out_specs=P(AXES, None, None), check_vma=False)
```

```python
import jax
import jax.numpy as jnp
from jax import lax
from jax.experimental import pallas as pl
from jax.experimental.pallas import tpu as pltpu
from jax.sharding import PartitionSpec as P

TILE = 90
CELLS = TILE * TILE
LANES = 128
CHUNKS = 64
WIDE = LANES * CHUNKS
HALF = 45
LAST = CELLS - TILE - (CHUNKS - 2) * LANES

ADVECT = 0.25
DIFFUSE = 0.15
STEP_SIZE = 0.5
CORIOLIS = 0.3
GRAVITY = 0.8

AXES = ("gx", "gy")
VMEM = pl.BlockSpec(memory_space=pltpu.VMEM)
SMEM = pl.BlockSpec(memory_space=pltpu.SMEM)
ANY = pl.BlockSpec(memory_space=pl.ANY)
HBM = pl.BlockSpec(memory_space=pltpu.HBM)


def over(value, count):
    return value >> (count.bit_length() - 1) if count & (count - 1) == 0 else value // count


def rest(value, count):
    return value & (count - 1) if count & (count - 1) == 0 else value % count


def link_x_even(x, y, nx, ny):
    return x ^ 1, y


def link_x_odd(x, y, nx, ny):
    return (((x + nx - 1) % nx ^ 1) + 1) % nx, y


def link_y_even(x, y, nx, ny):
    return x, y ^ 1


def link_y_odd(x, y, nx, ny):
    if y == 0 or y == ny - 1:
        return (x + nx // 2) % nx, y
    return x, ((y - 1) ^ 1) + 1


def swapped(x, nx):
    column = rest(x, nx // 2)
    return (column == 0) | (column == 2)


def link_u_first(x, y, nx, ny):
    return (link_y_even if swapped(x, nx) else link_y_odd)(x, y, nx, ny)


def link_u_second(x, y, nx, ny):
    return (link_y_odd if swapped(x, nx) else link_y_even)(x, y, nx, ny)


LINKS = (link_u_first, link_x_even, link_u_second, link_x_odd)


def pairs_of(link, nx, ny):
    out = []
    for x in range(nx):
        for y in range(ny):
            to_x, to_y = link(x, y, nx, ny)
            out.append((x * ny + y, to_x * ny + to_y))
    return out


U_ORDER = (0, 2)
X_ORDER = (3, 1)
BOTH = U_ORDER + X_ORDER
SECOND_ORDER = (2, 0, 3, 1)


def exchanged(pays, order, nx, ny):
    return [lax.ppermute(pay, AXES, pairs_of(LINKS[link], nx, ny)) for pay, link in zip(pays, order)]


def by_link(refs, order, links=(0, 1, 2, 3)):
    return [refs[order.index(link)] for link in links]


def partner(me, which, nx, ny):
    x, y = over(me, ny), rest(me, ny)
    if which == 1:
        return me + jnp.where(rest(x, 2) == 0, ny, -ny)
    if which == 3:
        return rest(me + jnp.where(rest(x, 2) == 1, ny, (nx - 1) * ny), nx * ny)
    even = me + jnp.where(rest(y, 2) == 0, 1, -1)
    pole = (y == 0) | (y == ny - 1)
    odd = jnp.where(pole, rest(me + nx // 2 * ny, nx * ny), me + jnp.where(rest(y, 2) == 1, 1, -1))
    return jnp.where(swapped(x, nx), even, odd) if which == 0 else jnp.where(swapped(x, nx), odd, even)


def lanes():
    return lax.broadcasted_iota(jnp.int32, (8, LANES), 1)


def rows():
    return lax.broadcasted_iota(jnp.int32, (8, LANES), 0)


def pick(values, index):
    return jnp.take_along_axis(values, index, axis=1)


def tiled(values, count):
    return jnp.concatenate([values] * count, axis=1)


def column_of():
    cell = lax.broadcasted_iota(jnp.int32, (8, WIDE), 1)
    line = jnp.floor((cell.astype(jnp.float32) + 0.5) * (1.0 / TILE)).astype(jnp.int32)
    return cell, cell - TILE * line


def edge_lines(state, column):
    lane = lanes()
    edge = (column == 0) | (column == TILE - 1)
    parts = []
    for low, high in ((0, HALF), (HALF, CHUNKS)):
        found = jnp.zeros((8, LANES), jnp.float32)
        for c in range(low, high):
            cut = slice(c * LANES, (c + 1) * LANES)
            found = jnp.where(edge[:, cut], state[:, cut], found)
        parts.append(found)
    east_at = (TILE * lane + TILE - 1) & (LANES - 1)
    west_at = (TILE * lane) & (LANES - 1)
    east = jnp.where(lane < 64, pick(parts[0], east_at), pick(parts[1], east_at))
    west = jnp.where(lane < 64, pick(parts[0], west_at), pick(parts[1], west_at))
    south = state[:, :LANES]
    before = pltpu.roll(state[:, (CHUNKS - 2) * LANES:(CHUNKS - 1) * LANES], LANES - LAST, 1)
    after = pltpu.roll(state[:, (CHUNKS - 1) * LANES:], LANES - LAST, 1)
    north = jnp.where(lane < LANES - LAST, before, after)
    return [south, east, north, west]


def spread(lines, cell, column):
    south, east, north, west = lines
    lane = lanes()
    odd = (lane & 1) == 1
    line_at = (37 * ((lane + jnp.where(odd, 39, 0)) >> 1)) & 63
    early = jnp.where(odd, pick(east, line_at), pick(west, line_at))
    late = jnp.where(odd, pick(east, line_at + 64), pick(west, line_at + 64))
    sides = jnp.concatenate([early] * HALF + [late] * (CHUNKS - HALF), axis=1)
    edge = (column == 0) | (column == TILE - 1)
    out = jnp.where(edge, sides, 0.0)
    first = jnp.where(lane < TILE, south, 0.0) + out[:, :LANES]
    moved = pltpu.roll(north, LAST, 1)
    before = out[:, (CHUNKS - 2) * LANES:(CHUNKS - 1) * LANES] + jnp.where(lane >= LAST, moved, 0.0)
    after = out[:, (CHUNKS - 1) * LANES:] + jnp.where(lane < LAST + TILE - LANES, moved, 0.0)
    return jnp.concatenate([first, out[:, LANES:(CHUNKS - 2) * LANES], before, after], axis=1)


def neighbours(state):
    cell, column = column_of()
    right = jnp.where(column == TILE - 1, 0.0, pltpu.roll(state, WIDE - 1, 1))
    left = jnp.where(column == 0, 0.0, pltpu.roll(state, 1, 1))
    up = jnp.where(cell >= CELLS - TILE, 0.0, pltpu.roll(state, WIDE - TILE, 1))
    down = jnp.where(cell < TILE, 0.0, pltpu.roll(state, TILE, 1))
    return right, left, up, down, cell, column


def row_of(values):
    return lax.broadcasted_iota(jnp.int32, values.shape, 0)


def repeated(values, first):
    row = row_of(values)
    if first == 0:
        pair = jnp.where(row < 2, values, pltpu.roll(values, 2, 0))
    else:
        pair = jnp.where(row < 4, values, pltpu.roll(values, 2, 0))
        pair = jnp.where(row < 2, pltpu.roll(values, 6, 0), pair)
        return pair
    return jnp.where(row < 4, pair, pltpu.roll(values, 4, 0))


def wet_rows(values):
    return jnp.broadcast_to(values[6:7], values.shape)


def turned(line, turns):
    row = row_of(line)
    swapped = jnp.where(row < 2, pltpu.roll(line, 6, 0), pltpu.roll(line, 2, 0))
    velocity = row < 4
    second = jnp.where(row < 2, swapped, -swapped)
    odd = jnp.where(turns % 2 == 1, 1, 0)
    out = jnp.where(jnp.logical_and(velocity, odd == 1), second, line)
    back = jnp.where(turns >= 2, 1, 0)
    return jnp.where(jnp.logical_and(velocity, back == 1), -out, out)


def flipped(line):
    return pick(line, jnp.maximum(TILE - 1 - lanes(), 0))


ROUTE = 48
OWN_AT, RELAY_AT = TILE, {0: TILE + 4, 2: TILE + 8}


class Rows:
    def __init__(self, ref):
        self.ref = ref

    def __getitem__(self, i):
        return jnp.broadcast_to(self.ref[i:i + 1, :], (8, LANES))


def my_index(ny):
    return lax.axis_index("gx") * ny + lax.axis_index("gy")


def sent_line(line, side, route, vector):
    line = jnp.where(route[32 + side] == 1, flipped(line), line)
    return turned(line, route[36 + side]) if vector else line


def chosen(lines, route, link):
    total = jnp.zeros((8, LANES), jnp.float32)
    for side in range(4):
        total = jnp.where(route[4 * link + side] == 1, lines[side], total)
    return total


def own_rims(sent, route):
    out = []
    for target in range(4):
        total = jnp.zeros((8, LANES), jnp.float32)
        for side in range(4):
            total = jnp.where(route[16 + 4 * side + target] == 1, sent[side], total)
        out.append(total)
    return out


def rims_of(route, base, came):
    out = []
    for side in range(4):
        rim = base[side] if base is not None else jnp.zeros((8, LANES), jnp.float32)
        for link in range(4):
            rim = jnp.where(route[4 * link + side] == 1, came[link], rim)
        out.append(rim)
    return out


def four_of(ref):
    return [ref[8 * side:8 * side + 8, :] for side in range(4)]


def columns_at(step):
    lane = lanes()
    odd = lane & 1
    shift = jnp.where(odd == 1, 39 + step, -step) if step % 2 == 0 else jnp.where(odd == 1, -step, 39 + step)
    column = jnp.where(odd == 1, TILE - 1 - step, step) if step % 2 == 0 else jnp.where(odd == 1, step, TILE - 1 - step)
    line_at = (37 * ((lane + shift) >> 1)) & 63
    return line_at, (TILE * line_at + column) >> 7


def raw_lines(chunk_of, step):
    lane = lanes()
    _, home = columns_at(step)
    parts = []
    for low, high in ((0, HALF), (HALF, CHUNKS)):
        found = chunk_of(low)
        for c in range(low + 1, high):
            found = jnp.where(home == c - low, chunk_of(c), found)
        parts.append(found)
    early = lane < 64
    out = [None] * 4
    for side, column in ((1, TILE - 1 - step), (3, step)):
        at = (TILE * lane + column) & (LANES - 1)
        out[side] = jnp.where(early, pick(parts[0], at), pick(parts[1], at))
    for side, first in ((0, TILE * step), (2, CELLS - TILE - TILE * step)):
        low, start = first // LANES, first % LANES
        if start == 0:
            out[side] = chunk_of(low)
        else:
            before = pltpu.roll(chunk_of(low), LANES - start, 1)
            after = pltpu.roll(chunk_of(low + 1), LANES - start, 1)
            out[side] = jnp.where(lane < LANES - start, before, after)
    return out


def spread_chunks(lines, step):
    lane = lanes()
    line_at, home = columns_at(step)
    odd = (lane & 1) == 1
    first_odd, first_even = (lines[1], lines[3]) if step % 2 == 0 else (lines[3], lines[1])
    early = jnp.where(odd, pick(first_odd, line_at), pick(first_even, line_at))
    late = jnp.where(odd, pick(first_odd, line_at + 64), pick(first_even, line_at + 64))
    out = []
    for c in range(CHUNKS):
        out.append(jnp.where(home == (c if c < HALF else c - HALF), early if c < HALF else late, 0.0))
    for side, first in ((0, TILE * step), (2, CELLS - TILE - TILE * step)):
        low, start = first // LANES, first % LANES
        line = jnp.where(lane < TILE, lines[side], 0.0)
        if start == 0:
            out[low] = out[low] + line
        else:
            moved = pltpu.roll(line, start, 1)
            out[low] = out[low] + jnp.where(lane >= start, moved, 0.0)
            if start + TILE > LANES:
                out[low + 1] = out[low + 1] + jnp.where(lane < start + TILE - LANES, moved, 0.0)
    return out


def load_kernel(shape, tiles_hbm, near_hbm, turn_hbm, fields_ref, wet_ref,
                raw, wet_raw, lines_ref, inner_ref, pay0, pay1, pay2, pay3, route_ref,
                tiles_ref, near_ref, turn_ref, sems):
    nx, ny = shape
    tables = [pltpu.make_async_copy(tiles_hbm, tiles_ref, sems.at[7]),
              pltpu.make_async_copy(near_hbm, near_ref, sems.at[8]),
              pltpu.make_async_copy(turn_hbm, turn_ref, sems.at[9])]
    copies = [pltpu.make_async_copy(fields_ref.at[:, 0], raw.at[0:6], sems.at[0])]
    copies.append(pltpu.make_async_copy(wet_ref.at[0], wet_raw.at[0], sems.at[6]))
    for copy in tables + copies:
        copy.start()
    for copy in tables:
        copy.wait()
    me = my_index(ny)
    route = [None] * ROUTE
    tile = tiles_ref[me]
    live = tile >= 0
    held = jnp.maximum(tile, 0)
    near = [jnp.where(live, near_ref[side, held], -1) for side in range(4)]
    turn = [turn_ref[side, held] for side in range(4)]
    for link in range(4):
        other = tiles_ref[partner(me, link, nx, ny)]
        for side in range(4):
            route[4 * link + side] = jnp.where((near[side] >= 0) & (near[side] == other), 1, 0)
    for side in range(4):
        target = (side + 2 + turn[side]) & 3
        for k in range(4):
            route[16 + 4 * side + k] = jnp.where((near[side] >= 0) & (near[side] == tile) & (target == k), 1, 0)
        route[32 + side] = jnp.where((target < 2) != (side >= 2), 1, 0)
        route[36 + side] = (4 - turn[side]) & 3
    route[40] = jnp.where(live, 1, 0)
    for i in range(41):
        route_ref[i:i + 1, :] = jnp.full((1, LANES), route[i], jnp.int32)
    for copy in copies:
        copy.wait()

    def chunk(ref, c):
        if c < CHUNKS - 1:
            return ref[:, c * LANES:(c + 1) * LANES]
        rest = CELLS - c * LANES
        part = ref[:, c * LANES:CELLS]
        return jnp.concatenate([part, jnp.zeros((8, LANES - rest), part.dtype)], axis=1)

    row, lane = rows(), lanes()
    both = []
    for step, ref in ((0, lines_ref), (1, inner_ref)):
        lines = []
        for value, wet in zip(raw_lines(lambda c: chunk(raw, c), step), raw_lines(lambda c: chunk(wet_raw, c), step)):
            wet = jnp.broadcast_to(wet[0:1], (8, LANES)).astype(jnp.float32)
            lines.append(jnp.where(row < 6, value * wet, jnp.where(row == 6, wet, 0.0)))
        for side in range(4):
            ref[8 * side:8 * side + 8, :] = lines[side]
        both.append(lines)
    ends = [jnp.where((lane == OWN_AT + 1) | (lane == OWN_AT + 2), TILE - 1, 0)] * 2
    corners = jnp.where(lane < OWN_AT + 2, pick(both[0][0], ends[0]), pick(both[0][2], ends[1]))
    at_corners = (lane >= OWN_AT) & (lane < OWN_AT + 4)
    sent = [sent_line(both[0][side], side, route, True) for side in range(4)]
    sent_inner = [sent_line(both[1][side], side, route, False) for side in range(4)]
    for link, pay in zip(BOTH, (pay0, pay1, pay2, pay3)):
        pay[0:8, :] = jnp.where(at_corners, corners, chosen(sent, route, link))
        pay[8:16, :] = chosen(sent_inner, route, link)


def pressure_of(tracer, row):
    return GRAVITY * jnp.where(row == 5, tracer + pltpu.roll(tracer, 1, 0), tracer)


def force_of(state, base, row):
    right, left, up, down, cell, column = neighbours(pressure_of(base, row))
    slope = jnp.where(row < 2, pltpu.roll(right - left, 4, 0), pltpu.roll(up - down, 6, 0))
    swapped = jnp.where(row < 2, pltpu.roll(state, 6, 0), -pltpu.roll(state, 2, 0))
    force = STEP_SIZE * (CORIOLIS * swapped - 0.5 * slope)
    return jnp.where(row < 4, wet_rows(state) * force, 0.0)


def masked_state(raw, wet_raw, state_ref):
    state_ref[:, (CHUNKS - 1) * LANES:] = jnp.zeros((8, LANES), jnp.float32)
    for low, high in ((0, (CHUNKS - 1) * LANES), ((CHUNKS - 1) * LANES, CELLS)):
        size = (8, high - low)
        row = lax.broadcasted_iota(jnp.int32, size, 0)
        wet = jnp.broadcast_to(wet_raw[0:1, low:high].astype(jnp.float32), size)
        state_ref[:, low:high] = jnp.where(row < 6, raw[:, low:high] * wet, jnp.where(row == 6, wet, 0.0))
    return state_ref[...]


def without_rims(state):
    right, left, up, down, cell, column = neighbours(state)
    first, second, wet = repeated(state, 0), repeated(state, 2), wet_rows(state)
    along = first * (right - left) + second * (up - down)
    round_sum = right + left + up + down - 4.0 * state
    return wet * (state - (0.5 * ADVECT) * along + DIFFUSE * round_sum), column


def if_live(route_ref, values):
    return jnp.where(tiled(Rows(route_ref)[40], CHUNKS) == 1, values, 0.0)


def base_kernel(raw, wet_raw, state_ref, base_ref, base_lines_ref):
    state = masked_state(raw, wet_raw, state_ref)
    base, column = without_rims(state)
    base_ref[...] = base
    lines = edge_lines(base, column)
    for side in range(4):
        base_lines_ref[8 * side:8 * side + 8, :] = lines[side]


def inner_kernel(shape, tiles_hbm, near_hbm, turn_hbm, halves_hbm, raw, wet_raw, route_ref,
                 almost_ref, plan_ref, flag, state_ref, tiles_ref, near_ref, turn_ref, halves_ref, table_ref, sems):
    copies = [pltpu.make_async_copy(tiles_hbm, tiles_ref, sems.at[0]),
              pltpu.make_async_copy(near_hbm, near_ref, sems.at[1]),
              pltpu.make_async_copy(turn_hbm, turn_ref, sems.at[2]),
              pltpu.make_async_copy(halves_hbm, halves_ref, sems.at[3]),
              pltpu.make_async_copy(near_hbm, table_ref.at[0:4], sems.at[4])]
    for copy in copies:
        copy.start()
    state = masked_state(raw, wet_raw, state_ref)
    base, _ = without_rims(state)
    almost_ref[...] = base
    for copy in copies:
        copy.wait()
    flag[0] = off_grid(shape, halves_ref, table_ref)
    corner_plan(shape, tiles_ref, near_ref, turn_ref, plan_ref)
    base = almost_ref[...]
    row = lax.broadcasted_iota(jnp.int32, (8, WIDE), 0)
    almost_ref[...] = if_live(route_ref, base + force_of(state_ref[...], base, row))


def off_grid(shape, halves_ref, table_ref):
    nx, ny = shape
    row, lane = rows(), lanes()
    tiles = [jnp.broadcast_to(halves_ref[half:half + 1, :], (8, LANES)) for half in range(2)]
    near = [table_ref[:, half * LANES:(half + 1) * LANES] for half in range(2)]

    def look(table, index):
        return jnp.where(index < LANES, pick(table[0], index & (LANES - 1)), pick(table[1], index & (LANES - 1)))

    worst = jnp.zeros((8, LANES), jnp.int32)
    for half in range(2):
        tile = tiles[half]
        mine = look(near, jnp.maximum(tile, 0))
        linked = (tile >= 0) & (mine >= 0) & (row < 4)
        other = [look(tiles, partner(lane + half * LANES, link, nx, ny)) for link in range(4)]
        over_x = (mine == other[1]) | (mine == other[3])
        kind = jnp.where(linked, jnp.where(mine == tile, 4, jnp.where(over_x, 1, 2)), 0)
        after = jnp.where(row < 3, pltpu.roll(kind, 7, 0), pltpu.roll(kind, 3, 0))
        odd = (kind == 4) | ((kind > 0) & (kind == after) & (row < 4))
        worst = jnp.where(odd, 1, worst)
    return jnp.max(worst)


def corner_plan(shape, tiles_ref, near_ref, turn_ref, plan_ref):
    nx, ny = shape
    me = my_index(ny)
    tile = tiles_ref[me]
    held = jnp.maximum(tile, 0)
    across = [partner(me, link, nx, ny) for link in range(4)]
    relayed = [(which, RELAY_AT[u], tiles_ref[partner(across[x], u, nx, ny)])
               for which, x in ((1, 1), (2, 3)) for u in (0, 2)]
    for link in range(4):
        other = tiles_ref[across[link]]
        side = jnp.int32(-1)
        for k in range(4):
            side = jnp.where((tile >= 0) & (other >= 0) & (near_ref[k, held] == other), k, side)
        facing = (side + 2 + turn_ref[jnp.maximum(side, 0), held]) & 3
        there = jnp.maximum(other, 0)
        for end in range(2):
            later = (side < 2) == (end == 0)
            lateral = jnp.where(later, facing + 1, facing + 3) & 3
            beyond = jnp.where(side >= 0, near_ref[lateral, there], -1)
            back = (lateral + 2 + turn_ref[lateral, there]) & 3
            corner = jnp.where(later, back + 1, back) & 3
            buffer, lane = jnp.int32(0), jnp.int32(0)
            for which, base, name in relayed:
                here = (beyond >= 0) & (beyond == name)
                buffer, lane = jnp.where(here, which, buffer), jnp.where(here, base + corner, lane)
            at = 2 * (2 * link + end)
            plan_ref[at:at + 1, :] = jnp.full((1, LANES), buffer, jnp.int32)
            plan_ref[at + 1:at + 2, :] = jnp.full((1, LANES), lane, jnp.int32)


def relay_kernel(pay0, pay1, came0, came1, after, out0, out1):
    lane = lanes()
    for pay, out in ((pay0, out0), (pay1, out1)):
        line = pay[0:8, :]
        for link, came in zip(U_ORDER, (came0, came1)):
            moved = pltpu.roll(came[0:8, :], RELAY_AT[link] - OWN_AT, 1)
            line = jnp.where((lane >= RELAY_AT[link]) & (lane < RELAY_AT[link] + 4), moved, line)
        out[0:8, :] = line
        out[8:16, :] = pay[8:16, :]


def edge_patches(lines, rims):
    patch = []
    for side in range(4):
        drift = repeated(lines[side], 0 if side % 2 == 1 else 2)
        sign = 1.0 if side in (1, 2) else -1.0
        patch.append(wet_rows(lines[side]) * (DIFFUSE - (sign * 0.5 * ADVECT) * drift) * rims[side])
    return patch


def with_ends(patch):
    south, east, north, west = patch
    end = TILE - 1
    return [
        south + at_ends(west, 0, 0) + at_ends(east, 0, end),
        east + at_ends(south, end, 0) + at_ends(north, end, end),
        north + at_ends(west, end, 0) + at_ends(east, end, end),
        west + at_ends(south, 0, 0) + at_ends(north, 0, end),
    ]


def pressure_at(tracer, shift, row):
    return GRAVITY * (pltpu.roll(tracer, shift, 0)
                      + jnp.where(row == (5 + shift) % 8, pltpu.roll(tracer, shift + 1, 0), 0.0))


def final_kernel(route_ref, plan_ref, lines_ref, inner_ref, almost_ref, first, second, third, fourth, out_ref, full, sems):
    lane, row = lanes(), rows()
    route, plan = Rows(route_ref), Rows(plan_ref)
    came = by_link((first, second, third, fourth), BOTH)
    outer = [came[link][0:8, :] for link in range(4)]
    ends = []
    for end in range(2):
        values = []
        for link in range(4):
            which, lane_from = plan[2 * (2 * link + end)], plan[2 * (2 * link + end) + 1]
            held = jnp.where(which == 2, outer[3], outer[1])
            values.append(jnp.where(which > 0, pick(held, lane_from), 0.0))
        ends.append(rims_of(route, None, values))
    rims = rims_of(route, None, outer)
    beyond = rims_of(route, None, [came[link][8:16, :] for link in range(4)])
    lines, inner = four_of(lines_ref), four_of(inner_ref)
    patch = edge_patches(lines, rims)
    kept = [jnp.where(lane < TILE, one, 0.0) for one in patch]
    across = [pressure_at(kept[side], 4 if side % 2 == 1 else 6, row) for side in range(4)]
    crossing = ((3, 1, 0), (0, 2, TILE - 1), (3, 1, TILE - 1), (0, 2, 0))
    on_edge, inside = [], []
    for side in range(4):
        sign = 1.0 if side in (1, 2) else -1.0
        line, wet, wet_in = rims[side], wet_rows(lines[side]), wet_rows(inner[side])
        after = jnp.where(lane == TILE - 1, ends[1][side], pltpu.roll(line, LANES - 1, 1))
        before = jnp.where(lane == 0, ends[0][side], pltpu.roll(line, 1, 1))
        upper, lower = pltpu.roll(line, 4, 0), pltpu.roll(line, 2, 0)
        normal, tangent = (upper, lower) if side % 2 == 1 else (lower, upper)
        along = normal * (sign * (beyond[side] - lines[side])) + tangent * (after - before)
        round_sum = after + before + beyond[side] + lines[side] - 4.0 * line
        tracer = wet_rows(line) * (line - (0.5 * ADVECT) * along + DIFFUSE * round_sum)
        to_normal, to_tangent = (4, 6) if side % 2 == 1 else (6, 4)
        own_row = row < 2 if side % 2 == 1 else (row >= 2) & (row < 4)
        cross_row = (row >= 2) & (row < 4) if side % 2 == 1 else row < 2
        cross = pressure_at(kept[side], to_tangent, row)
        start, stop, lane_there = crossing[side]
        drop = pltpu.roll(cross, LANES - 1, 1) - pltpu.roll(cross, 1, 1)
        drop = drop + at_ends(across[stop], lane_there, TILE - 2) - at_ends(across[start], lane_there, 1)
        push = jnp.where(own_row, sign * pressure_at(tracer, to_normal, row), 0.0)
        push = jnp.where(cross_row, drop, push)
        on_edge.append(patch[side] - (0.5 * STEP_SIZE) * wet * push)
        between = own_row & (lane > 0) & (lane < TILE - 1)
        inside.append(jnp.where(between, (-sign * 0.5 * STEP_SIZE) * wet_in * across[side], 0.0))
    edges, seconds = spread_chunks(on_edge, 0), spread_chunks(inside, 1)
    copies = []
    for low, high in ((0, 24), (24, CHUNKS)):
        for c in range(low, high):
            cut = slice(c * LANES, min((c + 1) * LANES, CELLS))
            width = cut.stop - cut.start
            full[:, cut] = (almost_ref[:, c * LANES:(c + 1) * LANES] + (edges[c] + seconds[c]))[:, :width]
        cells = pl.ds(low * LANES, min(high * LANES, CELLS) - low * LANES)
        copies.append(pltpu.make_async_copy(full.at[0:6, cells], out_ref.at[:, 0, cells], sems.at[len(copies)]))
        copies[-1].start()
    for copy in copies:
        copy.wait()


def write_out(full, out_ref, sems):
    copies = [pltpu.make_async_copy(full.at[c], out_ref.at[c, 0], sems.at[c]) for c in range(6)]
    for copy in copies:
        copy.start()
    for copy in copies:
        copy.wait()


def at_ends(line, lane_from, lane_to):
    value = jnp.broadcast_to(line[:, lane_from:lane_from + 1], (8, LANES))
    return jnp.where(lanes() == lane_to, value, 0.0)


def edge_kernel(route_ref, lines_ref, base_lines_ref, came0, came1, came2, came3,
                patch_ref, own_two_ref, pay0, pay1, pay2, pay3):
    route = Rows(route_ref)
    lines, base = four_of(lines_ref), four_of(base_lines_ref)
    own = own_rims([sent_line(lines[side], side, route, True) for side in range(4)], route)
    rims = rims_of(route, own, [came[0:8, :] for came in by_link((came0, came1, came2, came3), BOTH)])
    patch = edge_patches(lines, rims)
    whole = with_ends(patch)
    press = []
    for side in range(4):
        patch_ref[8 * side:8 * side + 8, :] = patch[side]
        press.append(sent_line(pressure_of(base[side] + whole[side], rows()), side, route, False))
    for link, pay in zip(SECOND_ORDER, (pay0, pay1, pay2, pay3)):
        pay[...] = chosen(press, route, link)
    own = own_rims(press, route)
    for side in range(4):
        own_two_ref[8 * side:8 * side + 8, :] = own[side]


def middle_kernel(route_ref, state_ref, base_ref, patch_ref, out_ref):
    state = state_ref[...]
    cell, column = column_of()
    base = base_ref[...] + spread(four_of(patch_ref), cell, column)
    row = lax.broadcasted_iota(jnp.int32, (8, WIDE), 0)
    out_ref[...] = if_live(route_ref, base + force_of(state, base, row))


def last_kernel(route_ref, lines_ref, own_ref, almost_ref, came0, came1, came2, came3, out_ref, full, sems):
    route = Rows(route_ref)
    rims = rims_of(route, four_of(own_ref), [came[...] for came in by_link((came0, came1, came2, came3), SECOND_ORDER)])
    patch = []
    for side in range(4):
        wet = wet_rows(lines_ref[8 * side:8 * side + 8, :])
        row = rows()
        rim = pltpu.roll(rims[side], 4 if side % 2 == 1 else 6, 0)
        mine = row < 2 if side % 2 == 1 else (row >= 2) & (row < 4)
        sign = -1.0 if side in (1, 2) else 1.0
        patch.append(jnp.where(mine, (sign * 0.5 * STEP_SIZE) * wet * rim, 0.0))
    cell, column = column_of()
    full[...] = (almost_ref[...] + spread(patch, cell, column))[:, :CELLS]
    write_out(full, out_ref, sems)


def sds(*shape, dtype=jnp.float32):
    return jax.ShapeDtypeStruct(shape, dtype)


PARAMS = pltpu.CompilerParams(vmem_limit_bytes=16 * 1024 * 1024)


def on_device(nx, ny, fields, wet_mask, tile_of_slot, neighbor, rotation):
    line, pair, four, wide = sds(8, LANES), sds(16, LANES), sds(32, LANES), sds(8, WIDE)
    scalars = pltpu.SMEM((4, nx * ny), jnp.int32)
    tables = [pltpu.with_memory_space_constraint(v, pltpu.HBM) for v in (tile_of_slot, neighbor.T, rotation.T)]
    inputs = [pltpu.with_memory_space_constraint(v, pltpu.HBM) for v in (fields.reshape(6, 1, CELLS), wet_mask)]
    halves = pltpu.with_memory_space_constraint(tile_of_slot.reshape(2, LANES), pltpu.HBM)
    raw, wet_raw, lines, inner, *pays, route = pl.pallas_call(
        lambda *refs: load_kernel((nx, ny), *refs),
        out_shape=[sds(8, CELLS), sds(8, CELLS, dtype=jnp.int32), four, four, pair, pair, pair, pair,
                   sds(ROUTE, LANES, dtype=jnp.int32)],
        in_specs=[HBM] * 5,
        out_specs=[VMEM] * 9,
        scratch_shapes=[pltpu.SMEM((nx * ny,), jnp.int32), scalars, scalars, pltpu.SemaphoreType.DMA((12,))],
        compiler_params=PARAMS, name="load",
    )(*tables, *inputs)
    came_u = exchanged(pays[:2], U_ORDER, nx, ny)
    almost, plan, flag = pl.pallas_call(
        lambda *refs: inner_kernel((nx, ny), *refs),
        out_shape=[wide, sds(16, LANES, dtype=jnp.int32), sds(1, dtype=jnp.int32)],
        in_specs=[HBM] * 4 + [VMEM] * 3, out_specs=[VMEM, VMEM, SMEM],
        scratch_shapes=[pltpu.VMEM((8, WIDE), jnp.float32), pltpu.SMEM((nx * ny,), jnp.int32), scalars, scalars,
                        pltpu.VMEM((2, LANES), jnp.int32), pltpu.VMEM((8, nx * ny), jnp.int32),
                        pltpu.SemaphoreType.DMA((5,))],
        compiler_params=PARAMS, name="inner",
        cost_estimate=pl.CostEstimate(flops=2000000, bytes_accessed=800000, transcendentals=0),
    )(*tables, halves, raw, wet_raw, route)
    sent = pl.pallas_call(
        relay_kernel, out_shape=[pair, pair], in_specs=[VMEM] * 4 + [ANY], out_specs=[VMEM] * 2,
        compiler_params=PARAMS, name="relay",
    )(*pays[2:], *came_u, almost)
    came_x = exchanged(sent, X_ORDER, nx, ny)
    result = pltpu.HBM((6, 1, CELLS), jnp.float32)
    writing = [pltpu.VMEM((8, CELLS), jnp.float32), pltpu.SemaphoreType.DMA((12,))]

    def grid_like():
        return pl.pallas_call(
            final_kernel, out_shape=result, in_specs=[VMEM] * 9, out_specs=HBM,
            scratch_shapes=writing, compiler_params=PARAMS, name="final",
        )(route, plan, lines, inner, almost, *came_u, *came_x)

    def general():
        came = came_u + came_x
        state, base, base_lines = pl.pallas_call(
            base_kernel, out_shape=[wide, wide, four], in_specs=[VMEM] * 2, out_specs=[VMEM] * 3,
            compiler_params=PARAMS, name="base",
            cost_estimate=pl.CostEstimate(flops=2000000, bytes_accessed=800000, transcendentals=0),
        )(raw, wet_raw)
        patch, own_two, *press = pl.pallas_call(
            edge_kernel, out_shape=[four, four, line, line, line, line],
            in_specs=[VMEM] * 7, out_specs=[VMEM] * 6,
            compiler_params=PARAMS, name="edge",
        )(route, lines, base_lines, *came)
        came_two = exchanged(press, SECOND_ORDER, nx, ny)
        nearly = pl.pallas_call(
            middle_kernel, out_shape=wide, in_specs=[VMEM] * 4, out_specs=VMEM,
            compiler_params=PARAMS, name="middle",
            cost_estimate=pl.CostEstimate(flops=2000000, bytes_accessed=800000, transcendentals=0),
        )(route, state, base, patch)
        return pl.pallas_call(
            last_kernel, out_shape=result, in_specs=[VMEM] * 8, out_specs=HBM,
            scratch_shapes=writing, compiler_params=PARAMS, name="last",
        )(route, lines, own_two, nearly, *came_two)

    out = lax.switch(flag[0], [grid_like, general])
    return out.reshape(1, 6, CELLS)


def solution(mesh):
    nx, ny = mesh.shape["gx"], mesh.shape["gy"]
    in_specs = (P(AXES, None, None), P(AXES, None), P(), P(), P())
    return jax.shard_map(lambda *args: on_device(nx, ny, *args), mesh=mesh, in_specs=in_specs,
                         out_specs=P(AXES, None, None), check_vma=False)
```

```python
import jax
import jax.numpy as jnp
from jax import lax
from jax.experimental import pallas as pl
from jax.experimental.pallas import tpu as pltpu
from jax.sharding import PartitionSpec as P

TILE = 90
CELLS = TILE * TILE
LANES = 128
CHUNKS = 64
WIDE = LANES * CHUNKS
HALF = 45
LAST = CELLS - TILE - (CHUNKS - 2) * LANES

ADVECT = 0.25
DIFFUSE = 0.15
STEP_SIZE = 0.5
CORIOLIS = 0.3
GRAVITY = 0.8

AXES = ("gx", "gy")
VMEM = pl.BlockSpec(memory_space=pltpu.VMEM)
SMEM = pl.BlockSpec(memory_space=pltpu.SMEM)
ANY = pl.BlockSpec(memory_space=pl.ANY)
HBM = pl.BlockSpec(memory_space=pltpu.HBM)


def over(value, count):
    return value >> (count.bit_length() - 1) if count & (count - 1) == 0 else value // count


def rest(value, count):
    return value & (count - 1) if count & (count - 1) == 0 else value % count


def link_x_even(x, y, nx, ny):
    return x ^ 1, y


def link_x_odd(x, y, nx, ny):
    return (((x + nx - 1) % nx ^ 1) + 1) % nx, y


def link_y_even(x, y, nx, ny):
    return x, y ^ 1


def link_y_odd(x, y, nx, ny):
    if y == 0 or y == ny - 1:
        return (x + nx // 2) % nx, y
    return x, ((y - 1) ^ 1) + 1


def swapped(x, nx):
    column = rest(x, nx // 2)
    return (column == 0) | (column == 2)


def link_u_first(x, y, nx, ny):
    return (link_y_even if swapped(x, nx) else link_y_odd)(x, y, nx, ny)


def link_u_second(x, y, nx, ny):
    return (link_y_odd if swapped(x, nx) else link_y_even)(x, y, nx, ny)


LINKS = (link_u_first, link_x_even, link_u_second, link_x_odd)


def pairs_of(link, nx, ny):
    out = []
    for x in range(nx):
        for y in range(ny):
            to_x, to_y = link(x, y, nx, ny)
            out.append((x * ny + y, to_x * ny + to_y))
    return out


U_ORDER = (0, 2)
X_ORDER = (3, 1)
BOTH = U_ORDER + X_ORDER
SECOND_ORDER = (2, 0, 3, 1)


def exchanged(pays, order, nx, ny):
    return [lax.ppermute(pay, AXES, pairs_of(LINKS[link], nx, ny)) for pay, link in zip(pays, order)]


def by_link(refs, order, links=(0, 1, 2, 3)):
    return [refs[order.index(link)] for link in links]


def partner(me, which, nx, ny):
    x, y = over(me, ny), rest(me, ny)
    if which == 1:
        return me + jnp.where(rest(x, 2) == 0, ny, -ny)
    if which == 3:
        return rest(me + jnp.where(rest(x, 2) == 1, ny, (nx - 1) * ny), nx * ny)
    even = me + jnp.where(rest(y, 2) == 0, 1, -1)
    pole = (y == 0) | (y == ny - 1)
    odd = jnp.where(pole, rest(me + nx // 2 * ny, nx * ny), me + jnp.where(rest(y, 2) == 1, 1, -1))
    return jnp.where(swapped(x, nx), even, odd) if which == 0 else jnp.where(swapped(x, nx), odd, even)


def lanes():
    return lax.broadcasted_iota(jnp.int32, (8, LANES), 1)


def rows():
    return lax.broadcasted_iota(jnp.int32, (8, LANES), 0)


def pick(values, index):
    return jnp.take_along_axis(values, index, axis=1)


def tiled(values, count):
    return jnp.concatenate([values] * count, axis=1)


def column_of():
    cell = lax.broadcasted_iota(jnp.int32, (8, WIDE), 1)
    line = jnp.floor((cell.astype(jnp.float32) + 0.5) * (1.0 / TILE)).astype(jnp.int32)
    return cell, cell - TILE * line


def edge_lines(state, column):
    lane = lanes()
    edge = (column == 0) | (column == TILE - 1)
    parts = []
    for low, high in ((0, HALF), (HALF, CHUNKS)):
        found = jnp.zeros((8, LANES), jnp.float32)
        for c in range(low, high):
            cut = slice(c * LANES, (c + 1) * LANES)
            found = jnp.where(edge[:, cut], state[:, cut], found)
        parts.append(found)
    east_at = (TILE * lane + TILE - 1) & (LANES - 1)
    west_at = (TILE * lane) & (LANES - 1)
    east = jnp.where(lane < 64, pick(parts[0], east_at), pick(parts[1], east_at))
    west = jnp.where(lane < 64, pick(parts[0], west_at), pick(parts[1], west_at))
    south = state[:, :LANES]
    before = pltpu.roll(state[:, (CHUNKS - 2) * LANES:(CHUNKS - 1) * LANES], LANES - LAST, 1)
    after = pltpu.roll(state[:, (CHUNKS - 1) * LANES:], LANES - LAST, 1)
    north = jnp.where(lane < LANES - LAST, before, after)
    return [south, east, north, west]


def spread(lines, cell, column):
    south, east, north, west = lines
    lane = lanes()
    odd = (lane & 1) == 1
    line_at = (37 * ((lane + jnp.where(odd, 39, 0)) >> 1)) & 63
    early = jnp.where(odd, pick(east, line_at), pick(west, line_at))
    late = jnp.where(odd, pick(east, line_at + 64), pick(west, line_at + 64))
    sides = jnp.concatenate([early] * HALF + [late] * (CHUNKS - HALF), axis=1)
    edge = (column == 0) | (column == TILE - 1)
    out = jnp.where(edge, sides, 0.0)
    first = jnp.where(lane < TILE, south, 0.0) + out[:, :LANES]
    moved = pltpu.roll(north, LAST, 1)
    before = out[:, (CHUNKS - 2) * LANES:(CHUNKS - 1) * LANES] + jnp.where(lane >= LAST, moved, 0.0)
    after = out[:, (CHUNKS - 1) * LANES:] + jnp.where(lane < LAST + TILE - LANES, moved, 0.0)
    return jnp.concatenate([first, out[:, LANES:(CHUNKS - 2) * LANES], before, after], axis=1)


def neighbours(state):
    cell, column = column_of()
    right = jnp.where(column == TILE - 1, 0.0, pltpu.roll(state, WIDE - 1, 1))
    left = jnp.where(column == 0, 0.0, pltpu.roll(state, 1, 1))
    up = jnp.where(cell >= CELLS - TILE, 0.0, pltpu.roll(state, WIDE - TILE, 1))
    down = jnp.where(cell < TILE, 0.0, pltpu.roll(state, TILE, 1))
    return right, left, up, down, cell, column


def row_of(values):
    return lax.broadcasted_iota(jnp.int32, values.shape, 0)


def repeated(values, first):
    row = row_of(values)
    if first == 0:
        pair = jnp.where(row < 2, values, pltpu.roll(values, 2, 0))
    else:
        pair = jnp.where(row < 4, values, pltpu.roll(values, 2, 0))
        pair = jnp.where(row < 2, pltpu.roll(values, 6, 0), pair)
        return pair
    return jnp.where(row < 4, pair, pltpu.roll(values, 4, 0))


def wet_rows(values):
    return jnp.broadcast_to(values[6:7], values.shape)


def turned(line, turns):
    row = row_of(line)
    swapped = jnp.where(row < 2, pltpu.roll(line, 6, 0), pltpu.roll(line, 2, 0))
    velocity = row < 4
    second = jnp.where(row < 2, swapped, -swapped)
    odd = jnp.where(turns % 2 == 1, 1, 0)
    out = jnp.where(jnp.logical_and(velocity, odd == 1), second, line)
    back = jnp.where(turns >= 2, 1, 0)
    return jnp.where(jnp.logical_and(velocity, back == 1), -out, out)


def flipped(line):
    return pick(line, jnp.maximum(TILE - 1 - lanes(), 0))


ROUTE = 48
OWN_AT, RELAY_AT = TILE, {0: TILE + 4, 2: TILE + 8}


class Rows:
    def __init__(self, ref):
        self.ref = ref

    def __getitem__(self, i):
        return jnp.broadcast_to(self.ref[i:i + 1, :], (8, LANES))


def my_index(ny):
    return lax.axis_index("gx") * ny + lax.axis_index("gy")


def sent_line(line, side, route, vector):
    line = jnp.where(route[32 + side] == 1, flipped(line), line)
    return turned(line, route[36 + side]) if vector else line


def chosen(lines, route, link):
    total = jnp.zeros((8, LANES), jnp.float32)
    for side in range(4):
        total = jnp.where(route[4 * link + side] == 1, lines[side], total)
    return total


def own_rims(sent, route):
    out = []
    for target in range(4):
        total = jnp.zeros((8, LANES), jnp.float32)
        for side in range(4):
            total = jnp.where(route[16 + 4 * side + target] == 1, sent[side], total)
        out.append(total)
    return out


def rims_of(route, base, came):
    out = []
    for side in range(4):
        rim = base[side] if base is not None else jnp.zeros((8, LANES), jnp.float32)
        for link in range(4):
            rim = jnp.where(route[4 * link + side] == 1, came[link], rim)
        out.append(rim)
    return out


def four_of(ref):
    return [ref[8 * side:8 * side + 8, :] for side in range(4)]


def columns_at(step):
    lane = lanes()
    odd = lane & 1
    shift = jnp.where(odd == 1, 39 + step, -step) if step % 2 == 0 else jnp.where(odd == 1, -step, 39 + step)
    column = jnp.where(odd == 1, TILE - 1 - step, step) if step % 2 == 0 else jnp.where(odd == 1, step, TILE - 1 - step)
    line_at = (37 * ((lane + shift) >> 1)) & 63
    return line_at, (TILE * line_at + column) >> 7


def raw_lines(chunk_of, step):
    lane = lanes()
    _, home = columns_at(step)
    parts = []
    for low, high in ((0, HALF), (HALF, CHUNKS)):
        found = chunk_of(low)
        for c in range(low + 1, high):
            found = jnp.where(home == c - low, chunk_of(c), found)
        parts.append(found)
    early = lane < 64
    out = [None] * 4
    for side, column in ((1, TILE - 1 - step), (3, step)):
        at = (TILE * lane + column) & (LANES - 1)
        out[side] = jnp.where(early, pick(parts[0], at), pick(parts[1], at))
    for side, first in ((0, TILE * step), (2, CELLS - TILE - TILE * step)):
        low, start = first // LANES, first % LANES
        if start == 0:
            out[side] = chunk_of(low)
        else:
            before = pltpu.roll(chunk_of(low), LANES - start, 1)
            after = pltpu.roll(chunk_of(low + 1), LANES - start, 1)
            out[side] = jnp.where(lane < LANES - start, before, after)
    return out


def spread_chunks(lines, step):
    lane = lanes()
    line_at, home = columns_at(step)
    odd = (lane & 1) == 1
    first_odd, first_even = (lines[1], lines[3]) if step % 2 == 0 else (lines[3], lines[1])
    early = jnp.where(odd, pick(first_odd, line_at), pick(first_even, line_at))
    late = jnp.where(odd, pick(first_odd, line_at + 64), pick(first_even, line_at + 64))
    out = []
    for c in range(CHUNKS):
        out.append(jnp.where(home == (c if c < HALF else c - HALF), early if c < HALF else late, 0.0))
    for side, first in ((0, TILE * step), (2, CELLS - TILE - TILE * step)):
        low, start = first // LANES, first % LANES
        line = jnp.where(lane < TILE, lines[side], 0.0)
        if start == 0:
            out[low] = out[low] + line
        else:
            moved = pltpu.roll(line, start, 1)
            out[low] = out[low] + jnp.where(lane >= start, moved, 0.0)
            if start + TILE > LANES:
                out[low + 1] = out[low + 1] + jnp.where(lane < start + TILE - LANES, moved, 0.0)
    return out


def load_kernel(shape, tiles_hbm, near_hbm, turn_hbm, fields_ref, wet_ref,
                raw, wet_raw, lines_ref, inner_ref, pay0, pay1, pay2, pay3, route_ref,
                tiles_ref, near_ref, turn_ref, sems):
    nx, ny = shape
    tables = [pltpu.make_async_copy(tiles_hbm, tiles_ref, sems.at[7]),
              pltpu.make_async_copy(near_hbm, near_ref, sems.at[8]),
              pltpu.make_async_copy(turn_hbm, turn_ref, sems.at[9])]
    copies = [pltpu.make_async_copy(fields_ref.at[:, 0], raw.at[0:6], sems.at[0])]
    copies.append(pltpu.make_async_copy(wet_ref.at[0], wet_raw.at[0], sems.at[6]))
    for copy in tables + copies:
        copy.start()
    for copy in tables:
        copy.wait()
    me = my_index(ny)
    route = [None] * ROUTE
    tile = tiles_ref[me]
    live = tile >= 0
    held = jnp.maximum(tile, 0)
    near = [jnp.where(live, near_ref[side, held], -1) for side in range(4)]
    turn = [turn_ref[side, held] for side in range(4)]
    for link in range(4):
        other = tiles_ref[partner(me, link, nx, ny)]
        for side in range(4):
            route[4 * link + side] = jnp.where((near[side] >= 0) & (near[side] == other), 1, 0)
    for side in range(4):
        target = (side + 2 + turn[side]) & 3
        for k in range(4):
            route[16 + 4 * side + k] = jnp.where((near[side] >= 0) & (near[side] == tile) & (target == k), 1, 0)
        route[32 + side] = jnp.where((target < 2) != (side >= 2), 1, 0)
        route[36 + side] = (4 - turn[side]) & 3
    route[40] = jnp.where(live, 1, 0)
    for i in range(41):
        route_ref[i:i + 1, :] = jnp.full((1, LANES), route[i], jnp.int32)
    for copy in copies:
        copy.wait()

    def chunk(ref, c):
        if c < CHUNKS - 1:
            return ref[:, c * LANES:(c + 1) * LANES]
        rest = CELLS - c * LANES
        part = ref[:, c * LANES:CELLS]
        return jnp.concatenate([part, jnp.zeros((8, LANES - rest), part.dtype)], axis=1)

    row, lane = rows(), lanes()
    both = []
    for step, ref in ((0, lines_ref), (1, inner_ref)):
        lines = []
        for value, wet in zip(raw_lines(lambda c: chunk(raw, c), step), raw_lines(lambda c: chunk(wet_raw, c), step)):
            wet = jnp.broadcast_to(wet[0:1], (8, LANES)).astype(jnp.float32)
            lines.append(jnp.where(row < 6, value * wet, jnp.where(row == 6, wet, 0.0)))
        for side in range(4):
            ref[8 * side:8 * side + 8, :] = lines[side]
        both.append(lines)
    ends = [jnp.where((lane == OWN_AT + 1) | (lane == OWN_AT + 2), TILE - 1, 0)] * 2
    corners = jnp.where(lane < OWN_AT + 2, pick(both[0][0], ends[0]), pick(both[0][2], ends[1]))
    at_corners = (lane >= OWN_AT) & (lane < OWN_AT + 4)
    sent = [sent_line(both[0][side], side, route, True) for side in range(4)]
    sent_inner = [sent_line(both[1][side], side, route, False) for side in range(4)]
    for link, pay in zip(BOTH, (pay0, pay1, pay2, pay3)):
        pay[0:8, :] = jnp.where(at_corners, corners, chosen(sent, route, link))
        pay[8:16, :] = chosen(sent_inner, route, link)


def pressure_of(tracer, row):
    return GRAVITY * jnp.where(row == 5, tracer + pltpu.roll(tracer, 1, 0), tracer)


def force_of(state, base, row):
    right, left, up, down, cell, column = neighbours(pressure_of(base, row))
    slope = jnp.where(row < 2, pltpu.roll(right - left, 4, 0), pltpu.roll(up - down, 6, 0))
    swapped = jnp.where(row < 2, pltpu.roll(state, 6, 0), -pltpu.roll(state, 2, 0))
    force = STEP_SIZE * (CORIOLIS * swapped - 0.5 * slope)
    return jnp.where(row < 4, wet_rows(state) * force, 0.0)


def masked_state(raw, wet_raw, state_ref):
    state_ref[:, (CHUNKS - 1) * LANES:] = jnp.zeros((8, LANES), jnp.float32)
    for low, high in ((0, (CHUNKS - 1) * LANES), ((CHUNKS - 1) * LANES, CELLS)):
        size = (8, high - low)
        row = lax.broadcasted_iota(jnp.int32, size, 0)
        wet = jnp.broadcast_to(wet_raw[0:1, low:high].astype(jnp.float32), size)
        state_ref[:, low:high] = jnp.where(row < 6, raw[:, low:high] * wet, jnp.where(row == 6, wet, 0.0))
    return state_ref[...]


def without_rims(state):
    right, left, up, down, cell, column = neighbours(state)
    first, second, wet = repeated(state, 0), repeated(state, 2), wet_rows(state)
    along = first * (right - left) + second * (up - down)
    round_sum = right + left + up + down - 4.0 * state
    return wet * (state - (0.5 * ADVECT) * along + DIFFUSE * round_sum), column


def if_live(route_ref, values):
    return jnp.where(tiled(Rows(route_ref)[40], CHUNKS) == 1, values, 0.0)


def base_kernel(raw, wet_raw, state_ref, base_ref, base_lines_ref):
    state = masked_state(raw, wet_raw, state_ref)
    base, column = without_rims(state)
    base_ref[...] = base
    lines = edge_lines(base, column)
    for side in range(4):
        base_lines_ref[8 * side:8 * side + 8, :] = lines[side]


def inner_kernel(shape, tiles_hbm, near_hbm, turn_hbm, halves_hbm, raw, wet_raw, route_ref,
                 almost_ref, plan_ref, flag, state_ref, tiles_ref, near_ref, turn_ref, halves_ref, table_ref, sems):
    copies = [pltpu.make_async_copy(tiles_hbm, tiles_ref, sems.at[0]),
              pltpu.make_async_copy(near_hbm, near_ref, sems.at[1]),
              pltpu.make_async_copy(turn_hbm, turn_ref, sems.at[2]),
              pltpu.make_async_copy(halves_hbm, halves_ref, sems.at[3]),
              pltpu.make_async_copy(near_hbm, table_ref.at[0:4], sems.at[4])]
    for copy in copies:
        copy.start()
    state = masked_state(raw, wet_raw, state_ref)
    base, _ = without_rims(state)
    almost_ref[...] = base
    for copy in copies:
        copy.wait()
    flag[0] = off_grid(shape, halves_ref, table_ref)
    corner_plan(shape, tiles_ref, near_ref, turn_ref, plan_ref)
    base = almost_ref[...]
    row = lax.broadcasted_iota(jnp.int32, (8, WIDE), 0)
    almost_ref[...] = if_live(route_ref, base + force_of(state_ref[...], base, row))


def off_grid(shape, halves_ref, table_ref):
    nx, ny = shape
    row, lane = rows(), lanes()
    tiles = [jnp.broadcast_to(halves_ref[half:half + 1, :], (8, LANES)) for half in range(2)]
    near = [table_ref[:, half * LANES:(half + 1) * LANES] for half in range(2)]

    def look(table, index):
        return jnp.where(index < LANES, pick(table[0], index & (LANES - 1)), pick(table[1], index & (LANES - 1)))

    worst = jnp.zeros((8, LANES), jnp.int32)
    for half in range(2):
        tile = tiles[half]
        mine = look(near, jnp.maximum(tile, 0))
        linked = (tile >= 0) & (mine >= 0) & (row < 4)
        other = [look(tiles, partner(lane + half * LANES, link, nx, ny)) for link in range(4)]
        over_x = (mine == other[1]) | (mine == other[3])
        kind = jnp.where(linked, jnp.where(mine == tile, 4, jnp.where(over_x, 1, 2)), 0)
        after = jnp.where(row < 3, pltpu.roll(kind, 7, 0), pltpu.roll(kind, 3, 0))
        odd = (kind == 4) | ((kind > 0) & (kind == after) & (row < 4))
        worst = jnp.where(odd, 1, worst)
    return jnp.max(worst)


def corner_plan(shape, tiles_ref, near_ref, turn_ref, plan_ref):
    nx, ny = shape
    me = my_index(ny)
    tile = tiles_ref[me]
    held = jnp.maximum(tile, 0)
    across = [partner(me, link, nx, ny) for link in range(4)]
    relayed = [(which, RELAY_AT[u], tiles_ref[partner(across[x], u, nx, ny)])
               for which, x in ((1, 1), (2, 3)) for u in (0, 2)]
    for link in range(4):
        other = tiles_ref[across[link]]
        side = jnp.int32(-1)
        for k in range(4):
            side = jnp.where((tile >= 0) & (other >= 0) & (near_ref[k, held] == other), k, side)
        facing = (side + 2 + turn_ref[jnp.maximum(side, 0), held]) & 3
        there = jnp.maximum(other, 0)
        for end in range(2):
            later = (side < 2) == (end == 0)
            lateral = jnp.where(later, facing + 1, facing + 3) & 3
            beyond = jnp.where(side >= 0, near_ref[lateral, there], -1)
            back = (lateral + 2 + turn_ref[lateral, there]) & 3
            corner = jnp.where(later, back + 1, back) & 3
            buffer, lane = jnp.int32(0), jnp.int32(0)
            for which, base, name in relayed:
                here = (beyond >= 0) & (beyond == name)
                buffer, lane = jnp.where(here, which, buffer), jnp.where(here, base + corner, lane)
            at = 2 * (2 * link + end)
            plan_ref[at:at + 1, :] = jnp.full((1, LANES), buffer, jnp.int32)
            plan_ref[at + 1:at + 2, :] = jnp.full((1, LANES), lane, jnp.int32)


def relay_kernel(pay0, pay1, came0, came1, after, out0, out1):
    lane = lanes()
    for pay, out in ((pay0, out0), (pay1, out1)):
        line = pay[0:8, :]
        for link, came in zip(U_ORDER, (came0, came1)):
            moved = pltpu.roll(came[0:8, :], RELAY_AT[link] - OWN_AT, 1)
            line = jnp.where((lane >= RELAY_AT[link]) & (lane < RELAY_AT[link] + 4), moved, line)
        out[0:8, :] = line
        out[8:16, :] = pay[8:16, :]


def edge_patches(lines, rims):
    patch = []
    for side in range(4):
        drift = repeated(lines[side], 0 if side % 2 == 1 else 2)
        sign = 1.0 if side in (1, 2) else -1.0
        patch.append(wet_rows(lines[side]) * (DIFFUSE - (sign * 0.5 * ADVECT) * drift) * rims[side])
    return patch


def with_ends(patch):
    south, east, north, west = patch
    end = TILE - 1
    return [
        south + at_ends(west, 0, 0) + at_ends(east, 0, end),
        east + at_ends(south, end, 0) + at_ends(north, end, end),
        north + at_ends(west, end, 0) + at_ends(east, end, end),
        west + at_ends(south, 0, 0) + at_ends(north, 0, end),
    ]


def pressure_at(tracer, shift, row):
    return GRAVITY * (pltpu.roll(tracer, shift, 0)
                      + jnp.where(row == (5 + shift) % 8, pltpu.roll(tracer, shift + 1, 0), 0.0))


def final_kernel(route_ref, plan_ref, lines_ref, inner_ref, almost_ref, first, second, third, fourth, out_ref, full, sems):
    lane, row = lanes(), rows()
    route, plan = Rows(route_ref), Rows(plan_ref)
    came = by_link((first, second, third, fourth), BOTH)
    outer = [came[link][0:8, :] for link in range(4)]
    ends = []
    for end in range(2):
        values = []
        for link in range(4):
            which, lane_from = plan[2 * (2 * link + end)], plan[2 * (2 * link + end) + 1]
            held = jnp.where(which == 2, outer[3], outer[1])
            values.append(jnp.where(which > 0, pick(held, lane_from), 0.0))
        ends.append(rims_of(route, None, values))
    rims = rims_of(route, None, outer)
    beyond = rims_of(route, None, [came[link][8:16, :] for link in range(4)])
    lines, inner = four_of(lines_ref), four_of(inner_ref)
    patch = edge_patches(lines, rims)
    kept = [jnp.where(lane < TILE, one, 0.0) for one in patch]
    across = [pressure_at(kept[side], 4 if side % 2 == 1 else 6, row) for side in range(4)]
    crossing = ((3, 1, 0), (0, 2, TILE - 1), (3, 1, TILE - 1), (0, 2, 0))
    on_edge, inside = [], []
    for side in range(4):
        sign = 1.0 if side in (1, 2) else -1.0
        line, wet, wet_in = rims[side], wet_rows(lines[side]), wet_rows(inner[side])
        after = jnp.where(lane == TILE - 1, ends[1][side], pltpu.roll(line, LANES - 1, 1))
        before = jnp.where(lane == 0, ends[0][side], pltpu.roll(line, 1, 1))
        upper, lower = pltpu.roll(line, 4, 0), pltpu.roll(line, 2, 0)
        normal, tangent = (upper, lower) if side % 2 == 1 else (lower, upper)
        along = normal * (sign * (beyond[side] - lines[side])) + tangent * (after - before)
        round_sum = after + before + beyond[side] + lines[side] - 4.0 * line
        tracer = wet_rows(line) * (line - (0.5 * ADVECT) * along + DIFFUSE * round_sum)
        to_normal, to_tangent = (4, 6) if side % 2 == 1 else (6, 4)
        own_row = row < 2 if side % 2 == 1 else (row >= 2) & (row < 4)
        cross_row = (row >= 2) & (row < 4) if side % 2 == 1 else row < 2
        cross = pressure_at(kept[side], to_tangent, row)
        start, stop, lane_there = crossing[side]
        drop = pltpu.roll(cross, LANES - 1, 1) - pltpu.roll(cross, 1, 1)
        drop = drop + at_ends(across[stop], lane_there, TILE - 2) - at_ends(across[start], lane_there, 1)
        push = jnp.where(own_row, sign * pressure_at(tracer, to_normal, row), 0.0)
        push = jnp.where(cross_row, drop, push)
        on_edge.append(patch[side] - (0.5 * STEP_SIZE) * wet * push)
        between = own_row & (lane > 0) & (lane < TILE - 1)
        inside.append(jnp.where(between, (-sign * 0.5 * STEP_SIZE) * wet_in * across[side], 0.0))
    edges, seconds = spread_chunks(on_edge, 0), spread_chunks(inside, 1)
    copies = []
    for low, high in ((0, 48), (48, CHUNKS)):
        for c in range(low, high):
            cut = slice(c * LANES, min((c + 1) * LANES, CELLS))
            width = cut.stop - cut.start
            full[:, cut] = (almost_ref[:, c * LANES:(c + 1) * LANES] + (edges[c] + seconds[c]))[:, :width]
        cells = pl.ds(low * LANES, min(high * LANES, CELLS) - low * LANES)
        copies.append(pltpu.make_async_copy(full.at[0:6, cells], out_ref.at[:, 0, cells], sems.at[len(copies)]))
        copies[-1].start()
    for copy in copies:
        copy.wait()


def write_out(full, out_ref, sems):
    copies = [pltpu.make_async_copy(full.at[c], out_ref.at[c, 0], sems.at[c]) for c in range(6)]
    for copy in copies:
        copy.start()
    for copy in copies:
        copy.wait()


def at_ends(line, lane_from, lane_to):
    value = jnp.broadcast_to(line[:, lane_from:lane_from + 1], (8, LANES))
    return jnp.where(lanes() == lane_to, value, 0.0)


def edge_kernel(route_ref, lines_ref, base_lines_ref, came0, came1, came2, came3,
                patch_ref, own_two_ref, pay0, pay1, pay2, pay3):
    route = Rows(route_ref)
    lines, base = four_of(lines_ref), four_of(base_lines_ref)
    own = own_rims([sent_line(lines[side], side, route, True) for side in range(4)], route)
    rims = rims_of(route, own, [came[0:8, :] for came in by_link((came0, came1, came2, came3), BOTH)])
    patch = edge_patches(lines, rims)
    whole = with_ends(patch)
    press = []
    for side in range(4):
        patch_ref[8 * side:8 * side + 8, :] = patch[side]
        press.append(sent_line(pressure_of(base[side] + whole[side], rows()), side, route, False))
    for link, pay in zip(SECOND_ORDER, (pay0, pay1, pay2, pay3)):
        pay[...] = chosen(press, route, link)
    own = own_rims(press, route)
    for side in range(4):
        own_two_ref[8 * side:8 * side + 8, :] = own[side]


def middle_kernel(route_ref, state_ref, base_ref, patch_ref, out_ref):
    state = state_ref[...]
    cell, column = column_of()
    base = base_ref[...] + spread(four_of(patch_ref), cell, column)
    row = lax.broadcasted_iota(jnp.int32, (8, WIDE), 0)
    out_ref[...] = if_live(route_ref, base + force_of(state, base, row))


def last_kernel(route_ref, lines_ref, own_ref, almost_ref, came0, came1, came2, came3, out_ref, full, sems):
    route = Rows(route_ref)
    rims = rims_of(route, four_of(own_ref), [came[...] for came in by_link((came0, came1, came2, came3), SECOND_ORDER)])
    patch = []
    for side in range(4):
        wet = wet_rows(lines_ref[8 * side:8 * side + 8, :])
        row = rows()
        rim = pltpu.roll(rims[side], 4 if side % 2 == 1 else 6, 0)
        mine = row < 2 if side % 2 == 1 else (row >= 2) & (row < 4)
        sign = -1.0 if side in (1, 2) else 1.0
        patch.append(jnp.where(mine, (sign * 0.5 * STEP_SIZE) * wet * rim, 0.0))
    cell, column = column_of()
    full[...] = (almost_ref[...] + spread(patch, cell, column))[:, :CELLS]
    write_out(full, out_ref, sems)


def sds(*shape, dtype=jnp.float32):
    return jax.ShapeDtypeStruct(shape, dtype)


PARAMS = pltpu.CompilerParams(vmem_limit_bytes=16 * 1024 * 1024)


def on_device(nx, ny, fields, wet_mask, tile_of_slot, neighbor, rotation):
    line, pair, four, wide = sds(8, LANES), sds(16, LANES), sds(32, LANES), sds(8, WIDE)
    scalars = pltpu.SMEM((4, nx * ny), jnp.int32)
    tables = [pltpu.with_memory_space_constraint(v, pltpu.HBM) for v in (tile_of_slot, neighbor.T, rotation.T)]
    inputs = [pltpu.with_memory_space_constraint(v, pltpu.HBM) for v in (fields.reshape(6, 1, CELLS), wet_mask)]
    halves = pltpu.with_memory_space_constraint(tile_of_slot.reshape(2, LANES), pltpu.HBM)
    raw, wet_raw, lines, inner, *pays, route = pl.pallas_call(
        lambda *refs: load_kernel((nx, ny), *refs),
        out_shape=[sds(8, CELLS), sds(8, CELLS, dtype=jnp.int32), four, four, pair, pair, pair, pair,
                   sds(ROUTE, LANES, dtype=jnp.int32)],
        in_specs=[HBM] * 5,
        out_specs=[VMEM] * 9,
        scratch_shapes=[pltpu.SMEM((nx * ny,), jnp.int32), scalars, scalars, pltpu.SemaphoreType.DMA((12,))],
        compiler_params=PARAMS, name="load",
    )(*tables, *inputs)
    came_u = exchanged(pays[:2], U_ORDER, nx, ny)
    almost, plan, flag = pl.pallas_call(
        lambda *refs: inner_kernel((nx, ny), *refs),
        out_shape=[wide, sds(16, LANES, dtype=jnp.int32), sds(1, dtype=jnp.int32)],
        in_specs=[HBM] * 4 + [VMEM] * 3, out_specs=[VMEM, VMEM, SMEM],
        scratch_shapes=[pltpu.VMEM((8, WIDE), jnp.float32), pltpu.SMEM((nx * ny,), jnp.int32), scalars, scalars,
                        pltpu.VMEM((2, LANES), jnp.int32), pltpu.VMEM((8, nx * ny), jnp.int32),
                        pltpu.SemaphoreType.DMA((5,))],
        compiler_params=PARAMS, name="inner",
        cost_estimate=pl.CostEstimate(flops=2000000, bytes_accessed=800000, transcendentals=0),
    )(*tables, halves, raw, wet_raw, route)
    sent = pl.pallas_call(
        relay_kernel, out_shape=[pair, pair], in_specs=[VMEM] * 4 + [ANY], out_specs=[VMEM] * 2,
        compiler_params=PARAMS, name="relay",
    )(*pays[2:], *came_u, almost)
    came_x = exchanged(sent, X_ORDER, nx, ny)
    result = pltpu.HBM((6, 1, CELLS), jnp.float32)
    writing = [pltpu.VMEM((8, CELLS), jnp.float32), pltpu.SemaphoreType.DMA((12,))]

    def grid_like():
        return pl.pallas_call(
            final_kernel, out_shape=result, in_specs=[VMEM] * 9, out_specs=HBM,
            scratch_shapes=writing, compiler_params=PARAMS, name="final",
        )(route, plan, lines, inner, almost, *came_u, *came_x)

    def general():
        came = came_u + came_x
        state, base, base_lines = pl.pallas_call(
            base_kernel, out_shape=[wide, wide, four], in_specs=[VMEM] * 2, out_specs=[VMEM] * 3,
            compiler_params=PARAMS, name="base",
            cost_estimate=pl.CostEstimate(flops=2000000, bytes_accessed=800000, transcendentals=0),
        )(raw, wet_raw)
        patch, own_two, *press = pl.pallas_call(
            edge_kernel, out_shape=[four, four, line, line, line, line],
            in_specs=[VMEM] * 7, out_specs=[VMEM] * 6,
            compiler_params=PARAMS, name="edge",
        )(route, lines, base_lines, *came)
        came_two = exchanged(press, SECOND_ORDER, nx, ny)
        nearly = pl.pallas_call(
            middle_kernel, out_shape=wide, in_specs=[VMEM] * 4, out_specs=VMEM,
            compiler_params=PARAMS, name="middle",
            cost_estimate=pl.CostEstimate(flops=2000000, bytes_accessed=800000, transcendentals=0),
        )(route, state, base, patch)
        return pl.pallas_call(
            last_kernel, out_shape=result, in_specs=[VMEM] * 8, out_specs=HBM,
            scratch_shapes=writing, compiler_params=PARAMS, name="last",
        )(route, lines, own_two, nearly, *came_two)

    out = lax.switch(flag[0], [grid_like, general])
    return out.reshape(1, 6, CELLS)


def solution(mesh):
    nx, ny = mesh.shape["gx"], mesh.shape["gy"]
    in_specs = (P(AXES, None, None), P(AXES, None), P(), P(), P())
    return jax.shard_map(lambda *args: on_device(nx, ny, *args), mesh=mesh, in_specs=in_specs,
                         out_specs=P(AXES, None, None), check_vma=False)
```
